256 devices in a mesh: gx: 64 (over z, x, y_hi), gy: 4 (over y_lo, core).
Axes of the slice: x: 4, y: 4 (y_hi: 2, y_lo: 2; y = y_hi * 2 + y_lo), z: 8, core: 2. Of those that a mesh axis runs over, the one named last changes fastest.
Arguments:
- features: bfloat16 [1024, 64, 256], P(('gx', 'gy')), may hold values from -12 to 12, as said below
- occupancy: int32 [1024, 64], P(('gx', 'gy')), may hold values from 0 to 1, as said below
- neighbours: int32 [1024, 27], P(('gx', 'gy')), may hold values from 0 to 12, as said below
- send_list: int32 [256, 8, 1], P(('gx', 'gy')), may hold values from 0 to 3, as said below
- weight: bfloat16 [27, 256, 256], replicated, may hold values from -0.078125 to 0.078125
- gamma: float32 [256], replicated, may hold values from 0.1 to 1.9
- beta: float32 [256], replicated, may hold values from -3 to 3
- out_grad: bfloat16 [1024, 64, 256], P(('gx', 'gy')), may hold values from -6 to 6
Outputs:
- block_out: bfloat16 [1024, 64, 256], P(('gx', 'gy'))
- feature_grad: bfloat16 [1024, 64, 256], P(('gx', 'gy'))
- weight_grad: bfloat16 [27, 256, 256], replicated
- gamma_grad: float32 [256], replicated
- beta_grad: float32 [256], replicated
The draws below stay inside these ranges and needn't reach their ends.
Inputs may be any that keep to these rules, and one draw needn't show every extreme that they name: `occupancy`: each device has between 2 and 4 live bricks, its first ones, and some device has all 4; voxels of the other bricks are 0. `neighbours`: values below 4 name a live brick of the same device, 4 + 1 d + h names halo place (d, h), and 12 names the zero brick; entry 13 of a live brick is the brick itself, and all entries of a brick that is not live are 12. `send_list`: for each device and direction, one live brick of that device. `features`: zero at voxels that are not occupied is not promised.
All inputs are finite; a program needn't handle non-finite values.
Results may differ from the reference program's by a relative error of at most 0.005.
Values may be sent and summed in bfloat16 or wider, within the bound.
A program may use at most 128 MiB of HBM per device.

```python
import math
import jax
import jax.numpy as jnp
import numpy as np
from jax import lax

C = 256
VOXELS = 64
B = 4
H = 1
NB = 1024
N_GX = 64
N_GY = 4


def live_bricks(key):
    devices = NB // B
    extra = jax.random.randint(jax.random.fold_in(key, 11), (devices,), 0, B - B // 2 + 1)
    fullest = jax.random.randint(jax.random.fold_in(key, 12), (), 0, devices)
    live = jnp.where(jnp.arange(devices) == fullest, B, B // 2 + extra)
    return (live.astype(jnp.int32), fullest)


def draw_features(key, part):
    key = jax.random.fold_in(key, 4)
    keys = jax.random.split(key, 3)
    voxel_scale = jnp.exp(jax.random.uniform(keys[0], (NB, 64, 1), jnp.float32, math.log(0.3), math.log(3.0)))
    channel_scale = jnp.exp(jax.random.uniform(keys[1], (1, 1, C), jnp.float32, math.log(0.5), math.log(2.0)))
    base = jnp.clip(jax.random.normal(keys[2], (NB, 64, C), jnp.float32), -4.0, 4.0)
    value = base * channel_scale * voxel_scale
    return jnp.clip(value, -12.0, 12.0).astype(jnp.bfloat16)


def draw_occupancy(key, part):
    live, fullest = live_bricks(key)
    key = jax.random.fold_in(key, 1)
    devices = NB // B
    brick = jnp.arange(NB, dtype=jnp.int32)
    device = brick // B
    slot = brick % B
    level = 250 + 500 * device // max(devices - 1, 1)
    draws = jax.random.randint(key, (NB, 64), 0, 1000)
    alive = slot < live[device]
    return ((draws < level[:, None]) & alive[:, None]).astype(jnp.int32)


def draw_neighbours(key, part):
    live, fullest = live_bricks(key)
    key = jax.random.fold_in(key, 2)
    keys = jax.random.split(key, 3)
    brick = jnp.arange(NB, dtype=jnp.int32)
    slot = brick % B
    mine = live[brick // B]
    kind = jax.random.randint(keys[0], (NB, 27), 0, 20)
    local = jax.random.randint(keys[1], (NB, 27), 0, mine[:, None])
    remote = jax.random.randint(keys[2], (NB, 27), B, B + 8 * H)
    empty = B + 8 * H
    table = jnp.where(kind < 8, local, jnp.where(kind < 15, remote, empty))
    table = table.at[:, 13].set(slot)
    table = jnp.where((slot < mine)[:, None], table, empty)
    table = table.at[0, 26].set(empty)
    return table.astype(jnp.int32)


def draw_send_list(key, part):
    live, fullest = live_bricks(key)
    key = jax.random.fold_in(key, 3)
    devices = NB // B
    slot = jnp.arange(B, dtype=jnp.int32)
    device = jnp.arange(devices, dtype=jnp.int32)
    direction = jnp.arange(8, dtype=jnp.int32)
    score = jax.random.randint(key, (devices, 8, B), 0, 2 ** 20) * B + slot[None, None, :]
    score = jnp.where(slot[None, None, :] < live[:, None, None], score, -1 - slot[None, None, :])
    lowest = (slot[None, None, :] == 0) & (direction[None, :, None] == 1)
    highest = (slot[None, None, :] == B - 1) & (direction[None, :, None] == 0) & (device[:, None, None] == fullest)
    score = jnp.where(lowest | highest, 2 ** 30, score)
    ignored, chosen = lax.top_k(score, H)
    return chosen.astype(jnp.int32)


def block_levels(stream_key, dims, cuts, least, high):
    gain = 1.0
    for dim, blocks in cuts:
        steps = jax.random.uniform(jax.random.fold_in(jax.random.fold_in(stream_key, 6), dim), (blocks,), jnp.float32, least / len(cuts), high / len(cuts))
        gain = gain * jnp.repeat(jnp.exp(steps), dims[dim] // blocks).reshape((-1,) + (1,) * (len(dims) - 1 - dim))
    return gain


def scatter_about(stream_key, shape, deviation, reach, cuts=(), held_as=jnp.bfloat16):
    entries = jax.random.normal(stream_key, shape, jnp.float32) * deviation
    if len(cuts) > 0:
        entries = block_levels(stream_key, shape, cuts, -0.22, 0.18) * entries
    return jnp.clip(entries, min=-reach, max=reach).astype(held_as)


def setup_inputs(seed: int = 0) -> dict:
    streams_of = jax.random.split(jax.random.key(seed), 9)
    return {
        "features": draw_features(jax.random.fold_in(streams_of[8], 71), 0),
        "occupancy": draw_occupancy(jax.random.fold_in(streams_of[8], 71), 0),
        "neighbours": draw_neighbours(jax.random.fold_in(streams_of[8], 71), 0),
        "send_list": draw_send_list(jax.random.fold_in(streams_of[8], 71), 0),
        "weight": scatter_about(streams_of[4], (27, C, C), (27 * C) ** -0.5, 0.078125),
        "gamma": jnp.clip(1.0 + 0.18 * jax.random.normal(streams_of[5], (C,), jnp.float32), 0.1, 1.9),
        "beta": scatter_about(streams_of[6], (C,), 0.5, 3.0, (), jnp.float32),
        "out_grad": scatter_about(streams_of[7], (NB, VOXELS, C), 1.0, 6.0, ((0, 256),)),
    }


DIRECTION_ROWS = (-1, -1, -1, 0, 0, 1, 1, 1)
DIRECTION_COLUMNS = (-1, 0, 1, -1, 1, -1, 0, 1)
BRICK_PICK = np.array([0, 1, 1, 1, 1, 2])
VOXEL_PICK = np.array([3, 0, 1, 2, 3, 0])
EPSILON = 1e-05

def assemble(extended, neighbour_table):
    brick_count = neighbour_table.shape[0]
    channels = extended.shape[-1]
    nearby = extended[neighbour_table].reshape(brick_count, 3, 3, 3, 4, 4, 4, channels)
    return nearby[:, BRICK_PICK[:, None, None], BRICK_PICK[None, :, None], BRICK_PICK[None, None, :], VOXEL_PICK[:, None, None], VOXEL_PICK[None, :, None], VOXEL_PICK[None, None, :], :]

def unfold(padded):
    brick_count = padded.shape[0]
    channels = padded.shape[-1]
    pieces = [padded[:, shift_x:shift_x + 4, shift_y:shift_y + 4, shift_z:shift_z + 4, :] for shift_x in range(3) for shift_y in range(3) for shift_z in range(3)]
    return jnp.concatenate(pieces, axis=-1).reshape(brick_count * 64, 27 * channels)

def fold_back(column_grad, brick_count, channels):
    blocks = column_grad.reshape(brick_count, 4, 4, 4, 27, channels)
    padded = jnp.zeros((brick_count, 6, 6, 6, channels), jnp.float32)
    for shift_x in range(3):
        for shift_y in range(3):
            for shift_z in range(3):
                padded = padded.at[:, shift_x:shift_x + 4, shift_y:shift_y + 4, shift_z:shift_z + 4, :].add(blocks[:, :, :, :, 9 * shift_x + 3 * shift_y + shift_z, :])
    return padded

def spread_back(padded_grad, neighbour_table, slot_count):
    brick_count = neighbour_table.shape[0]
    channels = padded_grad.shape[-1]
    nearby = jnp.zeros((brick_count, 3, 3, 3, 4, 4, 4, channels), jnp.float32)
    nearby = nearby.at[:, BRICK_PICK[:, None, None], BRICK_PICK[None, :, None], BRICK_PICK[None, None, :], VOXEL_PICK[:, None, None], VOXEL_PICK[None, :, None], VOXEL_PICK[None, None, :], :].set(padded_grad)
    nearby = nearby.reshape(brick_count * 27, 64 * channels)
    selector = (neighbour_table.reshape(-1)[None, :] == jnp.arange(slot_count, dtype=jnp.int32)[:, None]).astype(jnp.float32)
    summed = jnp.dot(selector, nearby, precision=lax.Precision.HIGHEST)
    return summed.reshape(slot_count, 64, channels)

def take_back(returned, chosen):
    channels = returned.shape[-1]
    selector = (chosen.reshape(-1)[None, :] == jnp.arange(B, dtype=jnp.int32)[:, None]).astype(jnp.float32)
    flat = returned.reshape(-1, 64 * channels).astype(jnp.float32)
    return jnp.dot(selector, flat, precision=lax.Precision.HIGHEST).reshape(B, 64, channels)

def reference(features, occupancy, neighbours, send_list, weight, gamma, beta, out_grad):
    devices = N_GX * N_GY
    channels = features.shape[-1]
    slot_count = B + 8 * H + 1
    occupied = occupancy.astype(jnp.float32)[:, :, None]
    masked = features * occupancy.astype(jnp.bfloat16)[:, :, None]
    masked_dev = masked.reshape(devices, B, 64, channels)
    tables = neighbours.reshape(devices, B, 27)
    rank = jnp.arange(devices, dtype=jnp.int32)
    row_index = rank // N_GY
    column_index = rank % N_GY
    groups = []
    for direction in range(8):
        source_row = row_index - DIRECTION_ROWS[direction]
        source_column = column_index - DIRECTION_COLUMNS[direction]
        valid = (source_row >= 0) & (source_row < N_GX) & (source_column >= 0) & (source_column < N_GY)
        source = jnp.where(valid, source_row * N_GY + source_column, 0).astype(jnp.int32)
        chosen = send_list[source, direction]
        arrived = masked_dev[source[:, None], chosen]
        groups.append(jnp.where(valid[:, None, None, None], arrived, jnp.zeros_like(arrived)))
    halo_bricks = jnp.stack(groups, axis=1).reshape(devices, 8 * H, 64, channels)
    extended = jnp.concatenate([masked_dev, halo_bricks, jnp.zeros((devices, 1, 64, channels), jnp.bfloat16)], axis=1)
    weight_rows = weight.reshape(27 * channels, channels)

    def forward_one(pair):
        columns = unfold(assemble(pair[0], pair[1]))
        return jnp.dot(columns, weight_rows, preferred_element_type=jnp.float32).reshape(B, 64, channels)
    convolved = lax.map(forward_one, (extended, tables)).reshape(devices * B, 64, channels) * occupied
    voxel_count = jnp.sum(occupied)
    average = lax.optimization_barrier(jnp.sum(convolved, axis=(0, 1))) / voxel_count
    centred = (convolved - average) * occupied
    variance = lax.optimization_barrier(jnp.sum(centred * centred, axis=(0, 1))) / voxel_count
    inverse_std = lax.rsqrt(variance + EPSILON)
    normalized = (convolved - average) * inverse_std
    normed = gamma * normalized + beta
    sigmoid_normed = jax.nn.sigmoid(normed)
    block_out = ((masked.astype(jnp.float32) + normed * sigmoid_normed) * occupied).astype(jnp.bfloat16)
    out_masked = out_grad.astype(jnp.float32) * occupied
    act_grad = out_masked * sigmoid_normed * (1.0 + normed * (1.0 - sigmoid_normed))
    grad_total = lax.optimization_barrier(jnp.sum(act_grad, axis=(0, 1)))
    grad_cross = lax.optimization_barrier(jnp.sum(act_grad * normalized, axis=(0, 1)))
    conv_grad = (gamma * inverse_std * (act_grad - grad_total / voxel_count - normalized * grad_cross / voxel_count) * occupied).astype(jnp.bfloat16)
    conv_grad_dev = conv_grad.reshape(devices, B, 64, channels)

    def backward_step(running, triple):
        columns = unfold(assemble(triple[0], triple[1]))
        flat_up = triple[2].reshape(B * 64, channels)
        running = running + lax.dot_general(columns, flat_up, (((0,), (0,)), ((), ())), preferred_element_type=jnp.float32)
        column_grad = lax.dot_general(flat_up, weight_rows, (((1,), (1,)), ((), ())), preferred_element_type=jnp.float32)
        extended_grad = spread_back(fold_back(column_grad, B, channels), triple[1], slot_count)
        ghost = extended_grad[B:B + 8 * H].astype(jnp.bfloat16).reshape(8, H, 64, channels)
        return (running, (extended_grad[:B], ghost))
    weight_sum, (local_grad, ghosts) = lax.scan(backward_step, jnp.zeros((27 * channels, channels), jnp.float32), (extended, tables, conv_grad_dev))
    backs = []
    for direction in range(8):
        target_row = row_index + DIRECTION_ROWS[direction]
        target_column = column_index + DIRECTION_COLUMNS[direction]
        valid = (target_row >= 0) & (target_row < N_GX) & (target_column >= 0) & (target_column < N_GY)
        target = jnp.where(valid, target_row * N_GY + target_column, 0).astype(jnp.int32)
        arrived = ghosts[target, direction]
        backs.append(jnp.where(valid[:, None, None, None], arrived, jnp.zeros_like(arrived)))
    returned = jnp.stack(backs, axis=1)
    extra = jax.vmap(take_back)(returned, send_list)
    gradient_sum = out_masked.reshape(devices, B, 64, channels) + local_grad + extra
    feature_grad = (gradient_sum.reshape(devices * B, 64, channels) * occupied).astype(jnp.bfloat16)
    inverse_root = lax.rsqrt(voxel_count)
    weight_grad = (weight_sum * inverse_root).astype(jnp.bfloat16).reshape(27, channels, channels)
    return (block_out, feature_grad, weight_grad, grad_cross * inverse_root, grad_total * inverse_root)
```

```python
import functools

import jax
import jax.numpy as jnp
from jax import lax
from jax.experimental import pallas as pl
from jax.experimental.pallas import tpu as pltpu
from jax.sharding import PartitionSpec as P

Z, X, YH, YL = 8, 4, 2, 2
Y = YH * YL
PLANE = X * Y * 2

ROWS = (-1, -1, -1, 0, 0, 1, 1, 1)
COLUMNS = (-1, 0, 1, -1, 1, -1, 0, 1)
EPSILON = 1e-05
MESH = pl.DeviceIdType.MESH
F32, BF16, I32 = jnp.float32, jnp.bfloat16, jnp.int32

PARTS = ((0, 14, 0), (14, 13, 16))


def coordinates():
    gx, gy = lax.axis_index("gx"), lax.axis_index("gy")
    z = lax.div(gx, X * YH)
    x = lax.rem(lax.div(gx, YH), X)
    y = lax.rem(gx, YH) * YL + lax.div(gy, 2)
    return z, x, y, lax.rem(gy, 2)


def device(z, x, y, c):
    return (z * (X * YH) + x * YH + lax.div(y, YL), lax.rem(y, YL) * 2 + c)


def ahead(value, steps, count):
    return lax.rem(value + (steps + count) % count, count)


def dot(a, b):
    return jnp.dot(a, b, preferred_element_type=F32)


def place_row(p):
    return (p >= 1).astype(I32) + (p >= 5).astype(I32)


def kernel(
    occ_ref, nb_ref, send_ref, feat_ref, gamma_ref, beta_ref, og_ref, w_hbm,
    block_ref, fgrad_ref, wgrad_ref, ggrad_ref, bgrad_ref,
    tab, occn, masked, packets, ext, gath, slabs, weight, conv_s, norm_s, cols_t,
    pl1, zs1, pl2, zs2,
    cg_s, grad_s, ghosts, returned,
    own, osend, crecv, s1, r1, s2, r2, s3, r3, outb,
    w_sem, halo_s, halo_r, p1_s, p1_r, z1_s, z1_r, p2_s, p2_r, z2_s, z2_r,
    gh_s, gh_r, c_s, c_r, q1_s, q1_r, q2_s, q2_r, q3_s, q3_r, a3_s, a3_r, a2_s, a2_r, a1_s, a1_r, a0_s, a0_r, o_sem,
):
    z, x, y, c = coordinates()
    gx, gy = lax.axis_index("gx"), lax.axis_index("gy")
    ngx, ngy = Z * X * YH, YL * 2
    me = (x * Y + y) * 2 + c

    def neighbour(u, v):
        return (ahead(gx, u, ngx), ahead(gy, v, ngy))

    plane = [(dx, dy, dc) for dx in range(X) for dy in range(Y) for dc in range(2) if dx + dy + dc > 0]

    def plane_mate(step):
        dx, dy, dc = step
        return ahead(x, dx, X), ahead(y, dy, Y), ahead(c, dc, 2)

    barrier = pltpu.get_barrier_semaphore()
    greeted = 0
    for d in range(8):
        pl.semaphore_signal(barrier, inc=1, device_id=neighbour(ROWS[d], COLUMNS[d]), device_id_type=MESH)
        greeted += 1
    for step in plane:
        pl.semaphore_signal(barrier, inc=1, device_id=device(z, *plane_mate(step)), device_id_type=MESH)
        greeted += 1
    for dz in range(1, Z):
        pl.semaphore_signal(barrier, inc=1, device_id=device(ahead(z, dz, Z), x, y, c), device_id_type=MESH)
        greeted += 1

    weight_copy = pltpu.make_async_copy(w_hbm, weight, w_sem)
    weight_copy.start()

    tab[...] = jnp.zeros_like(tab)
    tab[0:4, 0:64] = occ_ref[...].astype(F32)
    tab[8:12, 0:27] = nb_ref[...].astype(F32)

    def pick(first, index):
        rows = [tab[first + n : first + n + 1, :] for n in range(4)]
        return jnp.where(index == 0, rows[0], jnp.where(index == 1, rows[1], jnp.where(index == 2, rows[2], rows[3])))

    def iotas(rows, lanes):
        shape = (rows, lanes)
        return lax.broadcasted_iota(I32, shape, 0), lax.broadcasted_iota(I32, shape, 1)

    ones = jnp.ones((128, 256), BF16)
    row, lane = iotas(256, 128)
    by_brick = jnp.where(lane == jnp.bitwise_and(row, 63), pick(0, jnp.right_shift(row, 6)), 0.0)
    occ_brick = dot(by_brick.astype(BF16), ones)
    feat = feat_ref[...].reshape(256, 256)
    masked_value = (feat.astype(F32) * occ_brick).astype(BF16)
    masked[...] = masked_value.reshape(4, 64, 256)
    ext[0:4] = masked_value.reshape(4, 64, 256)
    for d in range(8):
        packets[d] = masked[send_ref[0, d]]

    pl.semaphore_wait(barrier, greeted)
    halo = []
    for d in range(8):
        copy = pltpu.make_async_remote_copy(
            src_ref=packets.at[d], dst_ref=ext.at[4 + d], send_sem=halo_s.at[d], recv_sem=halo_r.at[d],
            device_id=neighbour(ROWS[d], COLUMNS[d]), device_id_type=MESH)
        copy.start()
        halo.append(copy)

    by_voxel = jnp.where(
        lane == jnp.right_shift(row, 4) * 4 + jnp.bitwise_and(row, 3),
        pick(0, jnp.bitwise_and(jnp.right_shift(row, 2), 3)), 0.0)
    occ = dot(by_voxel.astype(BF16), ones)
    occn[...] = occ
    row, lane = iotas(256, 256)
    order = jnp.bitwise_and(jnp.right_shift(row, 2), 3) * 64 + jnp.right_shift(row, 4) * 4 + jnp.bitwise_and(row, 3)
    to_rows = jnp.where(lane == order, occ, 0.0).astype(BF16)
    order = jnp.bitwise_and(jnp.right_shift(lane, 2), 3) * 64 + jnp.right_shift(lane, 4) * 4 + jnp.bitwise_and(lane, 3)
    to_bricks = jnp.where(row == order, 1.0, 0.0).astype(BF16)
    out_masked = dot(to_rows, og_ref[...].reshape(256, 256))

    table = tab[8:16, :]
    for d in range(8):
        u, v = ROWS[d], COLUMNS[d]
        missing = jnp.int32(0)
        if u != 0:
            missing = missing + (gx == (0 if u > 0 else ngx - 1)).astype(I32)
        if v != 0:
            missing = missing + (gy == (0 if v > 0 else ngy - 1)).astype(I32)
        table = jnp.where((table == 4.0 + d) & (missing > 0), 12.0, table)
    tab[8:16, :] = table
    row, lane = iotas(576, 128)
    pq = jnp.right_shift(row, 4)
    p = jnp.right_shift(pq * 43, 8)
    q = pq - 6 * p
    brick, w = jnp.bitwise_and(jnp.right_shift(row, 2), 3), jnp.bitwise_and(row, 3)
    places = 9 * place_row(p) + 3 * place_row(q)
    voxels = 16 * jnp.bitwise_and(p + 3, 3) + 4 * jnp.bitwise_and(q + 3, 3)
    near = pick(8, brick)
    lane_f = lane.astype(F32)
    for shift in range(3):
        cell = w + shift
        found = dot(jnp.where(lane == places + place_row(cell), near, 0.0).astype(BF16), jnp.ones((128, 128), BF16))
        source = found * 64.0 + (voxels + jnp.bitwise_and(cell + 3, 3)).astype(F32)
        for j in range(6):
            gath[shift, :, j * 128 : (j + 1) * 128] = jnp.where(source == lane_f + 128.0 * j, 1.0, 0.0).astype(BF16)

    for copy in halo:
        copy.wait()
    extended = ext[...].reshape(768, 256)
    for shift in range(3):
        slabs[shift] = dot(gath[shift], extended).astype(BF16)

    def columns(k):
        a, b, shift = k // 9, k // 3 % 3, k % 3
        return jnp.concatenate(
            [slabs[shift, (a + i) * 96 + b * 16 : (a + i) * 96 + b * 16 + 64, :] for i in range(4)], axis=0)

    weight_copy.wait()
    conv = dot(columns(0), weight[0])
    for k in range(1, 27):
        conv = conv + dot(columns(k), weight[k])
    conv = conv * occ

    def two(value):
        return jnp.concatenate([value[:, :128], value[:, 128:]], axis=0)

    def one(tile):
        return jnp.concatenate([tile[0:1, :], tile[1:2, :]], axis=1)

    def spread_plane(buffer, send, receive):
        copies = []
        for i, step in enumerate(plane):
            copy = pltpu.make_async_remote_copy(
                src_ref=buffer.at[me], dst_ref=buffer.at[me], send_sem=send.at[i], recv_sem=receive.at[i],
                device_id=device(z, *plane_mate(step)), device_id_type=MESH)
            copy.start()
            copies.append(copy)
        return copies

    def meet_plane(copies, buffer, send, receive):
        for i, step in enumerate(plane):
            dx, dy, dc = step
            place = (ahead(x, -dx, X) * Y + ahead(y, -dy, Y)) * 2 + ahead(c, -dc, 2)
            copies[i].wait_send()
            pltpu.make_async_remote_copy(
                src_ref=buffer.at[place], dst_ref=buffer.at[place], send_sem=send.at[i], recv_sem=receive.at[i],
                device_id=device(z, x, y, c), device_id_type=MESH).wait_recv()

    def spread_depth(buffer, send, receive):
        copies = []
        for dz in range(1, Z):
            copy = pltpu.make_async_remote_copy(
                src_ref=buffer.at[z], dst_ref=buffer.at[z], send_sem=send.at[dz - 1], recv_sem=receive.at[dz - 1],
                device_id=device(ahead(z, dz, Z), x, y, c), device_id_type=MESH)
            copy.start()
            copies.append(copy)
        return copies

    def meet_depth(copies, buffer, send, receive):
        for dz in range(1, Z):
            place = ahead(z, -dz, Z)
            copies[dz - 1].wait_send()
            pltpu.make_async_remote_copy(
                src_ref=buffer.at[place], dst_ref=buffer.at[place], send_sem=send.at[dz - 1],
                recv_sem=receive.at[dz - 1], device_id=device(z, x, y, c), device_id_type=MESH).wait_recv()

    def merge(buffer, count):
        tiles = [buffer[i] for i in range(count)]
        total = sum(tiles[1:], tiles[0])
        mean = total[0:2, :] / jnp.maximum(total[4:5, :], 1.0)
        square = total[2:4, :]
        for tile in tiles:
            gap = tile[0:2, :] / jnp.maximum(tile[4:5, :], 1.0) - mean
            square = square + tile[4:5, :] * gap * gap
        return total[0:2, :], square, total[4:5, :]

    def write(buffer, place, sums, squares, number):
        buffer[place] = jnp.concatenate([sums, squares, number, jnp.zeros((3, 128), F32)], axis=0)

    number = jnp.sum(occ, axis=0, keepdims=True)
    sums = jnp.sum(conv, axis=0, keepdims=True)
    centred = (conv - sums / jnp.maximum(number, 1.0)) * occ
    squares = jnp.sum(centred * centred, axis=0, keepdims=True)
    write(pl1, me, two(sums), two(squares), number[:, :128])
    copies = spread_plane(pl1, p1_s, p1_r)
    conv_s[...] = conv
    for k in range(14):
        cols_t[k] = columns(k).T
    meet_plane(copies, pl1, p1_s, p1_r)
    write(zs1, z, *merge(pl1, PLANE))
    copies = spread_depth(zs1, z1_s, z1_r)
    meet_depth(copies, zs1, z1_s, z1_r)
    sums, squares, number = merge(zs1, Z)
    voxel_count = jnp.concatenate([number, number], axis=1)
    average = one(sums) / voxel_count
    inverse_std = lax.rsqrt(one(squares) / voxel_count + EPSILON)
    gamma, beta = gamma_ref[...], beta_ref[...]
    occ = occn[...]
    normalized = (conv_s[...] - average) * inverse_std
    normed = gamma * normalized + beta
    sigmoid = 1.0 / (1.0 + jnp.exp(-normed))
    act_grad = out_masked * sigmoid * (1.0 + normed * (1.0 - sigmoid))
    total = jnp.sum(act_grad, axis=0, keepdims=True)
    cross = jnp.sum(act_grad * normalized, axis=0, keepdims=True)
    write(pl2, me, two(total), two(cross), jnp.zeros((1, 128), F32))
    copies = spread_plane(pl2, p2_s, p2_r)
    centre = columns(13).astype(F32)
    block = (occ * (centre + normed * sigmoid)).astype(BF16)
    block_ref[...] = dot(to_bricks, block).astype(BF16).reshape(4, 64, 256)
    norm_s[...] = normalized
    for k in range(14, 27):
        cols_t[k] = columns(k).T
    meet_plane(copies, pl2, p2_s, p2_r)
    tiles = pl2[0]
    for i in range(1, PLANE):
        tiles = tiles + pl2[i]
    zs2[z] = tiles
    copies = spread_depth(zs2, z2_s, z2_r)
    meet_depth(copies, zs2, z2_s, z2_r)
    tiles = zs2[0]
    for i in range(1, Z):
        tiles = tiles + zs2[i]
    total, cross = one(tiles[0:2]), one(tiles[2:4])
    inverse_root = lax.rsqrt(voxel_count)
    ggrad_ref[...] = cross * inverse_root
    bgrad_ref[...] = total * inverse_root
    conv_grad = (gamma * inverse_std * (act_grad - total / voxel_count - norm_s[...] * cross / voxel_count) * occ).astype(BF16)
    cg_s[...] = conv_grad

    mine = jnp.where(c == 0, conv_grad[:, :128].astype(F32), conv_grad[:, 128:].astype(F32)).astype(BF16)
    other = jnp.where(c == 0, conv_grad[:, 128:].astype(F32), conv_grad[:, :128].astype(F32)).astype(BF16)
    halves = jnp.concatenate([mine, other], axis=1)
    sister = device(z, x, y, 1 - c)
    core_copies = []
    for part, (first, count, _) in enumerate(PARTS):
        for k in range(first, first + count):
            product = dot(cols_t[k], halves)
            own[k] = product[:, :128]
            osend[k] = product[:, 128:].astype(BF16)
        copy = pltpu.make_async_remote_copy(
            src_ref=osend.at[pl.ds(first, count)], dst_ref=crecv.at[pl.ds(first, count)],
            send_sem=c_s.at[part], recv_sem=c_r.at[part], device_id=sister, device_id_type=MESH)
        copy.start()
        core_copies.append(copy)

    grad_s[...] = jnp.zeros_like(grad_s)

    def column_grad(k):
        a, b, shift = k // 9, k // 3 % 3, k % 3
        product = lax.dot_general(cg_s[...], weight[k], (((1,), (1,)), ((), ())), preferred_element_type=F32)
        for i in range(4):
            start = (a + i) * 96 + b * 16
            grad_s[shift, start : start + 64, :] += product[i * 64 : (i + 1) * 64, :]

    for k in range(27):
        column_grad(k)

    spans = ((x, X, y, Y), (y, Y, x, X))

    def mate(part, stage, step):
        along_x = (part == 0) == (stage == 1)
        if along_x:
            return device(z, ahead(x, step, X), y, c)
        return device(z, x, ahead(y, step, Y), c)

    stage1 = []
    for part, (first, count, _) in enumerate(PARTS):
        core_copies[part].wait()
        place, length, _, _ = spans[part]
        for k in range(first, first + count):
            value = own[k] + crecv[k].astype(F32)
            own[k] = value
            s1[k] = value.astype(BF16)
        for step in range(1, length):
            target = ahead(place, step, length)
            copy = pltpu.make_async_remote_copy(
                src_ref=s1.at[pl.ds(first, count), pl.ds(pl.multiple_of(target * (256 // length), 16), 256 // length)],
                dst_ref=r1.at[step - 1, pl.ds(first, count), pl.ds(0, 256 // length)],
                send_sem=q1_s.at[part, step - 1], recv_sem=q1_r.at[part, step - 1],
                device_id=mate(part, 1, step), device_id_type=MESH)
            copy.start()
            stage1.append(copy)

    def brick_grad(rows):
        result = None
        for shift in range(3):
            value = grad_s[shift]
            high = value.astype(BF16)
            low = (value - high.astype(F32)).astype(BF16)
            select = gath[shift, :, rows]
            for piece in (high, low):
                term = lax.dot_general(select, piece, (((0,), (0,)), ((), ())), preferred_element_type=F32)
                result = term if result is None else result + term
        return result

    ghosts[...] = brick_grad(slice(256, 768)).astype(BF16).reshape(8, 64, 256)
    back = []
    for d in range(8):
        copy = pltpu.make_async_remote_copy(
            src_ref=ghosts.at[d], dst_ref=returned.at[d], send_sem=gh_s.at[d], recv_sem=gh_r.at[d],
            device_id=neighbour(-ROWS[d], -COLUMNS[d]), device_id_type=MESH)
        copy.start()
        back.append(copy)
    out_bricks = dot(to_bricks, out_masked.astype(BF16))
    local = out_bricks + brick_grad(slice(0, 256))
    for copy in back:
        copy.wait()
    for b in range(4):
        extra = local[b * 64 : (b + 1) * 64, :]
        for d in range(8):
            extra = extra + jnp.where(send_ref[0, d] == b, returned[d].astype(F32), 0.0)
        fgrad_ref[b] = (extra * occ_brick[b * 64 : (b + 1) * 64, :]).astype(BF16)

    for copy in stage1:
        copy.wait()
    stage2 = []
    for part, (first, count, _) in enumerate(PARTS):
        place, length, place2, length2 = spans[part]
        rows, rows2 = 256 // length, 256 // length // length2
        for k in range(first, first + count):
            value = own[k, pl.ds(pl.multiple_of(place * rows, 16), rows), :]
            for step in range(1, length):
                value = value + r1[step - 1, k, 0:rows, :].astype(F32)
            own[k, 0:rows, :] = value
            s2[k, 0:rows, :] = value.astype(BF16)
        for step in range(1, length2):
            target = ahead(place2, step, length2)
            copy = pltpu.make_async_remote_copy(
                src_ref=s2.at[pl.ds(first, count), pl.ds(pl.multiple_of(target * rows2, 16), rows2)],
                dst_ref=r2.at[step - 1, pl.ds(first, count), pl.ds(0, rows2)],
                send_sem=q2_s.at[part, step - 1], recv_sem=q2_r.at[part, step - 1],
                device_id=mate(part, 2, step), device_id_type=MESH)
            copy.start()
            stage2.append(copy)
    for copy in stage2:
        copy.wait()
    depth = 16 // Z
    small = 256 // (X * Y)
    for part, (first, count, base) in enumerate(PARTS):
        _, _, place2, length2 = spans[part]
        for k in range(16):
            if k < count:
                value = own[first + k, pl.ds(pl.multiple_of(place2 * small, 16), small), :]
                for step in range(1, length2):
                    value = value + r2[step - 1, first + k].astype(F32)
            else:
                value = jnp.zeros((small, 128), F32)
            s3[k // depth, part * depth + k % depth] = value
    stage3 = []
    for dz in range(1, Z):
        copy = pltpu.make_async_remote_copy(
            src_ref=s3.at[ahead(z, dz, Z)], dst_ref=r3.at[dz - 1], send_sem=q3_s.at[dz - 1], recv_sem=q3_r.at[dz - 1],
            device_id=device(ahead(z, dz, Z), x, y, c), device_id_type=MESH)
        copy.start()
        stage3.append(copy)
    for copy in stage3:
        copy.wait()
    value = s3[z]
    for dz in range(1, Z):
        value = value + r3[dz - 1]
    value = (value * inverse_root[:, :128].reshape(1, 1, 128)).astype(BF16)

    half = pl.ds(pl.multiple_of(c * 128, 128), 128)
    row_a = pl.ds(pl.multiple_of(x * (256 // X) + y * small, 16), small)
    row_b = pl.ds(pl.multiple_of(y * (256 // Y) + x * small, 16), small)
    blocks = ((0, row_a), (16, row_b))
    for part, (base, rows) in enumerate(blocks):
        outb[pl.ds(base + z * depth, depth), rows, half] = value[part * depth : (part + 1) * depth]

    def push(where, send, receive, target):
        return pltpu.make_async_remote_copy(
            src_ref=outb.at[where], dst_ref=outb.at[where], send_sem=send, recv_sem=receive,
            device_id=target, device_id_type=MESH)

    here = device(z, x, y, c)
    sent = []
    for part, (base, rows) in enumerate(blocks):
        for dz in range(1, Z):
            copy = push((pl.ds(base + z * depth, depth), rows, half), a3_s.at[part, dz - 1], a3_r.at[part, dz - 1],
                        device(ahead(z, dz, Z), x, y, c))
            copy.start()
            sent.append(copy)
    for part, (base, rows) in enumerate(blocks):
        for dz in range(1, Z):
            push((pl.ds(base + ahead(z, -dz, Z) * depth, depth), rows, half), a3_s.at[part, dz - 1],
                 a3_r.at[part, dz - 1], here).wait_recv()
    for part, (first, count, base) in enumerate(PARTS):
        _, _, _, length2 = spans[part]
        for step in range(1, length2):
            copy = push((pl.ds(base, count), blocks[part][1], half), a2_s.at[part, step - 1], a2_r.at[part, step - 1],
                        mate(part, 2, step))
            copy.start()
            sent.append(copy)
    for part, (first, count, base) in enumerate(PARTS):
        place, length, place2, length2 = spans[part]
        for step in range(1, length2):
            start = place * (256 // length) + ahead(place2, -step, length2) * small
            push((pl.ds(base, count), pl.ds(pl.multiple_of(start, 16), small), half), a2_s.at[part, step - 1],
                 a2_r.at[part, step - 1], here).wait_recv()
    for part, (first, count, base) in enumerate(PARTS):
        place, length, place2, length2 = spans[part]
        span = pl.ds(pl.multiple_of(place * (256 // length), 16), 256 // length)
        for step in range(1, length):
            copy = push((pl.ds(base, count), span, half), a1_s.at[part, step - 1], a1_r.at[part, step - 1],
                        mate(part, 1, step))
            copy.start()
            sent.append(copy)
    for part, (first, count, base) in enumerate(PARTS):
        place, length, place2, length2 = spans[part]
        for step in range(1, length):
            start = ahead(place, -step, length) * (256 // length)
            push((pl.ds(base, count), pl.ds(pl.multiple_of(start, 16), 256 // length), half), a1_s.at[part, step - 1],
                 a1_r.at[part, step - 1], here).wait_recv()
    for part, (first, count, base) in enumerate(PARTS):
        copy = push((pl.ds(base, count), pl.ds(0, 256), half), a0_s.at[part], a0_r.at[part], sister)
        copy.start()
        sent.append(copy)
    other_half = pl.ds(pl.multiple_of((1 - c) * 128, 128), 128)
    last = []
    for part, (first, count, base) in enumerate(PARTS):
        push((pl.ds(base, count), pl.ds(0, 256), other_half), a0_s.at[part], a0_r.at[part], here).wait_recv()
        copy = pltpu.make_async_copy(outb.at[pl.ds(base, count)], wgrad_ref.at[pl.ds(first, count)], o_sem.at[part])
        copy.start()
        last.append(copy)
    for copy in sent:
        copy.wait_send()
    for copy in last:
        copy.wait()


def on_device(features, occupancy, neighbours, send_list, weight, gamma, beta, out_grad):
    vmem = pl.BlockSpec(memory_space=pltpu.VMEM)
    small = 256 // (X * Y)
    near, far = max(X, Y) - 1, Z - 1
    depth = 16 // Z
    dma = pltpu.SemaphoreType.DMA
    scratch = [
        pltpu.VMEM((16, 128), F32),
        pltpu.VMEM((256, 256), F32),
        pltpu.VMEM((4, 64, 256), BF16),
        pltpu.VMEM((8, 64, 256), BF16),
        pltpu.VMEM((12, 64, 256), BF16),
        pltpu.VMEM((3, 576, 768), BF16),
        pltpu.VMEM((3, 576, 256), BF16),
        pltpu.VMEM((27, 256, 256), BF16),
        pltpu.VMEM((256, 256), F32),
        pltpu.VMEM((256, 256), F32),
        pltpu.VMEM((27, 256, 256), BF16),
        pltpu.VMEM((PLANE, 8, 128), F32),
        pltpu.VMEM((Z, 8, 128), F32),
        pltpu.VMEM((PLANE, 8, 128), F32),
        pltpu.VMEM((Z, 8, 128), F32),
        pltpu.VMEM((256, 256), BF16),
        pltpu.VMEM((3, 576, 256), F32),
        pltpu.VMEM((8, 64, 256), BF16),
        pltpu.VMEM((8, 64, 256), BF16),
        pltpu.VMEM((27, 256, 128), F32),
        pltpu.VMEM((27, 256, 128), BF16),
        pltpu.VMEM((27, 256, 128), BF16),
        pltpu.VMEM((27, 256, 128), BF16),
        pltpu.VMEM((near, 27, 256 // min(X, Y), 128), BF16),
        pltpu.VMEM((27, 256 // min(X, Y), 128), BF16),
        pltpu.VMEM((near, 27, small, 128), BF16),
        pltpu.VMEM((Z, 2 * depth, small, 128), F32),
        pltpu.VMEM((far, 2 * depth, small, 128), F32),
        pltpu.VMEM((32, 256, 256), BF16),
        dma, dma((8,)), dma((8,)),
        dma((PLANE - 1,)), dma((PLANE - 1,)), dma((far,)), dma((far,)),
        dma((PLANE - 1,)), dma((PLANE - 1,)), dma((far,)), dma((far,)),
        dma((8,)), dma((8,)), dma((2,)), dma((2,)),
        dma((2, near)), dma((2, near)), dma((2, near)), dma((2, near)), dma((far,)), dma((far,)),
        dma((2, far)), dma((2, far)), dma((2, near)), dma((2, near)), dma((2, near)), dma((2, near)),
        dma((2,)), dma((2,)), dma((2,)),
    ]
    block, fgrad, wgrad, ggrad, bgrad = pl.pallas_call(
        kernel,
        name="brick_block",
        out_shape=(
            jax.ShapeDtypeStruct((4, 64, 256), BF16),
            jax.ShapeDtypeStruct((4, 64, 256), BF16),
            jax.ShapeDtypeStruct((27, 256, 256), BF16),
            jax.ShapeDtypeStruct((1, 256), F32),
            jax.ShapeDtypeStruct((1, 256), F32),
        ),
        in_specs=[vmem, vmem, pl.BlockSpec(memory_space=pltpu.SMEM), vmem, vmem, vmem, vmem,
                  pl.BlockSpec(memory_space=pl.ANY)],
        out_specs=(vmem, vmem, pl.BlockSpec(memory_space=pl.ANY), vmem, vmem),
        scratch_shapes=scratch,
        compiler_params=pltpu.CompilerParams(
            collective_id=0, has_side_effects=True, vmem_limit_bytes=56 * 2**20),
    )(occupancy, neighbours, send_list.reshape(1, 8), features, gamma.reshape(1, 256), beta.reshape(1, 256), out_grad, weight)
    return block, fgrad, wgrad, ggrad.reshape(256), bgrad.reshape(256)


def solution(mesh):
    placed = (
        P(("gx", "gy"), None, None),
        P(("gx", "gy"), None),
        P(("gx", "gy"), None),
        P(("gx", "gy"), None, None),
        P(),
        P(),
        P(),
        P(("gx", "gy"), None, None),
    )
    return jax.shard_map(
        on_device,
        mesh=mesh,
        in_specs=placed,
        out_specs=(P(("gx", "gy"), None, None), P(("gx", "gy"), None, None), P(), P(), P()),
        check_vma=False,
    )
```

```python
import functools

import jax
import jax.numpy as jnp
from jax import lax
from jax.experimental import pallas as pl
from jax.experimental.pallas import tpu as pltpu
from jax.sharding import PartitionSpec as P

Z, X, YH, YL = 8, 4, 2, 2
Y = YH * YL

ROWS = (-1, -1, -1, 0, 0, 1, 1, 1)
COLUMNS = (-1, 0, 1, -1, 1, -1, 0, 1)
EPSILON = 1e-05
MESH = pl.DeviceIdType.MESH
F32, BF16, I32 = jnp.float32, jnp.bfloat16, jnp.int32

PIECES = ((0, 8, True), (8, 8, False), (16, 6, True), (22, 5, False))


def coordinates():
    gx, gy = lax.axis_index("gx"), lax.axis_index("gy")
    z = lax.div(gx, X * YH)
    x = lax.rem(lax.div(gx, YH), X)
    y = lax.rem(gx, YH) * YL + lax.div(gy, 2)
    return z, x, y, lax.rem(gy, 2)


def device(z, x, y, c):
    return (z * (X * YH) + x * YH + lax.div(y, YL), lax.rem(y, YL) * 2 + c)


def ahead(value, steps, count):
    return lax.rem(value + (steps + count) % count, count)


def dot(a, b):
    return jnp.dot(a, b, preferred_element_type=F32)


def place_row(p):
    return (p >= 1).astype(I32) + (p >= 5).astype(I32)


def kernel(
    occ_hbm, nb_hbm, send_ref, feat_hbm, gamma_hbm, beta_hbm, og_hbm, w_hbm,
    block_ref, fgrad_ref, outb, ggrad_ref, bgrad_ref,
    occ_ref, nb_ref, feat_ref, gamma_ref, beta_ref, og_ref, tab, occn, masked, packets, ext, gath, gath_t, slabs, weight, conv_s, norm_s, cols_t,
    deep1, wide1, deep2, wide2,
    cg_s, grad_s, local_s, ghosts, returned,
    own, osend, crecv, s1, r1, s2, r2, s3, r3,
    in_sem, halo_s, halo_r, d1_s, d1_r, w1_s, w1_r, d2_s, d2_r, w2_s, w2_r,
    gh_s, gh_r, c_s, c_r, q1_s, q1_r, q2_s, q2_r, q3_s, q3_r, a3_s, a3_r, a2_s, a2_r, a1_s, a1_r, a0_s, a0_r,
):
    z, x, y, c = coordinates()
    gx, gy = lax.axis_index("gx"), lax.axis_index("gy")
    ngx, ngy = Z * X * YH, YL * 2

    def neighbour(u, v):
        return (ahead(gx, u, ngx), ahead(gy, v, ngy))

    deep_group = [
        (device(ahead(z, dz, Z), x, y, ahead(c, dc, 2)), ahead(z, -dz, Z) * 2 + ahead(c, dc, 2))
        for dz in range(Z) for dc in range(2) if dz + dc > 0]
    wide_group = [
        (device(z, ahead(x, dx, X), ahead(y, dy, Y), c), ahead(x, -dx, X) * Y + ahead(y, -dy, Y))
        for dx in range(X) for dy in range(Y) if dx + dy > 0]

    barrier = pltpu.get_barrier_semaphore()
    friends = [neighbour(ROWS[d], COLUMNS[d]) for d in range(8)]
    friends += [friend for friend, _ in deep_group + wide_group]
    for friend in friends:
        pl.semaphore_signal(barrier, inc=1, device_id=friend, device_id_type=MESH)

    inputs = [
        pltpu.make_async_copy(source, target, in_sem.at[i])
        for i, (source, target) in enumerate((
            (occ_hbm, occ_ref), (feat_hbm, feat_ref), (nb_hbm, nb_ref), (og_hbm, og_ref),
            (gamma_hbm, gamma_ref), (beta_hbm, beta_ref), (w_hbm, weight)))]
    for copy in inputs:
        copy.start()

    tab[...] = jnp.zeros_like(tab)
    inputs[0].wait()
    inputs[1].wait()
    tab[0:4, 0:64] = occ_ref[...].astype(F32)

    def pick(first, index):
        rows = [tab[first + n : first + n + 1, :] for n in range(4)]
        return jnp.where(index == 0, rows[0], jnp.where(index == 1, rows[1], jnp.where(index == 2, rows[2], rows[3])))

    def iotas(rows, lanes):
        shape = (rows, lanes)
        return lax.broadcasted_iota(I32, shape, 0), lax.broadcasted_iota(I32, shape, 1)

    ones = jnp.ones((128, 256), BF16)
    row, lane = iotas(256, 128)
    by_brick = jnp.where(lane == jnp.bitwise_and(row, 63), pick(0, jnp.right_shift(row, 6)), 0.0)
    occ_brick = dot(by_brick.astype(BF16), ones)
    feat = feat_ref[...].reshape(256, 256)
    masked_value = (feat.astype(F32) * occ_brick).astype(BF16)
    masked[...] = masked_value.reshape(4, 64, 256)
    ext[0:4] = masked_value.reshape(4, 64, 256)
    for d in range(8):
        packets[d] = masked[send_ref[0, d]]

    pl.semaphore_wait(barrier, len(friends))
    halo = []
    for d in range(8):
        copy = pltpu.make_async_remote_copy(
            src_ref=packets.at[d], dst_ref=ext.at[4 + d], send_sem=halo_s.at[d], recv_sem=halo_r.at[d],
            device_id=neighbour(ROWS[d], COLUMNS[d]), device_id_type=MESH)
        copy.start()
        halo.append(copy)

    for copy in inputs[2:6]:
        copy.wait()
    by_voxel = jnp.where(
        lane == jnp.right_shift(row, 4) * 4 + jnp.bitwise_and(row, 3),
        pick(0, jnp.bitwise_and(jnp.right_shift(row, 2), 3)), 0.0)
    occ = dot(by_voxel.astype(BF16), ones)
    occn[...] = occ
    row, lane = iotas(256, 256)
    order = jnp.bitwise_and(jnp.right_shift(row, 2), 3) * 64 + jnp.right_shift(row, 4) * 4 + jnp.bitwise_and(row, 3)
    to_rows = jnp.where(lane == order, occ, 0.0).astype(BF16)
    order = jnp.bitwise_and(jnp.right_shift(lane, 2), 3) * 64 + jnp.right_shift(lane, 4) * 4 + jnp.bitwise_and(lane, 3)
    to_bricks = jnp.where(row == order, 1.0, 0.0).astype(BF16)
    out_masked = dot(to_rows, og_ref[...].reshape(256, 256))

    tab[8:12, 0:27] = nb_ref[...].astype(F32)
    table = tab[8:16, :]
    for d in range(8):
        u, v = ROWS[d], COLUMNS[d]
        missing = jnp.int32(0)
        if u != 0:
            missing = missing + (gx == (0 if u > 0 else ngx - 1)).astype(I32)
        if v != 0:
            missing = missing + (gy == (0 if v > 0 else ngy - 1)).astype(I32)
        table = jnp.where((table == 4.0 + d) & (missing > 0), 12.0, table)
    tab[8:16, :] = table
    row, lane = iotas(576, 128)
    pq = jnp.right_shift(row, 4)
    p = jnp.right_shift(pq * 43, 8)
    q = pq - 6 * p
    brick, w = jnp.bitwise_and(jnp.right_shift(row, 2), 3), jnp.bitwise_and(row, 3)
    places = 9 * place_row(p) + 3 * place_row(q)
    voxels = 16 * jnp.bitwise_and(p + 3, 3) + 4 * jnp.bitwise_and(q + 3, 3)
    near = pick(8, brick)
    lane_f = lane.astype(F32)
    for shift in range(3):
        cell = w + shift
        found = dot(jnp.where(lane == places + place_row(cell), near, 0.0).astype(BF16), jnp.ones((128, 128), BF16))
        source = found * 64.0 + (voxels + jnp.bitwise_and(cell + 3, 3)).astype(F32)
        for j in range(6):
            gath[shift, :, j * 128 : (j + 1) * 128] = jnp.where(source == lane_f + 128.0 * j, 1.0, 0.0).astype(BF16)

    for copy in halo:
        copy.wait()
    extended = ext[...].reshape(768, 256)
    for shift in range(3):
        slabs[shift] = dot(gath[shift], extended).astype(BF16)

    def columns(k):
        a, b, shift = k // 9, k // 3 % 3, k % 3
        return jnp.concatenate(
            [slabs[shift, (a + i) * 96 + b * 16 : (a + i) * 96 + b * 16 + 64, :] for i in range(4)], axis=0)

    inputs[6].wait()
    conv = dot(columns(0), weight[0])
    for k in range(1, 27):
        conv = conv + dot(columns(k), weight[k])
    conv = conv * occ

    def two(value):
        return jnp.concatenate([value[:, :128], value[:, 128:]], axis=0)

    def one(tile):
        return jnp.concatenate([tile[0:1, :], tile[1:2, :]], axis=1)

    def spread(buffer, place, group, send, receive):
        copies = []
        for i, (friend, _) in enumerate(group):
            copy = pltpu.make_async_remote_copy(
                src_ref=buffer.at[place], dst_ref=buffer.at[place], send_sem=send.at[i], recv_sem=receive.at[i],
                device_id=friend, device_id_type=MESH)
            copy.start()
            copies.append(copy)
        return copies

    def meet(copies, buffer, group, send, receive):
        for i, (friend, behind) in enumerate(group):
            pltpu.make_async_remote_copy(
                src_ref=buffer.at[behind], dst_ref=buffer.at[behind], send_sem=send.at[i], recv_sem=receive.at[i],
                device_id=friend, device_id_type=MESH).wait_recv()
        for copy in copies:
            copy.wait_send()

    deep, wide = z * 2 + c, x * Y + y

    def sum_of(buffer, count):
        total = buffer[0]
        for i in range(1, count):
            total = total + buffer[i]
        return total

    def merge(buffer, count):
        tiles = [buffer[i] for i in range(count)]
        total = sum(tiles[1:], tiles[0])
        mean = total[0:2, :] / jnp.maximum(total[4:5, :], 1.0)
        square = total[2:4, :]
        for tile in tiles:
            gap = tile[0:2, :] / jnp.maximum(tile[4:5, :], 1.0) - mean
            square = square + tile[4:5, :] * gap * gap
        return total[0:2, :], square, total[4:5, :]

    def write(buffer, place, sums, squares, number):
        buffer[place] = jnp.concatenate([sums, squares, number, jnp.zeros((3, 128), F32)], axis=0)

    number = jnp.sum(occ, axis=0, keepdims=True)
    sums = jnp.sum(conv, axis=0, keepdims=True)
    centred = (conv - sums / jnp.maximum(number, 1.0)) * occ
    squares = jnp.sum(centred * centred, axis=0, keepdims=True)
    write(deep1, deep, two(sums), two(squares), number[:, :128])
    copies = spread(deep1, deep, deep_group, d1_s, d1_r)
    conv_s[...] = conv
    for k in range(14):
        cols_t[k] = columns(k).T
    meet(copies, deep1, deep_group, d1_s, d1_r)
    write(wide1, wide, *merge(deep1, 2 * Z))
    copies = spread(wide1, wide, wide_group, w1_s, w1_r)
    for shift in range(2):
        gath_t[shift] = gath[shift].T
    meet(copies, wide1, wide_group, w1_s, w1_r)
    sums, squares, number = merge(wide1, X * Y)
    voxel_count = jnp.concatenate([number, number], axis=1)
    average = one(sums) / voxel_count
    inverse_std = lax.rsqrt(one(squares) / voxel_count + EPSILON)
    gamma, beta = gamma_ref[...], beta_ref[...]
    occ = occn[...]
    normalized = (conv_s[...] - average) * inverse_std
    normed = gamma * normalized + beta
    sigmoid = 1.0 / (1.0 + jnp.exp(-normed))
    act_grad = out_masked * sigmoid * (1.0 + normed * (1.0 - sigmoid))
    total = jnp.sum(act_grad, axis=0, keepdims=True)
    cross = jnp.sum(act_grad * normalized, axis=0, keepdims=True)
    write(deep2, deep, two(total), two(cross), jnp.zeros((1, 128), F32))
    copies = spread(deep2, deep, deep_group, d2_s, d2_r)
    centre = columns(13).astype(F32)
    block = (occ * (centre + normed * sigmoid)).astype(BF16)
    block_ref[...] = dot(to_bricks, block).astype(BF16).reshape(4, 64, 256)
    norm_s[...] = normalized
    for k in range(14, 27):
        cols_t[k] = columns(k).T
    meet(copies, deep2, deep_group, d2_s, d2_r)
    wide2[wide] = sum_of(deep2, 2 * Z)
    copies = spread(wide2, wide, wide_group, w2_s, w2_r)
    gath_t[2] = gath[2].T
    meet(copies, wide2, wide_group, w2_s, w2_r)
    tiles = sum_of(wide2, X * Y)
    total, cross = one(tiles[0:2]), one(tiles[2:4])
    inverse_root = lax.rsqrt(voxel_count)
    ggrad_ref[...] = cross * inverse_root
    bgrad_ref[...] = total * inverse_root
    conv_grad = (gamma * inverse_std * (act_grad - total / voxel_count - norm_s[...] * cross / voxel_count) * occ).astype(BF16)
    cg_s[...] = conv_grad

    mine = jnp.where(c == 0, conv_grad[:, :128].astype(F32), conv_grad[:, 128:].astype(F32)).astype(BF16)
    other = jnp.where(c == 0, conv_grad[:, 128:].astype(F32), conv_grad[:, :128].astype(F32)).astype(BF16)
    halves = jnp.concatenate([mine, other], axis=1)
    sister, here = device(z, x, y, 1 - c), device(z, x, y, c)
    small = 256 // (X * Y)
    half = pl.ds(pl.multiple_of(c * 128, 128), 128)
    other_half = pl.ds(pl.multiple_of((1 - c) * 128, 128), 128)
    depth = 8 // Z

    def axes(piece):
        return ((x, X), (y, Y)) if PIECES[piece][2] else ((y, Y), (x, X))

    def mate(piece, stage, step):
        if PIECES[piece][2] == (stage == 1):
            return device(z, ahead(x, step, X), y, c)
        return device(z, x, ahead(y, step, Y), c)

    def span(start, size):
        return pl.ds(pl.multiple_of(start, 16), size)

    def remote(source, target, send, receive, to):
        return pltpu.make_async_remote_copy(
            src_ref=source, dst_ref=target, send_sem=send, recv_sem=receive, device_id=to, device_id_type=MESH)

    going = {}
    sent = []

    def arrive(stage, piece):
        for copy in going.pop((stage, piece)):
            copy.wait()

    def heard(stage, piece):
        for copy in going.pop((stage, piece)):
            copy.wait_recv()

    def products(piece):
        first, count, _ = PIECES[piece]
        for k in range(first, first + count):
            product = dot(cols_t[k], halves)
            own[k] = product[:, :128]
            osend[k] = product[:, 128:].astype(BF16)
        copy = remote(osend.at[pl.ds(first, count)], crecv.at[pl.ds(first, count)], c_s.at[piece], c_r.at[piece], sister)
        copy.start()
        going["core", piece] = [copy]

    def stage1(piece):
        first, count, _ = PIECES[piece]
        (place, length), _ = axes(piece)
        rows = 256 // length
        arrive("core", piece)
        for k in range(first, first + count):
            value = own[k] + crecv[k].astype(F32)
            own[k] = value
            s1[k] = value.astype(BF16)
        going["one", piece] = []
        for step in range(1, length):
            copy = remote(
                s1.at[pl.ds(first, count), span(ahead(place, step, length) * rows, rows)],
                r1.at[step - 1, pl.ds(first, count)],
                q1_s.at[piece, step - 1], q1_r.at[piece, step - 1], mate(piece, 1, step))
            copy.start()
            going["one", piece].append(copy)

    def stage2(piece):
        first, count, _ = PIECES[piece]
        (place, length), (place2, length2) = axes(piece)
        rows = 256 // length
        arrive("one", piece)
        for k in range(first, first + count):
            value = own[k, span(place * rows, rows), :]
            for step in range(1, length):
                value = value + r1[step - 1, k].astype(F32)
            own[k, 0:rows, :] = value
            s2[k] = value.astype(BF16)
        going["two", piece] = []
        for step in range(1, length2):
            copy = remote(
                s2.at[pl.ds(first, count), span(ahead(place2, step, length2) * small, small)],
                r2.at[step - 1, pl.ds(first, count)],
                q2_s.at[piece, step - 1], q2_r.at[piece, step - 1], mate(piece, 2, step))
            copy.start()
            going["two", piece].append(copy)

    def stage3(piece):
        first, count, _ = PIECES[piece]
        _, (place2, length2) = axes(piece)
        arrive("two", piece)
        for k in range(8):
            if k < count:
                value = own[first + k, span(place2 * small, small), :]
                for step in range(1, length2):
                    value = value + r2[step - 1, first + k].astype(F32)
            else:
                value = jnp.zeros((small, 128), F32)
            s3[piece, k] = value
        going["three", piece] = []
        for dz in range(1, Z):
            copy = remote(
                s3.at[piece, pl.ds(ahead(z, dz, Z) * depth, depth)], r3.at[piece, dz - 1],
                q3_s.at[piece, dz - 1], q3_r.at[piece, dz - 1], device(ahead(z, dz, Z), x, y, c))
            copy.start()
            going["three", piece].append(copy)

    def fine(piece):
        (place, length), (place2, _) = axes(piece)
        return span(place * (256 // length) + place2 * small, small)

    def push(where, send, receive, to):
        return remote(outb.at[where], outb.at[where], send, receive, to)

    def back3(piece):
        arrive("three", piece)
        value = s3[piece, pl.ds(z * depth, depth)]
        for dz in range(1, Z):
            value = value + r3[piece, dz - 1]
        where = (pl.ds(piece * 8 + z * depth, depth), fine(piece), half)
        outb[where] = (value * inverse_root[:, :128].reshape(1, 1, 128)).astype(BF16)
        going["back3", piece] = []
        for dz in range(1, Z):
            copy = push(where, a3_s.at[piece, dz - 1], a3_r.at[piece, dz - 1], device(ahead(z, dz, Z), x, y, c))
            copy.start()
            sent.append(copy)
            going["back3", piece].append(push(
                (pl.ds(piece * 8 + ahead(z, -dz, Z) * depth, depth), fine(piece), half), a3_s.at[piece, dz - 1],
                a3_r.at[piece, dz - 1], here))

    def back2(piece):
        _, count, _ = PIECES[piece]
        (place, length), (place2, length2) = axes(piece)
        heard("back3", piece)
        going["back2", piece] = []
        for step in range(1, length2):
            copy = push((pl.ds(piece * 8, count), fine(piece), half), a2_s.at[piece, step - 1], a2_r.at[piece, step - 1],
                        mate(piece, 2, step))
            copy.start()
            sent.append(copy)
            start = place * (256 // length) + ahead(place2, -step, length2) * small
            going["back2", piece].append(push(
                (pl.ds(piece * 8, count), span(start, small), half), a2_s.at[piece, step - 1], a2_r.at[piece, step - 1],
                here))

    def back1(piece):
        _, count, _ = PIECES[piece]
        (place, length), _ = axes(piece)
        rows = 256 // length
        heard("back2", piece)
        going["back1", piece] = []
        for step in range(1, length):
            copy = push((pl.ds(piece * 8, count), span(place * rows, rows), half), a1_s.at[piece, step - 1],
                        a1_r.at[piece, step - 1], mate(piece, 1, step))
            copy.start()
            sent.append(copy)
            going["back1", piece].append(push(
                (pl.ds(piece * 8, count), span(ahead(place, -step, length) * rows, rows), half),
                a1_s.at[piece, step - 1], a1_r.at[piece, step - 1], here))

    def back0(piece):
        _, count, _ = PIECES[piece]
        heard("back1", piece)
        copy = push((pl.ds(piece * 8, count), pl.ds(0, 256), half), a0_s.at[piece], a0_r.at[piece], sister)
        copy.start()
        sent.append(copy)
        going["back0", piece] = [
            push((pl.ds(piece * 8, count), pl.ds(0, 256), other_half), a0_s.at[piece], a0_r.at[piece], here)]

    def finish(piece):
        heard("back0", piece)

    def column_grads():
        grad_s[...] = jnp.zeros_like(grad_s)
        for k in range(27):
            a, b, shift = k // 9, k // 3 % 3, k % 3
            product = lax.dot_general(cg_s[...], weight[k], (((1,), (1,)), ((), ())), preferred_element_type=F32)
            for i in range(4):
                start = (a + i) * 96 + b * 16
                grad_s[shift, start : start + 64, :] += product[i * 64 : (i + 1) * 64, :]

    def brick_grads():
        result = None
        for shift in range(3):
            value = grad_s[shift]
            high = value.astype(BF16)
            low = (value - high.astype(F32)).astype(BF16)
            term = dot(gath_t[shift], jnp.concatenate([high, low], axis=1))
            result = term if result is None else result + term
        result = result[:, :256] + result[:, 256:]
        local_s[...] = result[:256]
        ghosts[...] = result[256:].astype(BF16).reshape(8, 64, 256)
        going["ghosts", 0] = []
        for d in range(8):
            copy = remote(ghosts.at[d], returned.at[d], gh_s.at[d], gh_r.at[d], neighbour(-ROWS[d], -COLUMNS[d]))
            copy.start()
            going["ghosts", 0].append(copy)

    def feature_grads():
        out_bricks = dot(to_bricks, out_masked.astype(BF16))
        arrive("ghosts", 0)
        for b in range(4):
            rows = slice(b * 64, (b + 1) * 64)
            extra = out_bricks[rows] + local_s[rows, :]
            for d in range(8):
                extra = extra + jnp.where(send_ref[0, d] == b, returned[d].astype(F32), 0.0)
            fgrad_ref[b] = (extra * occ_brick[rows]).astype(BF16)

    schedule = (
        (products, 0), (products, 1), (products, 2), (products, 3),
        (stage1, 0), (stage1, 1), (stage1, 2), (stage1, 3),
        (column_grads,), (brick_grads,),
        (stage2, 0), (stage2, 1),
        (stage2, 2), (stage2, 3),
        (stage3, 0), (stage3, 1),
        (feature_grads,),
        (stage3, 2), (stage3, 3),
        (back3, 0), (back3, 1),
        (back3, 2), (back3, 3),
        (back2, 0), (back2, 1),
        (back2, 2), (back2, 3),
        (back1, 0), (back1, 1),
        (back1, 2), (back1, 3),
        (back0, 0), (back0, 1), (back0, 2), (back0, 3),
        (finish, 0), (finish, 1), (finish, 2), (finish, 3),
    )
    for step, *piece in schedule:
        step(*piece)
    for copy in sent:
        copy.wait_send()


def write_out(block, fgrad, wgrad, ggrad, bgrad, block_out, fgrad_out, wgrad_out, ggrad_out, bgrad_out, sems):
    pairs = [(block, block_out), (fgrad, fgrad_out), (ggrad, ggrad_out), (bgrad, bgrad_out)]
    for piece, (first, count, _) in enumerate(PIECES):
        pairs.append((wgrad.at[pl.ds(piece * 8, count)], wgrad_out.at[pl.ds(first, count)]))
    copies = [pltpu.make_async_copy(source, target, sems.at[i]) for i, (source, target) in enumerate(pairs)]
    for copy in copies:
        copy.start()
    for copy in copies:
        copy.wait()


def on_device(features, occupancy, neighbours, send_list, weight, gamma, beta, out_grad):
    vmem = pl.BlockSpec(memory_space=pltpu.VMEM)
    small = 256 // (X * Y)
    near, far = max(X, Y) - 1, Z - 1
    depth = 8 // Z
    pieces = len(PIECES)
    dma = pltpu.SemaphoreType.DMA
    scratch = [
        pltpu.VMEM((4, 64), I32),
        pltpu.VMEM((4, 27), I32),
        pltpu.VMEM((4, 64, 256), BF16),
        pltpu.VMEM((1, 256), F32),
        pltpu.VMEM((1, 256), F32),
        pltpu.VMEM((4, 64, 256), BF16),
        pltpu.VMEM((16, 128), F32),
        pltpu.VMEM((256, 256), F32),
        pltpu.VMEM((4, 64, 256), BF16),
        pltpu.VMEM((8, 64, 256), BF16),
        pltpu.VMEM((12, 64, 256), BF16),
        pltpu.VMEM((3, 576, 768), BF16),
        pltpu.VMEM((3, 768, 576), BF16),
        pltpu.VMEM((3, 576, 256), BF16),
        pltpu.VMEM((27, 256, 256), BF16),
        pltpu.VMEM((256, 256), F32),
        pltpu.VMEM((256, 256), F32),
        pltpu.VMEM((27, 256, 256), BF16),
        pltpu.VMEM((2 * Z, 8, 128), F32),
        pltpu.VMEM((X * Y, 8, 128), F32),
        pltpu.VMEM((2 * Z, 8, 128), F32),
        pltpu.VMEM((X * Y, 8, 128), F32),
        pltpu.VMEM((256, 256), BF16),
        pltpu.VMEM((3, 576, 256), F32),
        pltpu.VMEM((256, 256), F32),
        pltpu.VMEM((8, 64, 256), BF16),
        pltpu.VMEM((8, 64, 256), BF16),
        pltpu.VMEM((27, 256, 128), F32),
        pltpu.VMEM((27, 256, 128), BF16),
        pltpu.VMEM((27, 256, 128), BF16),
        pltpu.VMEM((27, 256, 128), BF16),
        pltpu.VMEM((near, 27, 256 // min(X, Y), 128), BF16),
        pltpu.VMEM((27, 256 // min(X, Y), 128), BF16),
        pltpu.VMEM((near, 27, small, 128), BF16),
        pltpu.VMEM((pieces, 8, small, 128), F32),
        pltpu.VMEM((pieces, far, depth, small, 128), F32),
        dma((7,)), dma((8,)), dma((8,)),
        dma((2 * Z - 1,)), dma((2 * Z - 1,)), dma((X * Y - 1,)), dma((X * Y - 1,)),
        dma((2 * Z - 1,)), dma((2 * Z - 1,)), dma((X * Y - 1,)), dma((X * Y - 1,)),
        dma((8,)), dma((8,)), dma((pieces,)), dma((pieces,)),
        dma((pieces, near)), dma((pieces, near)), dma((pieces, near)), dma((pieces, near)),
        dma((pieces, far)), dma((pieces, far)),
        dma((pieces, far)), dma((pieces, far)), dma((pieces, near)), dma((pieces, near)),
        dma((pieces, near)), dma((pieces, near)), dma((pieces,)), dma((pieces,)),
    ]
    anywhere = pl.BlockSpec(memory_space=pl.ANY)
    results = pl.pallas_call(
        kernel,
        name="brick_block",
        out_shape=(
            pltpu.VMEM((4, 64, 256), BF16),
            pltpu.VMEM((4, 64, 256), BF16),
            pltpu.VMEM((32, 256, 256), BF16),
            pltpu.VMEM((1, 256), F32),
            pltpu.VMEM((1, 256), F32),
        ),
        in_specs=[anywhere, anywhere, pl.BlockSpec(memory_space=pltpu.SMEM)] + [anywhere] * 5,
        out_specs=(vmem, vmem, vmem, vmem, vmem),
        scratch_shapes=scratch,
        compiler_params=pltpu.CompilerParams(
            collective_id=0, has_side_effects=True, vmem_limit_bytes=56 * 2**20),
    )(occupancy, neighbours, send_list.reshape(1, 8), features, gamma.reshape(1, 256), beta.reshape(1, 256), out_grad, weight)
    block, fgrad, wgrad, ggrad, bgrad = pl.pallas_call(
        write_out,
        name="write_out",
        out_shape=(
            jax.ShapeDtypeStruct((4, 64, 256), BF16),
            jax.ShapeDtypeStruct((4, 64, 256), BF16),
            jax.ShapeDtypeStruct((27, 256, 256), BF16),
            jax.ShapeDtypeStruct((1, 256), F32),
            jax.ShapeDtypeStruct((1, 256), F32),
        ),
        in_specs=[anywhere] * 5,
        out_specs=(anywhere,) * 5,
        scratch_shapes=[dma((4 + pieces,))],
        compiler_params=pltpu.CompilerParams(vmem_limit_bytes=8 * 2**20),
    )(*results)
    return block, fgrad, wgrad, ggrad.reshape(256), bgrad.reshape(256)


def solution(mesh):
    placed = (
        P(("gx", "gy"), None, None),
        P(("gx", "gy"), None),
        P(("gx", "gy"), None),
        P(("gx", "gy"), None, None),
        P(),
        P(),
        P(),
        P(("gx", "gy"), None, None),
    )
    return jax.shard_map(
        on_device,
        mesh=mesh,
        in_specs=placed,
        out_specs=(P(("gx", "gy"), None, None), P(("gx", "gy"), None, None), P(), P(), P()),
        check_vma=False,
    )
```

```python
import functools

import jax
import jax.numpy as jnp
from jax import lax
from jax.experimental import pallas as pl
from jax.experimental.pallas import tpu as pltpu
from jax.sharding import PartitionSpec as P

Z, X, YH, YL = 8, 4, 2, 2
Y = YH * YL

ROWS = (-1, -1, -1, 0, 0, 1, 1, 1)
COLUMNS = (-1, 0, 1, -1, 1, -1, 0, 1)
EPSILON = 1e-05
MESH = pl.DeviceIdType.MESH
F32, BF16, I32 = jnp.float32, jnp.bfloat16, jnp.int32

PARTS = ((0, 14), (14, 13))
PIECES = ((0, 6, 0), (14, 6, 1), (6, 8, 0), (20, 7, 1))


def far_first(count):
    return sorted(range(1, count), key=lambda step: -min(step, count - step))


def coordinates():
    gx, gy = lax.axis_index("gx"), lax.axis_index("gy")
    z = lax.div(gx, X * YH)
    x = lax.rem(lax.div(gx, YH), X)
    y = lax.rem(gx, YH) * YL + lax.div(gy, 2)
    return z, x, y, lax.rem(gy, 2)


def device(z, x, y, c):
    return (z * (X * YH) + x * YH + lax.div(y, YL), lax.rem(y, YL) * 2 + c)


def ahead(value, steps, count):
    return lax.rem(value + (steps + count) % count, count)


def dot(a, b):
    return jnp.dot(a, b, preferred_element_type=F32)


def place_row(p):
    return (p >= 1).astype(I32) + (p >= 5).astype(I32)


def kernel(
    occ_hbm, nb_hbm, send_ref, feat_hbm, gamma_hbm, beta_hbm, og_hbm, w_hbm,
    block_ref, fgrad_ref, outb, ggrad_ref, bgrad_ref,
    occ_ref, nb_ref, feat_ref, gamma_ref, beta_ref, og_ref, tab, occn, masked, packets, ext, gath, gath_t, slabs, weight, conv_s, norm_s, cols_t,
    deep1, wide1, deep2, wide2,
    cg_s, grad_s, local_s, ghosts, returned,
    cols_sister, half_grads, own, s1, r1, s2, r2, s3, t3, r3, gathered,
    in_sem, halo_s, halo_r, d1_s, d1_r, w1_s, w1_r, d2_s, d2_r, w2_s, w2_r,
    gh_s, gh_r, cols_s, cols_r, c_s, c_r, q1_s, q1_r, q2_s, q2_r, q3_s, q3_r, a3_s, a3_r, a2_s, a2_r, a1_s, a1_r, a0_s, a0_r,
):
    z, x, y, c = coordinates()
    gx, gy = lax.axis_index("gx"), lax.axis_index("gy")
    ngx, ngy = Z * X * YH, YL * 2

    def neighbour(u, v):
        return (ahead(gx, u, ngx), ahead(gy, v, ngy))

    deep_group = [
        (device(ahead(z, dz, Z), x, y, ahead(c, dc, 2)), ahead(z, -dz, Z) * 2 + ahead(c, dc, 2))
        for dz in far_first(Z) + [0] for dc in (1, 0) if dz + dc > 0]
    wide_group = [
        (device(z, ahead(x, dx, X), ahead(y, dy, Y), c), ahead(x, -dx, X) * Y + ahead(y, -dy, Y))
        for dx, dy in sorted(
            ((dx, dy) for dx in range(X) for dy in range(Y) if dx + dy > 0),
            key=lambda step: -min(step[0], X - step[0]) - min(step[1], Y - step[1]))]

    inputs = [
        pltpu.make_async_copy(source, target, in_sem.at[i])
        for i, (source, target) in enumerate((
            (occ_hbm, occ_ref), (feat_hbm, feat_ref), (nb_hbm, nb_ref), (og_hbm, og_ref),
            (gamma_hbm, gamma_ref), (beta_hbm, beta_ref), (w_hbm, weight)))]
    inputs[0].start()
    inputs[1].start()

    barrier = pltpu.get_barrier_semaphore()
    friends = [neighbour(ROWS[d], COLUMNS[d]) for d in range(8)]
    friends += [friend for friend, _ in deep_group + wide_group]
    for friend in friends:
        pl.semaphore_signal(barrier, inc=1, device_id=friend, device_id_type=MESH)
    for copy in inputs[2:]:
        copy.start()

    sent = []

    def settle():
        for copy in sent:
            copy.wait_send()
        sent.clear()

    tab[...] = jnp.zeros_like(tab)
    inputs[0].wait()
    inputs[1].wait()
    tab[0:4, 0:64] = occ_ref[...].astype(F32)

    def pick(first, index):
        rows = [tab[first + n : first + n + 1, :] for n in range(4)]
        return jnp.where(index == 0, rows[0], jnp.where(index == 1, rows[1], jnp.where(index == 2, rows[2], rows[3])))

    def iotas(rows, lanes):
        shape = (rows, lanes)
        return lax.broadcasted_iota(I32, shape, 0), lax.broadcasted_iota(I32, shape, 1)

    ones = jnp.ones((128, 256), BF16)
    row, lane = iotas(256, 128)
    by_brick = jnp.where(lane == jnp.bitwise_and(row, 63), pick(0, jnp.right_shift(row, 6)), 0.0)
    occ_brick = dot(by_brick.astype(BF16), ones)
    feat = feat_ref[...].reshape(256, 256)
    masked_value = (feat.astype(F32) * occ_brick).astype(BF16)
    masked[...] = masked_value.reshape(4, 64, 256)
    ext[0:4] = masked_value.reshape(4, 64, 256)
    for d in range(8):
        packets[d] = masked[send_ref[0, d]]

    pl.semaphore_wait(barrier, len(friends))
    halo = []
    for d in range(8):
        copy = pltpu.make_async_remote_copy(
            src_ref=packets.at[d], dst_ref=ext.at[4 + d], send_sem=halo_s.at[d], recv_sem=halo_r.at[d],
            device_id=neighbour(ROWS[d], COLUMNS[d]), device_id_type=MESH)
        copy.start()
        halo.append(copy)

    for copy in inputs[2:6]:
        copy.wait()
    by_voxel = jnp.where(
        lane == jnp.right_shift(row, 4) * 4 + jnp.bitwise_and(row, 3),
        pick(0, jnp.bitwise_and(jnp.right_shift(row, 2), 3)), 0.0)
    occ = dot(by_voxel.astype(BF16), ones)
    occn[...] = occ
    row, lane = iotas(256, 256)
    order = jnp.bitwise_and(jnp.right_shift(row, 2), 3) * 64 + jnp.right_shift(row, 4) * 4 + jnp.bitwise_and(row, 3)
    to_rows = jnp.where(lane == order, occ, 0.0).astype(BF16)
    order = jnp.bitwise_and(jnp.right_shift(lane, 2), 3) * 64 + jnp.right_shift(lane, 4) * 4 + jnp.bitwise_and(lane, 3)
    to_bricks = jnp.where(row == order, 1.0, 0.0).astype(BF16)
    out_masked = dot(to_rows, og_ref[...].reshape(256, 256))

    tab[8:12, 0:27] = nb_ref[...].astype(F32)
    table = tab[8:16, :]
    for d in range(8):
        u, v = ROWS[d], COLUMNS[d]
        missing = jnp.int32(0)
        if u != 0:
            missing = missing + (gx == (0 if u > 0 else ngx - 1)).astype(I32)
        if v != 0:
            missing = missing + (gy == (0 if v > 0 else ngy - 1)).astype(I32)
        table = jnp.where((table == 4.0 + d) & (missing > 0), 12.0, table)
    tab[8:16, :] = table
    row, lane = iotas(576, 128)
    pq = jnp.right_shift(row, 4)
    p = jnp.right_shift(pq * 43, 8)
    q = pq - 6 * p
    brick, w = jnp.bitwise_and(jnp.right_shift(row, 2), 3), jnp.bitwise_and(row, 3)
    places = 9 * place_row(p) + 3 * place_row(q)
    voxels = 16 * jnp.bitwise_and(p + 3, 3) + 4 * jnp.bitwise_and(q + 3, 3)
    near = pick(8, brick)
    lane_f = lane.astype(F32)
    for shift in range(3):
        cell = w + shift
        found = dot(jnp.where(lane == places + place_row(cell), near, 0.0).astype(BF16), jnp.ones((128, 128), BF16))
        source = found * 64.0 + (voxels + jnp.bitwise_and(cell + 3, 3)).astype(F32)
        for j in range(6):
            gath[shift, :, j * 128 : (j + 1) * 128] = jnp.where(source == lane_f + 128.0 * j, 1.0, 0.0).astype(BF16)

    for copy in halo:
        copy.wait_recv()
    sent.extend(halo)
    extended = ext[...].reshape(768, 256)
    for shift in range(3):
        slabs[shift] = dot(gath[shift], extended).astype(BF16)

    def columns(k):
        a, b, shift = k // 9, k // 3 % 3, k % 3
        return jnp.concatenate(
            [slabs[shift, (a + i) * 96 + b * 16 : (a + i) * 96 + b * 16 + 64, :] for i in range(4)], axis=0)

    inputs[6].wait()
    conv = dot(columns(0), weight[0])
    for k in range(1, 27):
        conv = conv + dot(columns(k), weight[k])
    conv = conv * occ

    def two(value):
        return jnp.concatenate([value[:, :128], value[:, 128:]], axis=0)

    def one(tile):
        return jnp.concatenate([tile[0:1, :], tile[1:2, :]], axis=1)

    def spread(buffer, place, group, send, receive):
        copies = []
        for i, (friend, _) in enumerate(group):
            copy = pltpu.make_async_remote_copy(
                src_ref=buffer.at[place], dst_ref=buffer.at[place], send_sem=send.at[i], recv_sem=receive.at[i],
                device_id=friend, device_id_type=MESH)
            copy.start()
            copies.append(copy)
        return copies

    def meet(copies, buffer, group, send, receive):
        for i, (friend, behind) in enumerate(group):
            pltpu.make_async_remote_copy(
                src_ref=buffer.at[behind], dst_ref=buffer.at[behind], send_sem=send.at[i], recv_sem=receive.at[i],
                device_id=friend, device_id_type=MESH).wait_recv()
        sent.extend(copies)

    deep, wide = z * 2 + c, x * Y + y

    def sum_of(buffer, count):
        total = buffer[0]
        for i in range(1, count):
            total = total + buffer[i]
        return total

    def merge(buffer, count):
        tiles = [buffer[i] for i in range(count)]
        total = sum(tiles[1:], tiles[0])
        mean = total[0:2, :] / jnp.maximum(total[4:5, :], 1.0)
        square = total[2:4, :]
        for tile in tiles:
            gap = tile[0:2, :] / jnp.maximum(tile[4:5, :], 1.0) - mean
            square = square + tile[4:5, :] * gap * gap
        return total[0:2, :], square, total[4:5, :]

    def write(buffer, place, sums, squares, number):
        buffer[place] = jnp.concatenate([sums, squares, number, jnp.zeros((3, 128), F32)], axis=0)

    number = jnp.sum(occ, axis=0, keepdims=True)
    sums = jnp.sum(conv, axis=0, keepdims=True)
    centred = (conv - sums / jnp.maximum(number, 1.0)) * occ
    squares = jnp.sum(centred * centred, axis=0, keepdims=True)
    write(deep1, deep, two(sums), two(squares), number[:, :128])
    copies = spread(deep1, deep, deep_group, d1_s, d1_r)
    conv_s[...] = conv
    sister, here = device(z, x, y, 1 - c), device(z, x, y, c)

    def share_columns(first, count, i):
        for k in range(first, first + count):
            cols_t[k] = columns(k).T
        copy = pltpu.make_async_remote_copy(
            src_ref=cols_t.at[pl.ds(first, count)], dst_ref=cols_sister.at[pl.ds(first, count)],
            send_sem=cols_s.at[i], recv_sem=cols_r.at[i], device_id=sister, device_id_type=MESH)
        copy.start()
        return copy

    shared = [share_columns(0, 14, 0)]
    meet(copies, deep1, deep_group, d1_s, d1_r)
    write(wide1, wide, *merge(deep1, 2 * Z))
    copies = spread(wide1, wide, wide_group, w1_s, w1_r)
    for shift in range(2):
        gath_t[shift] = gath[shift].T
    meet(copies, wide1, wide_group, w1_s, w1_r)
    sums, squares, number = merge(wide1, X * Y)
    voxel_count = jnp.concatenate([number, number], axis=1)
    average = one(sums) / voxel_count
    inverse_std = lax.rsqrt(one(squares) / voxel_count + EPSILON)
    gamma, beta = gamma_ref[...], beta_ref[...]
    occ = occn[...]
    normalized = (conv_s[...] - average) * inverse_std
    normed = gamma * normalized + beta
    sigmoid = 1.0 / (1.0 + jnp.exp(-normed))
    act_grad = out_masked * sigmoid * (1.0 + normed * (1.0 - sigmoid))
    total = jnp.sum(act_grad, axis=0, keepdims=True)
    cross = jnp.sum(act_grad * normalized, axis=0, keepdims=True)
    write(deep2, deep, two(total), two(cross), jnp.zeros((1, 128), F32))
    copies = spread(deep2, deep, deep_group, d2_s, d2_r)
    centre = columns(13).astype(F32)
    block = (occ * (centre + normed * sigmoid)).astype(BF16)
    block_ref[...] = dot(to_bricks, block).astype(BF16).reshape(4, 64, 256)
    norm_s[...] = normalized
    shared.append(share_columns(14, 13, 1))
    meet(copies, deep2, deep_group, d2_s, d2_r)
    wide2[wide] = sum_of(deep2, 2 * Z)
    copies = spread(wide2, wide, wide_group, w2_s, w2_r)
    gath_t[2] = gath[2].T
    meet(copies, wide2, wide_group, w2_s, w2_r)
    tiles = sum_of(wide2, X * Y)
    total, cross = one(tiles[0:2]), one(tiles[2:4])
    inverse_root = lax.rsqrt(voxel_count)
    ggrad_ref[...] = cross * inverse_root
    bgrad_ref[...] = total * inverse_root
    conv_grad = (gamma * inverse_std * (act_grad - total / voxel_count - norm_s[...] * cross / voxel_count) * occ).astype(BF16)
    cg_s[...] = conv_grad

    half_grads[0] = jnp.where(c == 0, conv_grad[:, :128].astype(F32), conv_grad[:, 128:].astype(F32)).astype(BF16)
    half_grads[1] = jnp.where(c == 0, conv_grad[:, 128:].astype(F32), conv_grad[:, :128].astype(F32)).astype(BF16)
    shared.append(pltpu.make_async_remote_copy(
        src_ref=half_grads.at[1], dst_ref=half_grads.at[2], send_sem=c_s, recv_sem=c_r,
        device_id=sister, device_id_type=MESH))
    shared[2].start()
    small = 256 // (X * Y)
    half = pl.ds(pl.multiple_of(c * 128, 128), 128)
    other_half = pl.ds(pl.multiple_of((1 - c) * 128, 128), 128)
    depth = 16 // Z

    def axes(part):
        return ((y, Y), (x, X)) if part else ((x, X), (y, Y))

    def mate(part, stage, step):
        if part == stage - 1:
            return device(z, ahead(x, step, X), y, c)
        return device(z, x, ahead(y, step, Y), c)

    def span(start, size):
        return pl.ds(pl.multiple_of(start, 16), size)

    def remote(source, target, send, receive, to):
        return pltpu.make_async_remote_copy(
            src_ref=source, dst_ref=target, send_sem=send, recv_sem=receive, device_id=to, device_id_type=MESH)

    going = {}

    def arrive(stage, piece):
        for copy in going.pop((stage, piece)):
            copy.wait_recv()
            sent.append(copy)

    def heard(stage, piece):
        for copy in going.pop((stage, piece)):
            copy.wait_recv()

    def products(piece):
        first, count, _ = PIECES[piece]
        for k in range(first, first + count):
            own[k] = dot(cols_t[k], half_grads[0])

    def hear_sister():
        for copy in shared:
            copy.wait_recv()
            sent.append(copy)

    def stage1(piece):
        first, count, part = PIECES[piece]
        (place, length), _ = axes(part)
        rows = 256 // length
        for k in range(first, first + count):
            value = own[k] + dot(cols_sister[k], half_grads[2])
            own[k] = value
            s1[k] = value.astype(BF16)
        for step in far_first(length):
            copy = remote(
                s1.at[pl.ds(first, count), span(ahead(place, step, length) * rows, rows)],
                r1.at[step - 1, pl.ds(first, count)],
                q1_s.at[piece, step - 1], q1_r.at[piece, step - 1], mate(part, 1, step))
            copy.start()
            going.setdefault(("one", part), []).append(copy)

    def stage2(part):
        first, count = PARTS[part]
        (place, length), (place2, length2) = axes(part)
        rows = 256 // length
        arrive("one", part)
        for k in range(first, first + count):
            value = own[k, span(place * rows, rows), :]
            for step in range(1, length):
                value = value + r1[step - 1, k].astype(F32)
            own[k, 0:rows, :] = value
            s2[k] = value.astype(BF16)
        going["two", part] = []
        for step in far_first(length2):
            copy = remote(
                s2.at[pl.ds(first, count), span(ahead(place2, step, length2) * small, small)],
                r2.at[step - 1, pl.ds(first, count)],
                q2_s.at[part, step - 1], q2_r.at[part, step - 1], mate(part, 2, step))
            copy.start()
            going["two", part].append(copy)

    def stage3():
        for part, (first, count) in enumerate(PARTS):
            _, (place2, length2) = axes(part)
            arrive("two", part)
            for k in range(16):
                if k < count:
                    value = own[first + k, span(place2 * small, small), :]
                    for step in range(1, length2):
                        value = value + r2[step - 1, first + k].astype(F32)
                else:
                    value = jnp.zeros((small, 128), F32)
                t3[k, part] = value
                s3[k, part] = value.astype(BF16)
        going["three", 0] = []
        for dz in far_first(Z):
            copy = remote(
                s3.at[pl.ds(ahead(z, dz, Z) * depth, depth)], r3.at[dz - 1],
                q3_s.at[dz - 1], q3_r.at[dz - 1], device(ahead(z, dz, Z), x, y, c))
            copy.start()
            going["three", 0].append(copy)

    def fine(part):
        (place, length), (place2, _) = axes(part)
        return span(place * (256 // length) + place2 * small, small)

    def push(where, send, receive, to):
        return remote(outb.at[where], outb.at[where], send, receive, to)

    def back3():
        arrive("three", 0)
        mine = pl.ds(z * depth, depth)
        value = t3[mine]
        for dz in range(1, Z):
            value = value + r3[dz - 1].astype(F32)
        gathered[mine] = (value * inverse_root[:, :128].reshape(1, 1, 1, 128)).astype(BF16)
        going["back3", 0] = []
        for dz in far_first(Z):
            copy = remote(gathered.at[mine], gathered.at[mine], a3_s.at[dz - 1], a3_r.at[dz - 1],
                          device(ahead(z, dz, Z), x, y, c))
            copy.start()
            sent.append(copy)
            behind = gathered.at[pl.ds(ahead(z, -dz, Z) * depth, depth)]
            going["back3", 0].append(remote(behind, behind, a3_s.at[dz - 1], a3_r.at[dz - 1], here))

    def back2():
        heard("back3", 0)
        for part, (_, count) in enumerate(PARTS):
            (place, length), (place2, length2) = axes(part)
            going["back2", part] = []
            for step in far_first(length2):
                copy = remote(gathered.at[pl.ds(0, count), part], outb.at[pl.ds(part * 16, count), fine(part), half],
                              a2_s.at[part, step - 1], a2_r.at[part, step - 1], mate(part, 2, step))
                copy.start()
                sent.append(copy)
                start = place * (256 // length) + ahead(place2, -step, length2) * small
                going["back2", part].append(push(
                    (pl.ds(part * 16, count), span(start, small), half), a2_s.at[part, step - 1],
                    a2_r.at[part, step - 1], here))
        for part, (_, count) in enumerate(PARTS):
            outb[pl.ds(part * 16, count), fine(part), half] = gathered[0:count, part]

    def strip(part, step, lanes):
        (place, length), _ = axes(part)
        rows = 256 // length
        return pl.ds(part * 16, PARTS[part][1]), span(ahead(place, -step, length) * rows, rows), lanes

    def hand_over(part, step):
        copy = push(strip(part, step, half), a0_s.at[part, step], a0_r.at[part, step], sister)
        copy.start()
        sent.append(copy)

    def back1(part):
        _, length = axes(part)[0]
        heard("back2", part)
        for step in far_first(length):
            copy = push(strip(part, 0, half), a1_s.at[part, step - 1], a1_r.at[part, step - 1], mate(part, 1, step))
            copy.start()
            sent.append(copy)
        hand_over(part, 0)

    def back0():
        for step in (1, 3, 2):
            for part in range(2):
                if step < axes(part)[0][1]:
                    push(strip(part, step, half), a1_s.at[part, step - 1], a1_r.at[part, step - 1], here).wait_recv()
                    hand_over(part, step)

    def finish():
        for step in (0, 1, 3, 2):
            for part in range(2):
                if step < axes(part)[0][1]:
                    push(strip(part, step, other_half), a0_s.at[part, step], a0_r.at[part, step], here).wait_recv()

    def column_grads():
        grad_s[...] = jnp.zeros_like(grad_s)
        for k in range(27):
            a, b, shift = k // 9, k // 3 % 3, k % 3
            product = lax.dot_general(cg_s[...], weight[k], (((1,), (1,)), ((), ())), preferred_element_type=F32)
            for i in range(4):
                start = (a + i) * 96 + b * 16
                grad_s[shift, start : start + 64, :] += product[i * 64 : (i + 1) * 64, :]

    def brick_grads():
        result = None
        for shift in range(3):
            value = grad_s[shift]
            high = value.astype(BF16)
            low = (value - high.astype(F32)).astype(BF16)
            term = dot(gath_t[shift], jnp.concatenate([high, low], axis=1))
            result = term if result is None else result + term
        result = result[:, :256] + result[:, 256:]
        local_s[...] = result[:256]
        ghosts[...] = result[256:].astype(BF16).reshape(8, 64, 256)
        going["ghosts", 0] = []
        for d in range(8):
            copy = remote(ghosts.at[d], returned.at[d], gh_s.at[d], gh_r.at[d], neighbour(-ROWS[d], -COLUMNS[d]))
            copy.start()
            going["ghosts", 0].append(copy)

    def feature_grads():
        out_bricks = dot(to_bricks, out_masked.astype(BF16))
        arrive("ghosts", 0)
        for b in range(4):
            rows = slice(b * 64, (b + 1) * 64)
            extra = out_bricks[rows] + local_s[rows, :]
            for d in range(8):
                extra = extra + jnp.where(send_ref[0, d] == b, returned[d].astype(F32), 0.0)
            fgrad_ref[b] = (extra * occ_brick[rows]).astype(BF16)

    schedule = (
        (products, 0), (products, 1), (hear_sister,),
        (stage1, 0), (stage1, 1),
        (products, 2), (products, 3), (stage1, 2), (stage1, 3),
        (column_grads,), (settle,),
        (stage2, 0), (stage2, 1), (stage3,),
        (brick_grads,), (back3,),
        (feature_grads,),
        (back2,),
        (back1, 0), (back1, 1),
        (settle,),
        (back0,), (finish,), (settle,),
    )
    for step, *piece in schedule:
        step(*piece)


def write_out(block, fgrad, wgrad, ggrad, bgrad, block_out, fgrad_out, wgrad_out, ggrad_out, bgrad_out, sems):
    pairs = [(block, block_out), (fgrad, fgrad_out), (ggrad, ggrad_out), (bgrad, bgrad_out)]
    for part, (first, count) in enumerate(PARTS):
        pairs.append((wgrad.at[pl.ds(part * 16, count)], wgrad_out.at[pl.ds(first, count)]))
    copies = [pltpu.make_async_copy(source, target, sems.at[i]) for i, (source, target) in enumerate(pairs)]
    for copy in copies:
        copy.start()
    for copy in copies:
        copy.wait()


def on_device(features, occupancy, neighbours, send_list, weight, gamma, beta, out_grad):
    vmem = pl.BlockSpec(memory_space=pltpu.VMEM)
    small = 256 // (X * Y)
    near, far = max(X, Y) - 1, Z - 1
    depth = 16 // Z
    pieces = len(PIECES)
    dma = pltpu.SemaphoreType.DMA
    scratch = [
        pltpu.VMEM((4, 64), I32),
        pltpu.VMEM((4, 27), I32),
        pltpu.VMEM((4, 64, 256), BF16),
        pltpu.VMEM((1, 256), F32),
        pltpu.VMEM((1, 256), F32),
        pltpu.VMEM((4, 64, 256), BF16),
        pltpu.VMEM((16, 128), F32),
        pltpu.VMEM((256, 256), F32),
        pltpu.VMEM((4, 64, 256), BF16),
        pltpu.VMEM((8, 64, 256), BF16),
        pltpu.VMEM((12, 64, 256), BF16),
        pltpu.VMEM((3, 576, 768), BF16),
        pltpu.VMEM((3, 768, 576), BF16),
        pltpu.VMEM((3, 576, 256), BF16),
        pltpu.VMEM((27, 256, 256), BF16),
        pltpu.VMEM((256, 256), F32),
        pltpu.VMEM((256, 256), F32),
        pltpu.VMEM((27, 256, 256), BF16),
        pltpu.VMEM((2 * Z, 8, 128), F32),
        pltpu.VMEM((X * Y, 8, 128), F32),
        pltpu.VMEM((2 * Z, 8, 128), F32),
        pltpu.VMEM((X * Y, 8, 128), F32),
        pltpu.VMEM((256, 256), BF16),
        pltpu.VMEM((3, 576, 256), F32),
        pltpu.VMEM((256, 256), F32),
        pltpu.VMEM((8, 64, 256), BF16),
        pltpu.VMEM((8, 64, 256), BF16),
        pltpu.VMEM((27, 256, 256), BF16),
        pltpu.VMEM((3, 256, 128), BF16),
        pltpu.VMEM((27, 256, 128), F32),
        pltpu.VMEM((27, 256, 128), BF16),
        pltpu.VMEM((near, 27, 256 // min(X, Y), 128), BF16),
        pltpu.VMEM((27, 256 // min(X, Y), 128), BF16),
        pltpu.VMEM((near, 27, small, 128), BF16),
        pltpu.VMEM((16, 2, small, 128), BF16),
        pltpu.VMEM((16, 2, small, 128), F32),
        pltpu.VMEM((far, depth, 2, small, 128), BF16),
        pltpu.VMEM((16, 2, small, 128), BF16),
        dma((7,)), dma((8,)), dma((8,)),
        dma((2 * Z - 1,)), dma((2 * Z - 1,)), dma((X * Y - 1,)), dma((X * Y - 1,)),
        dma((2 * Z - 1,)), dma((2 * Z - 1,)), dma((X * Y - 1,)), dma((X * Y - 1,)),
        dma((8,)), dma((8,)), dma((2,)), dma((2,)), dma, dma,
        dma((pieces, near)), dma((pieces, near)), dma((2, near)), dma((2, near)), dma((far,)), dma((far,)),
        dma((far,)), dma((far,)), dma((2, near)), dma((2, near)),
        dma((2, near)), dma((2, near)), dma((2, near + 1)), dma((2, near + 1)),
    ]
    anywhere = pl.BlockSpec(memory_space=pl.ANY)
    results = pl.pallas_call(
        kernel,
        name="brick_block",
        out_shape=(
            pltpu.VMEM((4, 64, 256), BF16),
            pltpu.VMEM((4, 64, 256), BF16),
            pltpu.VMEM((32, 256, 256), BF16),
            pltpu.VMEM((1, 256), F32),
            pltpu.VMEM((1, 256), F32),
        ),
        in_specs=[anywhere, anywhere, pl.BlockSpec(memory_space=pltpu.SMEM)] + [anywhere] * 5,
        out_specs=(vmem, vmem, vmem, vmem, vmem),
        scratch_shapes=scratch,
        compiler_params=pltpu.CompilerParams(
            collective_id=0, has_side_effects=True, vmem_limit_bytes=56 * 2**20),
    )(occupancy, neighbours, send_list.reshape(1, 8), features, gamma.reshape(1, 256), beta.reshape(1, 256), out_grad, weight)
    block, fgrad, wgrad, ggrad, bgrad = pl.pallas_call(
        write_out,
        name="write_out",
        out_shape=(
            jax.ShapeDtypeStruct((4, 64, 256), BF16),
            jax.ShapeDtypeStruct((4, 64, 256), BF16),
            jax.ShapeDtypeStruct((27, 256, 256), BF16),
            jax.ShapeDtypeStruct((1, 256), F32),
            jax.ShapeDtypeStruct((1, 256), F32),
        ),
        in_specs=[anywhere] * 5,
        out_specs=(anywhere,) * 5,
        scratch_shapes=[dma((6,))],
        compiler_params=pltpu.CompilerParams(vmem_limit_bytes=8 * 2**20),
    )(*results)
    return block, fgrad, wgrad, ggrad.reshape(256), bgrad.reshape(256)


def solution(mesh):
    placed = (
        P(("gx", "gy"), None, None),
        P(("gx", "gy"), None),
        P(("gx", "gy"), None),
        P(("gx", "gy"), None, None),
        P(),
        P(),
        P(),
        P(("gx", "gy"), None, None),
    )
    return jax.shard_map(
        on_device,
        mesh=mesh,
        in_specs=placed,
        out_specs=(P(("gx", "gy"), None, None), P(("gx", "gy"), None, None), P(), P(), P()),
        check_vma=False,
    )
```

```python
import functools

import jax
import jax.numpy as jnp
from jax import lax
from jax.experimental import pallas as pl
from jax.experimental.pallas import tpu as pltpu
from jax.sharding import PartitionSpec as P

Z, X, YH, YL = 8, 4, 2, 2
Y = YH * YL

ROWS = (-1, -1, -1, 0, 0, 1, 1, 1)
COLUMNS = (-1, 0, 1, -1, 1, -1, 0, 1)
EPSILON = 1e-05
MESH = pl.DeviceIdType.MESH
F32, BF16, I32 = jnp.float32, jnp.bfloat16, jnp.int32

PARTS = ((0, 11), (11, 11))
PIECES = ((0, 5, 0), (11, 5, 1), (5, 6, 0), (16, 6, 1))
THIRD = (22, 5)


def slots():
    return -(-THIRD[0] // Z) * Z


def far_first(count):
    return sorted(range(1, count), key=lambda step: -min(step, count - step))


def coordinates():
    gx, gy = lax.axis_index("gx"), lax.axis_index("gy")
    z = lax.div(gx, X * YH)
    x = lax.rem(lax.div(gx, YH), X)
    y = lax.rem(gx, YH) * YL + lax.div(gy, 2)
    return z, x, y, lax.rem(gy, 2)


def device(z, x, y, c):
    return (z * (X * YH) + x * YH + lax.div(y, YL), lax.rem(y, YL) * 2 + c)


def ahead(value, steps, count):
    return lax.rem(value + (steps + count) % count, count)


def dot(a, b):
    return jnp.dot(a, b, preferred_element_type=F32)


def place_row(p):
    return (p >= 1).astype(I32) + (p >= 5).astype(I32)


def kernel(
    occ_hbm, nb_hbm, send_ref, feat_hbm, gamma_hbm, beta_hbm, og_hbm, w_hbm,
    block_ref, fgrad_ref, outb, ggrad_ref, bgrad_ref,
    occ_ref, nb_ref, feat_ref, gamma_ref, beta_ref, og_ref, tab, occn, masked, packets, ext, gath, gath_t, slabs, weight, conv_s, norm_s, cols_t,
    deep1, wide1, deep2, wide2,
    cg_s, grad_s, local_s, ghosts, returned,
    cols_sister, half_grads, own, s1, r1, s2, r2, s3, t3, r3, gathered, rz, own2z, s2z, r2z, own3z, s3z, r3z,
    in_sem, halo_s, halo_r, d1_s, d1_r, w1_s, w1_r, d2_s, d2_r, w2_s, w2_r,
    gh_s, gh_r, cols_s, cols_r, c_s, c_r, q1_s, q1_r, q2_s, q2_r, q3_s, q3_r, a3_s, a3_r, a2_s, a2_r, a1_s, a1_r, a0_s, a0_r,
    z1_s, z1_r, z2_s, z2_r, z3_s, z3_r, b3_s, b3_r, b2_s, b2_r, b1_s, b1_r, b0_s, b0_r,
):
    z, x, y, c = coordinates()
    gx, gy = lax.axis_index("gx"), lax.axis_index("gy")
    ngx, ngy = Z * X * YH, YL * 2

    def neighbour(u, v):
        return (ahead(gx, u, ngx), ahead(gy, v, ngy))

    deep_group = [
        (device(ahead(z, dz, Z), x, y, ahead(c, dc, 2)), ahead(z, -dz, Z) * 2 + ahead(c, dc, 2))
        for dz in far_first(Z) + [0] for dc in (1, 0) if dz + dc > 0]
    wide_group = [
        (device(z, ahead(x, dx, X), ahead(y, dy, Y), c), ahead(x, -dx, X) * Y + ahead(y, -dy, Y))
        for dx, dy in sorted(
            ((dx, dy) for dx in range(X) for dy in range(Y) if dx + dy > 0),
            key=lambda step: -min(step[0], X - step[0]) - min(step[1], Y - step[1]))]

    inputs = [
        pltpu.make_async_copy(source, target, in_sem.at[i])
        for i, (source, target) in enumerate((
            (occ_hbm, occ_ref), (feat_hbm, feat_ref), (nb_hbm, nb_ref), (og_hbm, og_ref),
            (gamma_hbm, gamma_ref), (beta_hbm, beta_ref), (w_hbm, weight)))]
    inputs[0].start()
    inputs[1].start()

    barrier = pltpu.get_barrier_semaphore()
    friends = [neighbour(ROWS[d], COLUMNS[d]) for d in range(8)]
    friends += [friend for friend, _ in deep_group + wide_group]
    for friend in friends:
        pl.semaphore_signal(barrier, inc=1, device_id=friend, device_id_type=MESH)
    for copy in inputs[2:]:
        copy.start()

    sent = []

    def settle():
        for copy in sent:
            copy.wait_send()
        sent.clear()

    tab[...] = jnp.zeros_like(tab)
    inputs[0].wait()
    inputs[1].wait()
    tab[0:4, 0:64] = occ_ref[...].astype(F32)

    def pick(first, index):
        rows = [tab[first + n : first + n + 1, :] for n in range(4)]
        return jnp.where(index == 0, rows[0], jnp.where(index == 1, rows[1], jnp.where(index == 2, rows[2], rows[3])))

    def iotas(rows, lanes):
        shape = (rows, lanes)
        return lax.broadcasted_iota(I32, shape, 0), lax.broadcasted_iota(I32, shape, 1)

    ones = jnp.ones((128, 256), BF16)
    row, lane = iotas(256, 128)
    by_brick = jnp.where(lane == jnp.bitwise_and(row, 63), pick(0, jnp.right_shift(row, 6)), 0.0)
    occ_brick = dot(by_brick.astype(BF16), ones)
    feat = feat_ref[...].reshape(256, 256)
    masked_value = (feat.astype(F32) * occ_brick).astype(BF16)
    masked[...] = masked_value.reshape(4, 64, 256)
    ext[0:4] = masked_value.reshape(4, 64, 256)
    for d in range(8):
        packets[d] = masked[send_ref[0, d]]

    pl.semaphore_wait(barrier, len(friends))
    halo = []
    for d in range(8):
        copy = pltpu.make_async_remote_copy(
            src_ref=packets.at[d], dst_ref=ext.at[4 + d], send_sem=halo_s.at[d], recv_sem=halo_r.at[d],
            device_id=neighbour(ROWS[d], COLUMNS[d]), device_id_type=MESH)
        copy.start()
        halo.append(copy)

    for copy in inputs[2:6]:
        copy.wait()
    by_voxel = jnp.where(
        lane == jnp.right_shift(row, 4) * 4 + jnp.bitwise_and(row, 3),
        pick(0, jnp.bitwise_and(jnp.right_shift(row, 2), 3)), 0.0)
    occ = dot(by_voxel.astype(BF16), ones)
    occn[...] = occ
    row, lane = iotas(256, 256)
    order = jnp.bitwise_and(jnp.right_shift(row, 2), 3) * 64 + jnp.right_shift(row, 4) * 4 + jnp.bitwise_and(row, 3)
    to_rows = jnp.where(lane == order, occ, 0.0).astype(BF16)
    order = jnp.bitwise_and(jnp.right_shift(lane, 2), 3) * 64 + jnp.right_shift(lane, 4) * 4 + jnp.bitwise_and(lane, 3)
    to_bricks = jnp.where(row == order, 1.0, 0.0).astype(BF16)
    out_masked = dot(to_rows, og_ref[...].reshape(256, 256))

    tab[8:12, 0:27] = nb_ref[...].astype(F32)
    table = tab[8:16, :]
    for d in range(8):
        u, v = ROWS[d], COLUMNS[d]
        missing = jnp.int32(0)
        if u != 0:
            missing = missing + (gx == (0 if u > 0 else ngx - 1)).astype(I32)
        if v != 0:
            missing = missing + (gy == (0 if v > 0 else ngy - 1)).astype(I32)
        table = jnp.where((table == 4.0 + d) & (missing > 0), 12.0, table)
    tab[8:16, :] = table
    row, lane = iotas(576, 128)
    pq = jnp.right_shift(row, 4)
    p = jnp.right_shift(pq * 43, 8)
    q = pq - 6 * p
    brick, w = jnp.bitwise_and(jnp.right_shift(row, 2), 3), jnp.bitwise_and(row, 3)
    places = 9 * place_row(p) + 3 * place_row(q)
    voxels = 16 * jnp.bitwise_and(p + 3, 3) + 4 * jnp.bitwise_and(q + 3, 3)
    near = pick(8, brick)
    lane_f = lane.astype(F32)
    for shift in range(3):
        cell = w + shift
        found = dot(jnp.where(lane == places + place_row(cell), near, 0.0).astype(BF16), jnp.ones((128, 128), BF16))
        source = found * 64.0 + (voxels + jnp.bitwise_and(cell + 3, 3)).astype(F32)
        for j in range(6):
            gath[shift, :, j * 128 : (j + 1) * 128] = jnp.where(source == lane_f + 128.0 * j, 1.0, 0.0).astype(BF16)

    for copy in halo:
        copy.wait_recv()
    sent.extend(halo)
    extended = ext[...].reshape(768, 256)
    for shift in range(3):
        slabs[shift] = dot(gath[shift], extended).astype(BF16)

    def columns(k):
        a, b, shift = k // 9, k // 3 % 3, k % 3
        return jnp.concatenate(
            [slabs[shift, (a + i) * 96 + b * 16 : (a + i) * 96 + b * 16 + 64, :] for i in range(4)], axis=0)

    inputs[6].wait()
    conv = dot(columns(0), weight[0])
    for k in range(1, 27):
        conv = conv + dot(columns(k), weight[k])
    conv = conv * occ

    def two(value):
        return jnp.concatenate([value[:, :128], value[:, 128:]], axis=0)

    def one(tile):
        return jnp.concatenate([tile[0:1, :], tile[1:2, :]], axis=1)

    def spread(buffer, place, group, send, receive):
        copies = []
        for i, (friend, _) in enumerate(group):
            copy = pltpu.make_async_remote_copy(
                src_ref=buffer.at[place], dst_ref=buffer.at[place], send_sem=send.at[i], recv_sem=receive.at[i],
                device_id=friend, device_id_type=MESH)
            copy.start()
            copies.append(copy)
        return copies

    def meet(copies, buffer, group, send, receive):
        for i, (friend, behind) in enumerate(group):
            pltpu.make_async_remote_copy(
                src_ref=buffer.at[behind], dst_ref=buffer.at[behind], send_sem=send.at[i], recv_sem=receive.at[i],
                device_id=friend, device_id_type=MESH).wait_recv()
        sent.extend(copies)

    deep, wide = z * 2 + c, x * Y + y

    def sum_of(buffer, count):
        total = buffer[0]
        for i in range(1, count):
            total = total + buffer[i]
        return total

    def merge(buffer, count):
        tiles = [buffer[i] for i in range(count)]
        total = sum(tiles[1:], tiles[0])
        mean = total[0:2, :] / jnp.maximum(total[4:5, :], 1.0)
        square = total[2:4, :]
        for tile in tiles:
            gap = tile[0:2, :] / jnp.maximum(tile[4:5, :], 1.0) - mean
            square = square + tile[4:5, :] * gap * gap
        return total[0:2, :], square, total[4:5, :]

    def write(buffer, place, sums, squares, number):
        buffer[place] = jnp.concatenate([sums, squares, number, jnp.zeros((3, 128), F32)], axis=0)

    number = jnp.sum(occ, axis=0, keepdims=True)
    sums = jnp.sum(conv, axis=0, keepdims=True)
    centred = (conv - sums / jnp.maximum(number, 1.0)) * occ
    squares = jnp.sum(centred * centred, axis=0, keepdims=True)
    write(deep1, deep, two(sums), two(squares), number[:, :128])
    copies = spread(deep1, deep, deep_group, d1_s, d1_r)
    conv_s[...] = conv
    sister, here = device(z, x, y, 1 - c), device(z, x, y, c)

    def share_columns(first, count, i):
        for k in range(first, first + count):
            cols_t[k] = columns(k).T
        copy = pltpu.make_async_remote_copy(
            src_ref=cols_t.at[pl.ds(first, count)], dst_ref=cols_sister.at[pl.ds(first, count)],
            send_sem=cols_s.at[i], recv_sem=cols_r.at[i], device_id=sister, device_id_type=MESH)
        copy.start()
        return copy

    shared = [share_columns(0, 14, 0)]
    meet(copies, deep1, deep_group, d1_s, d1_r)
    write(wide1, wide, *merge(deep1, 2 * Z))
    copies = spread(wide1, wide, wide_group, w1_s, w1_r)
    for shift in range(2):
        gath_t[shift] = gath[shift].T
    meet(copies, wide1, wide_group, w1_s, w1_r)
    sums, squares, number = merge(wide1, X * Y)
    voxel_count = jnp.concatenate([number, number], axis=1)
    average = one(sums) / voxel_count
    inverse_std = lax.rsqrt(one(squares) / voxel_count + EPSILON)
    gamma, beta = gamma_ref[...], beta_ref[...]
    occ = occn[...]
    normalized = (conv_s[...] - average) * inverse_std
    normed = gamma * normalized + beta
    sigmoid = 1.0 / (1.0 + jnp.exp(-normed))
    act_grad = out_masked * sigmoid * (1.0 + normed * (1.0 - sigmoid))
    total = jnp.sum(act_grad, axis=0, keepdims=True)
    cross = jnp.sum(act_grad * normalized, axis=0, keepdims=True)
    write(deep2, deep, two(total), two(cross), jnp.zeros((1, 128), F32))
    copies = spread(deep2, deep, deep_group, d2_s, d2_r)
    centre = columns(13).astype(F32)
    block = (occ * (centre + normed * sigmoid)).astype(BF16)
    block_ref[...] = dot(to_bricks, block).astype(BF16).reshape(4, 64, 256)
    norm_s[...] = normalized
    shared.append(share_columns(14, 13, 1))
    meet(copies, deep2, deep_group, d2_s, d2_r)
    wide2[wide] = sum_of(deep2, 2 * Z)
    copies = spread(wide2, wide, wide_group, w2_s, w2_r)
    gath_t[2] = gath[2].T
    meet(copies, wide2, wide_group, w2_s, w2_r)
    tiles = sum_of(wide2, X * Y)
    total, cross = one(tiles[0:2]), one(tiles[2:4])
    inverse_root = lax.rsqrt(voxel_count)
    ggrad_ref[...] = cross * inverse_root
    bgrad_ref[...] = total * inverse_root
    conv_grad = (gamma * inverse_std * (act_grad - total / voxel_count - norm_s[...] * cross / voxel_count) * occ).astype(BF16)
    cg_s[...] = conv_grad

    half_grads[0] = jnp.where(c == 0, conv_grad[:, :128].astype(F32), conv_grad[:, 128:].astype(F32)).astype(BF16)
    half_grads[1] = jnp.where(c == 0, conv_grad[:, 128:].astype(F32), conv_grad[:, :128].astype(F32)).astype(BF16)
    shared.append(pltpu.make_async_remote_copy(
        src_ref=half_grads.at[1], dst_ref=half_grads.at[2], send_sem=c_s, recv_sem=c_r,
        device_id=sister, device_id_type=MESH))
    shared[2].start()
    small = 256 // (X * Y)
    half = pl.ds(pl.multiple_of(c * 128, 128), 128)
    other_half = pl.ds(pl.multiple_of((1 - c) * 128, 128), 128)
    depth = slots() // Z
    first_z, count_z = THIRD
    owners = [i * Z // count_z for i in range(count_z)]
    slot = sum(i * (z == owner).astype(I32) for i, owner in enumerate(owners))
    is_owner = sum((z == owner).astype(I32) for owner in owners) > 0

    def axes(part):
        return ((y, Y), (x, X)) if part else ((x, X), (y, Y))

    def mate(part, stage, step):
        if part == stage - 1:
            return device(z, ahead(x, step, X), y, c)
        return device(z, x, ahead(y, step, Y), c)

    def span(start, size):
        return pl.ds(pl.multiple_of(start, 16), size)

    def remote(source, target, send, receive, to):
        return pltpu.make_async_remote_copy(
            src_ref=source, dst_ref=target, send_sem=send, recv_sem=receive, device_id=to, device_id_type=MESH)

    going = {}

    def arrive(stage, piece):
        for copy in going.pop((stage, piece)):
            copy.wait_recv()
            sent.append(copy)

    def heard(stage, piece):
        for copy in going.pop((stage, piece)):
            copy.wait_recv()

    def products(piece):
        first, count, _ = PIECES[piece]
        for k in range(first, first + count):
            own[k] = dot(cols_t[k], half_grads[0])

    def hear_sister():
        for copy in shared:
            copy.wait_recv()
            sent.append(copy)

    def stage1(piece):
        first, count, part = PIECES[piece]
        (place, length), _ = axes(part)
        rows = 256 // length
        for k in range(first, first + count):
            value = own[k] + dot(cols_sister[k], half_grads[2])
            own[k] = value
            s1[k] = value.astype(BF16)
        for step in far_first(length):
            copy = remote(
                s1.at[pl.ds(first, count), span(ahead(place, step, length) * rows, rows)],
                r1.at[step - 1, pl.ds(first, count)],
                q1_s.at[piece, step - 1], q1_r.at[piece, step - 1], mate(part, 1, step))
            copy.start()
            going.setdefault(("one", part), []).append(copy)

    def stage2(part):
        first, count = PARTS[part]
        (place, length), (place2, length2) = axes(part)
        rows = 256 // length
        arrive("one", part)
        for k in range(first, first + count):
            value = own[k, span(place * rows, rows), :]
            for step in range(1, length):
                value = value + r1[step - 1, k].astype(F32)
            own[k, 0:rows, :] = value
            s2[k] = value.astype(BF16)
        going["two", part] = []
        for step in far_first(length2):
            copy = remote(
                s2.at[pl.ds(first, count), span(ahead(place2, step, length2) * small, small)],
                r2.at[step - 1, pl.ds(first, count)],
                q2_s.at[part, step - 1], q2_r.at[part, step - 1], mate(part, 2, step))
            copy.start()
            going["two", part].append(copy)

    def stage3():
        for part, (first, count) in enumerate(PARTS):
            _, (place2, length2) = axes(part)
            arrive("two", part)
            for k in range(first, first + count):
                value = own[k, span(place2 * small, small), :]
                for step in range(1, length2):
                    value = value + r2[step - 1, k].astype(F32)
                t3[k] = value
                s3[k] = value.astype(BF16)
        for k in range(first_z, slots()):
            t3[k] = jnp.zeros((small, 128), F32)
            s3[k] = jnp.zeros((small, 128), BF16)
        going["three", 0] = []
        for dz in far_first(Z):
            copy = remote(
                s3.at[pl.ds(ahead(z, dz, Z) * depth, depth)], r3.at[dz - 1],
                q3_s.at[dz - 1], q3_r.at[dz - 1], device(ahead(z, dz, Z), x, y, c))
            copy.start()
            going["three", 0].append(copy)

    def fine(part):
        (place, length), (place2, _) = axes(part)
        return span(place * (256 // length) + place2 * small, small)

    def push(where, send, receive, to):
        return remote(outb.at[where], outb.at[where], send, receive, to)

    def back3():
        arrive("three", 0)
        mine = pl.ds(z * depth, depth)
        value = t3[mine]
        for dz in range(1, Z):
            value = value + r3[dz - 1].astype(F32)
        gathered[mine] = (value * inverse_root[:, :128].reshape(1, 1, 128)).astype(BF16)
        going["back3", 0] = []
        for dz in far_first(Z):
            copy = remote(gathered.at[mine], gathered.at[mine], a3_s.at[dz - 1], a3_r.at[dz - 1],
                          device(ahead(z, dz, Z), x, y, c))
            copy.start()
            sent.append(copy)
            behind = gathered.at[pl.ds(ahead(z, -dz, Z) * depth, depth)]
            going["back3", 0].append(remote(behind, behind, a3_s.at[dz - 1], a3_r.at[dz - 1], here))

    def back2():
        heard("back3", 0)
        for part, (first, count) in enumerate(PARTS):
            (place, length), (place2, length2) = axes(part)
            going["back2", part] = []
            for step in far_first(length2):
                copy = remote(gathered.at[pl.ds(first, count)], outb.at[pl.ds(first, count), fine(part), half],
                              a2_s.at[part, step - 1], a2_r.at[part, step - 1], mate(part, 2, step))
                copy.start()
                sent.append(copy)
                start = place * (256 // length) + ahead(place2, -step, length2) * small
                going["back2", part].append(push(
                    (pl.ds(first, count), span(start, small), half), a2_s.at[part, step - 1],
                    a2_r.at[part, step - 1], here))
        for part, (first, count) in enumerate(PARTS):
            outb[pl.ds(first, count), fine(part), half] = gathered[first : first + count]

    def strip(part, step, lanes):
        (place, length), _ = axes(part)
        rows = 256 // length
        return pl.ds(*PARTS[part]), span(ahead(place, -step, length) * rows, rows), lanes

    def hand_over(part, step):
        copy = push(strip(part, step, half), a0_s.at[part, step], a0_r.at[part, step], sister)
        copy.start()
        sent.append(copy)

    def back1(part):
        _, length = axes(part)[0]
        heard("back2", part)
        for step in far_first(length):
            copy = push(strip(part, 0, half), a1_s.at[part, step - 1], a1_r.at[part, step - 1], mate(part, 1, step))
            copy.start()
            sent.append(copy)
        hand_over(part, 0)

    def back0():
        for step in (1, 3, 2):
            for part in range(2):
                if step < axes(part)[0][1]:
                    push(strip(part, step, half), a1_s.at[part, step - 1], a1_r.at[part, step - 1], here).wait_recv()
                    hand_over(part, step)

    def finish():
        for step in (0, 1, 3, 2):
            for part in range(2):
                if step < axes(part)[0][1]:
                    push(strip(part, step, other_half), a0_s.at[part, step], a0_r.at[part, step], here).wait_recv()

    rows_x, mine_z = 256 // X, first_z + slot

    def toward(i):
        steps = lax.rem(owners[i] + Z - z, Z)
        place = jnp.maximum(steps - 1, 0)
        return remote(s1.at[first_z + i], rz.at[place], z1_s.at[i], z1_r.at[place], device(jnp.int32(owners[i]), x, y, c))

    def along_x(step):
        return remote(s2z.at[span(ahead(x, step, X) * rows_x, rows_x)], r2z.at[step - 1], z2_s.at[step - 1],
                      z2_r.at[step - 1], device(z, ahead(x, step, X), y, c))

    def along_y(step):
        return remote(s3z.at[span(ahead(y, step, Y) * small, small)], r3z.at[step - 1], z3_s.at[step - 1],
                      z3_r.at[step - 1], device(z, x, ahead(y, step, Y), c))

    def back_y(step, behind):
        rows = span(x * rows_x + ahead(y, -behind, Y) * small, small)
        return push((mine_z, rows, half), b3_s.at[step - 1], b3_r.at[step - 1], device(z, x, ahead(y, step, Y), c))

    def back_x(step, behind):
        rows = span(ahead(x, -behind, X) * rows_x, rows_x)
        return push((mine_z, rows, half), b2_s.at[step - 1], b2_r.at[step - 1], device(z, ahead(x, step, X), y, c))

    def back_z(dz):
        return push((mine_z, pl.ds(0, 256), half), b1_s.at[dz - 1], b1_r.at[slot], device(ahead(z, dz, Z), x, y, c))

    def products_z():
        for k in range(first_z, first_z + count_z):
            own[k] = dot(cols_t[k], half_grads[0])

    def stage1_z():
        for i in range(count_z):
            k = first_z + i
            value = own[k] + dot(cols_sister[k], half_grads[2])
            own[k] = value
            s1[k] = value.astype(BF16)

            @pl.when(z != owners[i])
            def _():
                toward(i).start()

    def stage2_z():
        @pl.when(is_owner)
        def _():
            value = own[mine_z]
            for place in range(Z - 1):
                remote(s1.at[first_z], rz.at[place], z1_s.at[0], z1_r.at[place], here).wait_recv()
                value = value + rz[place].astype(F32)
            own2z[...] = value
            s2z[...] = value.astype(BF16)
            for step in far_first(X):
                along_x(step).start()

    def stage3_z():
        @pl.when(is_owner)
        def _():
            value = own2z[span(x * rows_x, rows_x), :]
            for step in far_first(X):
                along_x(step).wait_recv()
                value = value + r2z[step - 1].astype(F32)
            own3z[...] = value
            s3z[...] = value.astype(BF16)
            for step in far_first(Y):
                along_y(step).start()

    def back3_z():
        @pl.when(is_owner)
        def _():
            value = own3z[span(y * small, small), :]
            for step in far_first(Y):
                along_y(step).wait_recv()
                value = value + r3z[step - 1].astype(F32)
            outb[mine_z, span(x * rows_x + y * small, small), half] = (value * inverse_root[:, :128]).astype(BF16)
            for step in far_first(Y):
                back_y(step, 0).start()

    def back2_z():
        @pl.when(is_owner)
        def _():
            for step in far_first(Y):
                back_y(step, step).wait_recv()
            for step in far_first(X):
                back_x(step, 0).start()

    def back1_z():
        @pl.when(is_owner)
        def _():
            for step in far_first(X):
                back_x(step, step).wait_recv()
            for dz in far_first(Z):
                back_z(dz).start()

    def offset_z(i, lanes, send, receive, to):
        return push((first_z + i, pl.ds(0, 256), lanes), send, receive, to)

    def back0_z():
        for i in range(count_z):
            @pl.when(z != owners[i])
            def _():
                offset_z(i, half, b1_s.at[0], b1_r.at[i], here).wait_recv()

            copy = offset_z(i, half, b0_s.at[i], b0_r.at[i], sister)
            copy.start()
            sent.append(copy)

    def finish_z():
        for i in range(count_z):
            @pl.when(z != owners[i])
            def _():
                toward(i).wait_send()

        @pl.when(is_owner)
        def _():
            for step in range(1, X):
                along_x(step).wait_send()
                back_x(step, 0).wait_send()
            for step in range(1, Y):
                along_y(step).wait_send()
                back_y(step, 0).wait_send()
            for dz in range(1, Z):
                back_z(dz).wait_send()

        for i in range(count_z):
            offset_z(i, other_half, b0_s.at[i], b0_r.at[i], here).wait_recv()

    def column_grads():
        grad_s[...] = jnp.zeros_like(grad_s)
        for k in range(27):
            a, b, shift = k // 9, k // 3 % 3, k % 3
            product = lax.dot_general(cg_s[...], weight[k], (((1,), (1,)), ((), ())), preferred_element_type=F32)
            for i in range(4):
                start = (a + i) * 96 + b * 16
                grad_s[shift, start : start + 64, :] += product[i * 64 : (i + 1) * 64, :]

    def brick_grads():
        result = None
        for shift in range(3):
            value = grad_s[shift]
            high = value.astype(BF16)
            low = (value - high.astype(F32)).astype(BF16)
            term = dot(gath_t[shift], jnp.concatenate([high, low], axis=1))
            result = term if result is None else result + term
        result = result[:, :256] + result[:, 256:]
        local_s[...] = result[:256]
        ghosts[...] = result[256:].astype(BF16).reshape(8, 64, 256)
        going["ghosts", 0] = []
        for d in range(8):
            copy = remote(ghosts.at[d], returned.at[d], gh_s.at[d], gh_r.at[d], neighbour(-ROWS[d], -COLUMNS[d]))
            copy.start()
            going["ghosts", 0].append(copy)

    def feature_grads():
        out_bricks = dot(to_bricks, out_masked.astype(BF16))
        arrive("ghosts", 0)
        for b in range(4):
            rows = slice(b * 64, (b + 1) * 64)
            extra = out_bricks[rows] + local_s[rows, :]
            for d in range(8):
                extra = extra + jnp.where(send_ref[0, d] == b, returned[d].astype(F32), 0.0)
            fgrad_ref[b] = (extra * occ_brick[rows]).astype(BF16)

    schedule = (
        (products, 0), (products, 1), (products_z,), (hear_sister,),
        (stage1, 0), (stage1, 1), (stage1_z,),
        (products, 2), (products, 3), (stage1, 2), (stage1, 3),
        (column_grads,), (settle,),
        (stage2, 0), (stage2, 1), (stage2_z,),
        (stage3,), (stage3_z,),
        (brick_grads,),
        (back3_z,), (back3,),
        (back2_z,), (feature_grads,), (back2,),
        (back1_z,), (back1, 0), (back1, 1),
        (settle,),
        (back0,), (back0_z,), (finish,), (finish_z,), (settle,),
    )
    for step, *piece in schedule:
        step(*piece)


def write_out(block, fgrad, wgrad, ggrad, bgrad, block_out, fgrad_out, wgrad_out, ggrad_out, bgrad_out, sems):
    pairs = [(block, block_out), (fgrad, fgrad_out), (ggrad, ggrad_out), (bgrad, bgrad_out)]
    pairs.append((wgrad, wgrad_out))
    copies = [pltpu.make_async_copy(source, target, sems.at[i]) for i, (source, target) in enumerate(pairs)]
    for copy in copies:
        copy.start()
    for copy in copies:
        copy.wait()


def on_device(features, occupancy, neighbours, send_list, weight, gamma, beta, out_grad):
    vmem = pl.BlockSpec(memory_space=pltpu.VMEM)
    small = 256 // (X * Y)
    near, far = max(X, Y) - 1, Z - 1
    depth = slots() // Z
    third = THIRD[1]
    pieces = len(PIECES)
    dma = pltpu.SemaphoreType.DMA
    scratch = [
        pltpu.VMEM((4, 64), I32),
        pltpu.VMEM((4, 27), I32),
        pltpu.VMEM((4, 64, 256), BF16),
        pltpu.VMEM((1, 256), F32),
        pltpu.VMEM((1, 256), F32),
        pltpu.VMEM((4, 64, 256), BF16),
        pltpu.VMEM((16, 128), F32),
        pltpu.VMEM((256, 256), F32),
        pltpu.VMEM((4, 64, 256), BF16),
        pltpu.VMEM((8, 64, 256), BF16),
        pltpu.VMEM((12, 64, 256), BF16),
        pltpu.VMEM((3, 576, 768), BF16),
        pltpu.VMEM((3, 768, 576), BF16),
        pltpu.VMEM((3, 576, 256), BF16),
        pltpu.VMEM((27, 256, 256), BF16),
        pltpu.VMEM((256, 256), F32),
        pltpu.VMEM((256, 256), F32),
        pltpu.VMEM((27, 256, 256), BF16),
        pltpu.VMEM((2 * Z, 8, 128), F32),
        pltpu.VMEM((X * Y, 8, 128), F32),
        pltpu.VMEM((2 * Z, 8, 128), F32),
        pltpu.VMEM((X * Y, 8, 128), F32),
        pltpu.VMEM((256, 256), BF16),
        pltpu.VMEM((3, 576, 256), F32),
        pltpu.VMEM((256, 256), F32),
        pltpu.VMEM((8, 64, 256), BF16),
        pltpu.VMEM((8, 64, 256), BF16),
        pltpu.VMEM((27, 256, 256), BF16),
        pltpu.VMEM((3, 256, 128), BF16),
        pltpu.VMEM((27, 256, 128), F32),
        pltpu.VMEM((27, 256, 128), BF16),
        pltpu.VMEM((near, 27, 256 // min(X, Y), 128), BF16),
        pltpu.VMEM((27, 256 // min(X, Y), 128), BF16),
        pltpu.VMEM((near, 27, small, 128), BF16),
        pltpu.VMEM((slots(), small, 128), BF16),
        pltpu.VMEM((slots(), small, 128), F32),
        pltpu.VMEM((far, depth, small, 128), BF16),
        pltpu.VMEM((slots(), small, 128), BF16),
        pltpu.VMEM((far, 256, 128), BF16),
        pltpu.VMEM((256, 128), F32),
        pltpu.VMEM((256, 128), BF16),
        pltpu.VMEM((near, 256 // X, 128), BF16),
        pltpu.VMEM((256 // X, 128), F32),
        pltpu.VMEM((256 // X, 128), BF16),
        pltpu.VMEM((near, small, 128), BF16),
        dma((7,)), dma((8,)), dma((8,)),
        dma((2 * Z - 1,)), dma((2 * Z - 1,)), dma((X * Y - 1,)), dma((X * Y - 1,)),
        dma((2 * Z - 1,)), dma((2 * Z - 1,)), dma((X * Y - 1,)), dma((X * Y - 1,)),
        dma((8,)), dma((8,)), dma((2,)), dma((2,)), dma, dma,
        dma((pieces, near)), dma((pieces, near)), dma((2, near)), dma((2, near)), dma((far,)), dma((far,)),
        dma((far,)), dma((far,)), dma((2, near)), dma((2, near)),
        dma((2, near)), dma((2, near)), dma((2, near + 1)), dma((2, near + 1)),
        dma((third,)), dma((far,)), dma((near,)), dma((near,)), dma((near,)), dma((near,)),
        dma((near,)), dma((near,)), dma((near,)), dma((near,)), dma((far,)), dma((third,)), dma((third,)), dma((third,)),
    ]
    anywhere = pl.BlockSpec(memory_space=pl.ANY)
    results = pl.pallas_call(
        kernel,
        name="brick_block",
        out_shape=(
            pltpu.VMEM((4, 64, 256), BF16),
            pltpu.VMEM((4, 64, 256), BF16),
            pltpu.VMEM((27, 256, 256), BF16),
            pltpu.VMEM((1, 256), F32),
            pltpu.VMEM((1, 256), F32),
        ),
        in_specs=[anywhere, anywhere, pl.BlockSpec(memory_space=pltpu.SMEM)] + [anywhere] * 5,
        out_specs=(vmem, vmem, vmem, vmem, vmem),
        scratch_shapes=scratch,
        compiler_params=pltpu.CompilerParams(
            collective_id=0, has_side_effects=True, vmem_limit_bytes=56 * 2**20),
    )(occupancy, neighbours, send_list.reshape(1, 8), features, gamma.reshape(1, 256), beta.reshape(1, 256), out_grad, weight)
    block, fgrad, wgrad, ggrad, bgrad = pl.pallas_call(
        write_out,
        name="write_out",
        out_shape=(
            jax.ShapeDtypeStruct((4, 64, 256), BF16),
            jax.ShapeDtypeStruct((4, 64, 256), BF16),
            jax.ShapeDtypeStruct((27, 256, 256), BF16),
            jax.ShapeDtypeStruct((1, 256), F32),
            jax.ShapeDtypeStruct((1, 256), F32),
        ),
        in_specs=[anywhere] * 5,
        out_specs=(anywhere,) * 5,
        scratch_shapes=[dma((5,))],
        compiler_params=pltpu.CompilerParams(vmem_limit_bytes=8 * 2**20),
    )(*results)
    return block, fgrad, wgrad, ggrad.reshape(256), bgrad.reshape(256)


def solution(mesh):
    placed = (
        P(("gx", "gy"), None, None),
        P(("gx", "gy"), None),
        P(("gx", "gy"), None),
        P(("gx", "gy"), None, None),
        P(),
        P(),
        P(),
        P(("gx", "gy"), None, None),
    )
    return jax.shard_map(
        on_device,
        mesh=mesh,
        in_specs=placed,
        out_specs=(P(("gx", "gy"), None, None), P(("gx", "gy"), None, None), P(), P(), P()),
        check_vma=False,
    )
```

```python
import functools

import jax
import jax.numpy as jnp
from jax import lax
from jax.experimental import pallas as pl
from jax.experimental.pallas import tpu as pltpu
from jax.sharding import PartitionSpec as P

Z, X, YH, YL = 8, 4, 2, 2
Y = YH * YL

ROWS = (-1, -1, -1, 0, 0, 1, 1, 1)
COLUMNS = (-1, 0, 1, -1, 1, -1, 0, 1)
EPSILON = 1e-05
MESH = pl.DeviceIdType.MESH
F32, BF16, I32 = jnp.float32, jnp.bfloat16, jnp.int32

PARTS = ((0, 11), (11, 11))
PIECES = ((0, 5, 0), (11, 5, 1), (5, 6, 0), (16, 6, 1))
THIRD = (22, 5)


def slots():
    return -(-THIRD[0] // Z) * Z


def far_first(count):
    return sorted(range(1, count), key=lambda step: -min(step, count - step))


def coordinates():
    gx, gy = lax.axis_index("gx"), lax.axis_index("gy")
    z = lax.div(gx, X * YH)
    x = lax.rem(lax.div(gx, YH), X)
    y = lax.rem(gx, YH) * YL + lax.div(gy, 2)
    return z, x, y, lax.rem(gy, 2)


def device(z, x, y, c):
    return (z * (X * YH) + x * YH + lax.div(y, YL), lax.rem(y, YL) * 2 + c)


def ahead(value, steps, count):
    return lax.rem(value + (steps + count) % count, count)


def dot(a, b):
    return jnp.dot(a, b, preferred_element_type=F32)


def place_row(p):
    return (p >= 1).astype(I32) + (p >= 5).astype(I32)


def kernel(
    occ_hbm, nb_hbm, send_ref, feat_hbm, gamma_hbm, beta_hbm, og_hbm, w_hbm,
    block_ref, fgrad_ref, outb, ggrad_ref, bgrad_ref,
    occ_ref, nb_ref, feat_ref, gamma_ref, beta_ref, og_ref, tab, occn, masked, packets, ext, gath, gath_t, slabs, weight, conv_s, norm_s, cols_t,
    deep1, wide1, deep2, wide2,
    cg_s, grad_s, local_s, ghosts, returned,
    cols_sister, half_grads, own, s1, r1, s2, r2, s3, t3, r3, gathered, rz, own2z, s2z, r2z, own3z, s3z, r3z,
    in_sem, halo_s, halo_r, d1_s, d1_r, w1_s, w1_r, d2_s, d2_r, w2_s, w2_r,
    gh_s, gh_r, cols_s, cols_r, c_s, c_r, q1_s, q1_r, q2_s, q2_r, q3_s, q3_r, a3_s, a3_r, a2_s, a2_r, a1_s, a1_r, a0_s, a0_r,
    z1_s, z1_r, z2_s, z2_r, z3_s, z3_r, b3_s, b3_r, b2_s, b2_r, b1_s, b1_r, b0_s, b0_r,
):
    z, x, y, c = coordinates()
    gx, gy = lax.axis_index("gx"), lax.axis_index("gy")
    ngx, ngy = Z * X * YH, YL * 2

    def neighbour(u, v):
        return (ahead(gx, u, ngx), ahead(gy, v, ngy))

    deep_group = [
        (device(ahead(z, dz, Z), x, y, ahead(c, dc, 2)), ahead(z, -dz, Z) * 2 + ahead(c, dc, 2))
        for dz in far_first(Z) + [0] for dc in (1, 0) if dz + dc > 0]
    wide_group = [
        (device(z, ahead(x, dx, X), ahead(y, dy, Y), c), ahead(x, -dx, X) * Y + ahead(y, -dy, Y))
        for dx, dy in sorted(
            ((dx, dy) for dx in range(X) for dy in range(Y) if dx + dy > 0),
            key=lambda step: -min(step[0], X - step[0]) - min(step[1], Y - step[1]))]

    inputs = [
        pltpu.make_async_copy(source, target, in_sem.at[i])
        for i, (source, target) in enumerate((
            (occ_hbm, occ_ref), (feat_hbm, feat_ref), (nb_hbm, nb_ref), (og_hbm, og_ref),
            (gamma_hbm, gamma_ref), (beta_hbm, beta_ref), (w_hbm, weight)))]
    inputs[0].start()
    inputs[1].start()

    barrier = pltpu.get_barrier_semaphore()
    friends = [neighbour(ROWS[d], COLUMNS[d]) for d in range(8)]
    friends += [friend for friend, _ in deep_group + wide_group]
    for friend in friends:
        pl.semaphore_signal(barrier, inc=1, device_id=friend, device_id_type=MESH)
    for copy in inputs[2:]:
        copy.start()

    sent = []

    def settle():
        for copy in sent:
            copy.wait_send()
        sent.clear()

    tab[...] = jnp.zeros_like(tab)
    inputs[0].wait()
    inputs[1].wait()
    tab[0:4, 0:64] = occ_ref[...].astype(F32)

    def pick(first, index):
        rows = [tab[first + n : first + n + 1, :] for n in range(4)]
        return jnp.where(index == 0, rows[0], jnp.where(index == 1, rows[1], jnp.where(index == 2, rows[2], rows[3])))

    def iotas(rows, lanes):
        shape = (rows, lanes)
        return lax.broadcasted_iota(I32, shape, 0), lax.broadcasted_iota(I32, shape, 1)

    ones = jnp.ones((128, 256), BF16)
    row, lane = iotas(256, 128)
    by_brick = jnp.where(lane == jnp.bitwise_and(row, 63), pick(0, jnp.right_shift(row, 6)), 0.0)
    occ_brick = dot(by_brick.astype(BF16), ones)
    feat = feat_ref[...].reshape(256, 256)
    masked_value = (feat.astype(F32) * occ_brick).astype(BF16)
    masked[...] = masked_value.reshape(4, 64, 256)
    ext[0:4] = masked_value.reshape(4, 64, 256)
    for d in range(8):
        packets[d] = masked[send_ref[0, d]]

    pl.semaphore_wait(barrier, len(friends))
    halo = []
    for d in range(8):
        copy = pltpu.make_async_remote_copy(
            src_ref=packets.at[d], dst_ref=ext.at[4 + d], send_sem=halo_s.at[d], recv_sem=halo_r.at[d],
            device_id=neighbour(ROWS[d], COLUMNS[d]), device_id_type=MESH)
        copy.start()
        halo.append(copy)

    for copy in inputs[2:6]:
        copy.wait()
    by_voxel = jnp.where(
        lane == jnp.right_shift(row, 4) * 4 + jnp.bitwise_and(row, 3),
        pick(0, jnp.bitwise_and(jnp.right_shift(row, 2), 3)), 0.0)
    occ = dot(by_voxel.astype(BF16), ones)
    occn[...] = occ
    row, lane = iotas(256, 256)
    order = jnp.bitwise_and(jnp.right_shift(row, 2), 3) * 64 + jnp.right_shift(row, 4) * 4 + jnp.bitwise_and(row, 3)
    to_rows = jnp.where(lane == order, occ, 0.0).astype(BF16)
    order = jnp.bitwise_and(jnp.right_shift(lane, 2), 3) * 64 + jnp.right_shift(lane, 4) * 4 + jnp.bitwise_and(lane, 3)
    to_bricks = jnp.where(row == order, 1.0, 0.0).astype(BF16)
    out_masked = dot(to_rows, og_ref[...].reshape(256, 256))

    tab[8:12, 0:27] = nb_ref[...].astype(F32)
    table = tab[8:16, :]
    for d in range(8):
        u, v = ROWS[d], COLUMNS[d]
        missing = jnp.int32(0)
        if u != 0:
            missing = missing + (gx == (0 if u > 0 else ngx - 1)).astype(I32)
        if v != 0:
            missing = missing + (gy == (0 if v > 0 else ngy - 1)).astype(I32)
        table = jnp.where((table == 4.0 + d) & (missing > 0), 12.0, table)
    tab[8:16, :] = table
    row, lane = iotas(576, 128)
    pq = jnp.right_shift(row, 4)
    p = jnp.right_shift(pq * 43, 8)
    q = pq - 6 * p
    brick, w = jnp.bitwise_and(jnp.right_shift(row, 2), 3), jnp.bitwise_and(row, 3)
    places = 9 * place_row(p) + 3 * place_row(q)
    voxels = 16 * jnp.bitwise_and(p + 3, 3) + 4 * jnp.bitwise_and(q + 3, 3)
    near = pick(8, brick)
    lane_f = lane.astype(F32)
    for shift in range(3):
        cell = w + shift
        found = dot(jnp.where(lane == places + place_row(cell), near, 0.0).astype(BF16), jnp.ones((128, 128), BF16))
        source = found * 64.0 + (voxels + jnp.bitwise_and(cell + 3, 3)).astype(F32)
        for j in range(6):
            gath[shift, :, j * 128 : (j + 1) * 128] = jnp.where(source == lane_f + 128.0 * j, 1.0, 0.0).astype(BF16)

    for copy in halo:
        copy.wait_recv()
    sent.extend(halo)
    extended = ext[...].reshape(768, 256)
    for shift in range(3):
        slabs[shift] = dot(gath[shift], extended).astype(BF16)

    def columns(k):
        a, b, shift = k // 9, k // 3 % 3, k % 3
        return jnp.concatenate(
            [slabs[shift, (a + i) * 96 + b * 16 : (a + i) * 96 + b * 16 + 64, :] for i in range(4)], axis=0)

    inputs[6].wait()
    conv = dot(columns(0), weight[0])
    for k in range(1, 27):
        conv = conv + dot(columns(k), weight[k])
    conv = conv * occ

    def two(value):
        return jnp.concatenate([value[:, :128], value[:, 128:]], axis=0)

    def one(tile):
        return jnp.concatenate([tile[0:1, :], tile[1:2, :]], axis=1)

    def spread(buffer, place, group, send, receive):
        copies = []
        for i, (friend, _) in enumerate(group):
            copy = pltpu.make_async_remote_copy(
                src_ref=buffer.at[place], dst_ref=buffer.at[place], send_sem=send.at[i], recv_sem=receive.at[i],
                device_id=friend, device_id_type=MESH)
            copy.start()
            copies.append(copy)
        return copies

    def meet(copies, buffer, group, send, receive):
        for i, (friend, behind) in enumerate(group):
            pltpu.make_async_remote_copy(
                src_ref=buffer.at[behind], dst_ref=buffer.at[behind], send_sem=send.at[i], recv_sem=receive.at[i],
                device_id=friend, device_id_type=MESH).wait_recv()
        sent.extend(copies)

    deep, wide = z * 2 + c, x * Y + y

    def sum_of(buffer, count):
        total = buffer[0]
        for i in range(1, count):
            total = total + buffer[i]
        return total

    def merge(buffer, count):
        tiles = [buffer[i] for i in range(count)]
        total = sum(tiles[1:], tiles[0])
        mean = total[0:2, :] / jnp.maximum(total[4:5, :], 1.0)
        square = total[2:4, :]
        for tile in tiles:
            gap = tile[0:2, :] / jnp.maximum(tile[4:5, :], 1.0) - mean
            square = square + tile[4:5, :] * gap * gap
        return total[0:2, :], square, total[4:5, :]

    def write(buffer, place, sums, squares, number):
        buffer[place] = jnp.concatenate([sums, squares, number, jnp.zeros((3, 128), F32)], axis=0)

    number = jnp.sum(occ, axis=0, keepdims=True)
    sums = jnp.sum(conv, axis=0, keepdims=True)
    centred = (conv - sums / jnp.maximum(number, 1.0)) * occ
    squares = jnp.sum(centred * centred, axis=0, keepdims=True)
    write(deep1, deep, two(sums), two(squares), number[:, :128])
    copies = spread(deep1, deep, deep_group, d1_s, d1_r)
    conv_s[...] = conv
    sister, here = device(z, x, y, 1 - c), device(z, x, y, c)

    def share_columns(first, count, i):
        for k in range(first, first + count):
            cols_t[k] = columns(k).T
        copy = pltpu.make_async_remote_copy(
            src_ref=cols_t.at[pl.ds(first, count)], dst_ref=cols_sister.at[pl.ds(first, count)],
            send_sem=cols_s.at[i], recv_sem=cols_r.at[i], device_id=sister, device_id_type=MESH)
        copy.start()
        return copy

    shared = [share_columns(0, 14, 0)]
    meet(copies, deep1, deep_group, d1_s, d1_r)
    write(wide1, wide, *merge(deep1, 2 * Z))
    copies = spread(wide1, wide, wide_group, w1_s, w1_r)
    for shift in range(2):
        gath_t[shift] = gath[shift].T
    meet(copies, wide1, wide_group, w1_s, w1_r)
    sums, squares, number = merge(wide1, X * Y)
    voxel_count = jnp.concatenate([number, number], axis=1)
    average = one(sums) / voxel_count
    inverse_std = lax.rsqrt(one(squares) / voxel_count + EPSILON)
    gamma, beta = gamma_ref[...], beta_ref[...]
    occ = occn[...]
    normalized = (conv_s[...] - average) * inverse_std
    normed = gamma * normalized + beta
    sigmoid = 1.0 / (1.0 + jnp.exp(-normed))
    act_grad = out_masked * sigmoid * (1.0 + normed * (1.0 - sigmoid))
    total = jnp.sum(act_grad, axis=0, keepdims=True)
    cross = jnp.sum(act_grad * normalized, axis=0, keepdims=True)
    write(deep2, deep, two(total), two(cross), jnp.zeros((1, 128), F32))
    copies = spread(deep2, deep, deep_group, d2_s, d2_r)
    centre = columns(13).astype(F32)
    block = (occ * (centre + normed * sigmoid)).astype(BF16)
    block_ref[...] = dot(to_bricks, block).astype(BF16).reshape(4, 64, 256)
    norm_s[...] = normalized
    shared.append(share_columns(14, 13, 1))
    meet(copies, deep2, deep_group, d2_s, d2_r)
    wide2[wide] = sum_of(deep2, 2 * Z)
    copies = spread(wide2, wide, wide_group, w2_s, w2_r)
    gath_t[2] = gath[2].T
    meet(copies, wide2, wide_group, w2_s, w2_r)
    tiles = sum_of(wide2, X * Y)
    total, cross = one(tiles[0:2]), one(tiles[2:4])
    inverse_root = lax.rsqrt(voxel_count)
    ggrad_ref[...] = cross * inverse_root
    bgrad_ref[...] = total * inverse_root
    conv_grad = (gamma * inverse_std * (act_grad - total / voxel_count - norm_s[...] * cross / voxel_count) * occ).astype(BF16)
    cg_s[...] = conv_grad

    half_grads[0] = jnp.where(c == 0, conv_grad[:, :128].astype(F32), conv_grad[:, 128:].astype(F32)).astype(BF16)
    half_grads[1] = jnp.where(c == 0, conv_grad[:, 128:].astype(F32), conv_grad[:, :128].astype(F32)).astype(BF16)
    shared.append(pltpu.make_async_remote_copy(
        src_ref=half_grads.at[1], dst_ref=half_grads.at[2], send_sem=c_s, recv_sem=c_r,
        device_id=sister, device_id_type=MESH))
    shared[2].start()
    small = 256 // (X * Y)
    half = pl.ds(pl.multiple_of(c * 128, 128), 128)
    other_half = pl.ds(pl.multiple_of((1 - c) * 128, 128), 128)
    depth = slots() // Z
    first_z, count_z = THIRD
    owners = [i * Z // count_z for i in range(count_z)]
    slot = sum(i * (z == owner).astype(I32) for i, owner in enumerate(owners))
    is_owner = sum((z == owner).astype(I32) for owner in owners) > 0

    def axes(part):
        return ((y, Y), (x, X)) if part else ((x, X), (y, Y))

    def mate(part, stage, step):
        if part == stage - 1:
            return device(z, ahead(x, step, X), y, c)
        return device(z, x, ahead(y, step, Y), c)

    def span(start, size):
        return pl.ds(pl.multiple_of(start, 16), size)

    def remote(source, target, send, receive, to):
        return pltpu.make_async_remote_copy(
            src_ref=source, dst_ref=target, send_sem=send, recv_sem=receive, device_id=to, device_id_type=MESH)

    going = {}

    def arrive(stage, piece):
        for copy in going.pop((stage, piece)):
            copy.wait_recv()
            sent.append(copy)

    def heard(stage, piece):
        for copy in going.pop((stage, piece)):
            copy.wait_recv()

    def products(piece):
        first, count, _ = PIECES[piece]
        for k in range(first, first + count):
            own[k] = dot(cols_t[k], half_grads[0])

    def hear_sister():
        for copy in shared:
            copy.wait_recv()
            sent.append(copy)

    def stage1(piece):
        first, count, part = PIECES[piece]
        (place, length), _ = axes(part)
        rows = 256 // length
        for k in range(first, first + count):
            value = own[k] + dot(cols_sister[k], half_grads[2])
            own[k] = value
            s1[k] = value.astype(BF16)
        for step in far_first(length):
            copy = remote(
                s1.at[pl.ds(first, count), span(ahead(place, step, length) * rows, rows)],
                r1.at[step - 1, pl.ds(first, count)],
                q1_s.at[piece, step - 1], q1_r.at[piece, step - 1], mate(part, 1, step))
            copy.start()
            going.setdefault(("one", part), []).append(copy)

    def stage2(part):
        first, count = PARTS[part]
        (place, length), (place2, length2) = axes(part)
        rows = 256 // length
        arrive("one", part)
        for k in range(first, first + count):
            value = own[k, span(place * rows, rows), :]
            for step in range(1, length):
                value = value + r1[step - 1, k].astype(F32)
            own[k, 0:rows, :] = value
            s2[k] = value.astype(BF16)
        going["two", part] = []
        for step in far_first(length2):
            copy = remote(
                s2.at[pl.ds(first, count), span(ahead(place2, step, length2) * small, small)],
                r2.at[step - 1, pl.ds(first, count)],
                q2_s.at[part, step - 1], q2_r.at[part, step - 1], mate(part, 2, step))
            copy.start()
            going["two", part].append(copy)

    def stage3():
        for part, (first, count) in enumerate(PARTS):
            _, (place2, length2) = axes(part)
            arrive("two", part)
            for k in range(first, first + count):
                value = own[k, span(place2 * small, small), :]
                for step in range(1, length2):
                    value = value + r2[step - 1, k].astype(F32)
                t3[k] = value
                s3[k] = value.astype(BF16)
        for k in range(first_z, slots()):
            t3[k] = jnp.zeros((small, 128), F32)
            s3[k] = jnp.zeros((small, 128), BF16)
        going["three", 0] = []
        for dz in far_first(Z):
            copy = remote(
                s3.at[pl.ds(ahead(z, dz, Z) * depth, depth)], r3.at[dz - 1],
                q3_s.at[dz - 1], q3_r.at[dz - 1], device(ahead(z, dz, Z), x, y, c))
            copy.start()
            going["three", 0].append(copy)

    def fine(part):
        (place, length), (place2, _) = axes(part)
        return span(place * (256 // length) + place2 * small, small)

    def push(where, send, receive, to):
        return remote(outb.at[where], outb.at[where], send, receive, to)

    def back3():
        arrive("three", 0)
        mine = pl.ds(z * depth, depth)
        value = t3[mine]
        for dz in range(1, Z):
            value = value + r3[dz - 1].astype(F32)
        gathered[mine] = (value * inverse_root[:, :128].reshape(1, 1, 128)).astype(BF16)
        going["back3", 0] = []
        for dz in far_first(Z):
            copy = remote(gathered.at[mine], gathered.at[mine], a3_s.at[dz - 1], a3_r.at[dz - 1],
                          device(ahead(z, dz, Z), x, y, c))
            copy.start()
            sent.append(copy)
            behind = gathered.at[pl.ds(ahead(z, -dz, Z) * depth, depth)]
            going["back3", 0].append(remote(behind, behind, a3_s.at[dz - 1], a3_r.at[dz - 1], here))

    def back2():
        heard("back3", 0)
        for part, (first, count) in enumerate(PARTS):
            (place, length), (place2, length2) = axes(part)
            going["back2", part] = []
            for step in far_first(length2):
                copy = remote(gathered.at[pl.ds(first, count)], outb.at[pl.ds(first, count), fine(part), half],
                              a2_s.at[part, step - 1], a2_r.at[part, step - 1], mate(part, 2, step))
                copy.start()
                sent.append(copy)
                start = place * (256 // length) + ahead(place2, -step, length2) * small
                going["back2", part].append(push(
                    (pl.ds(first, count), span(start, small), half), a2_s.at[part, step - 1],
                    a2_r.at[part, step - 1], here))
        for part, (first, count) in enumerate(PARTS):
            outb[pl.ds(first, count), fine(part), half] = gathered[first : first + count]

    def strip(part, step, lanes):
        (place, length), _ = axes(part)
        rows = 256 // length
        return pl.ds(*PARTS[part]), span(ahead(place, -step, length) * rows, rows), lanes

    def hand_over(part, step):
        copy = push(strip(part, step, half), a0_s.at[part, step], a0_r.at[part, step], sister)
        copy.start()
        sent.append(copy)

    def back1(part):
        _, length = axes(part)[0]
        heard("back2", part)
        for step in far_first(length):
            copy = push(strip(part, 0, half), a1_s.at[part, step - 1], a1_r.at[part, step - 1], mate(part, 1, step))
            copy.start()
            sent.append(copy)
        hand_over(part, 0)

    def back0():
        for step in (1, 3, 2):
            for part in range(2):
                if step < axes(part)[0][1]:
                    push(strip(part, step, half), a1_s.at[part, step - 1], a1_r.at[part, step - 1], here).wait_recv()
                    hand_over(part, step)

    def finish():
        for step in (0, 1, 3, 2):
            for part in range(2):
                if step < axes(part)[0][1]:
                    push(strip(part, step, other_half), a0_s.at[part, step], a0_r.at[part, step], here).wait_recv()

    rows_x, mine_z = 256 // X, first_z + slot

    def toward(i):
        steps = lax.rem(owners[i] + Z - z, Z)
        place = jnp.maximum(steps - 1, 0)
        return remote(s1.at[first_z + i], rz.at[place], z1_s.at[i], z1_r.at[place], device(jnp.int32(owners[i]), x, y, c))

    def along_x(step):
        return remote(s2z.at[span(ahead(x, step, X) * rows_x, rows_x)], r2z.at[step - 1], z2_s.at[step - 1],
                      z2_r.at[step - 1], device(z, ahead(x, step, X), y, c))

    def along_y(step):
        return remote(s3z.at[span(ahead(y, step, Y) * small, small)], r3z.at[step - 1], z3_s.at[step - 1],
                      z3_r.at[step - 1], device(z, x, ahead(y, step, Y), c))

    def back_y(step, behind):
        rows = span(x * rows_x + ahead(y, -behind, Y) * small, small)
        return push((mine_z, rows, half), b3_s.at[step - 1], b3_r.at[step - 1], device(z, x, ahead(y, step, Y), c))

    def back_x(step, behind):
        rows = span(ahead(x, -behind, X) * rows_x, rows_x)
        return push((mine_z, rows, half), b2_s.at[step - 1], b2_r.at[step - 1], device(z, ahead(x, step, X), y, c))

    def back_z(dz):
        return push((mine_z, pl.ds(0, 256), half), b1_s.at[dz - 1], b1_r.at[slot], device(ahead(z, dz, Z), x, y, c))

    def products_z():
        for k in range(first_z, first_z + count_z):
            own[k] = dot(cols_t[k], half_grads[0])

    def stage1_z():
        for i in range(count_z):
            k = first_z + i
            value = own[k] + dot(cols_sister[k], half_grads[2])
            own[k] = value
            s1[k] = value.astype(BF16)

            @pl.when(z != owners[i])
            def _():
                toward(i).start()

    def stage2_z():
        @pl.when(is_owner)
        def _():
            value = own[mine_z]
            for place in range(Z - 1):
                remote(s1.at[first_z], rz.at[place], z1_s.at[0], z1_r.at[place], here).wait_recv()
                value = value + rz[place].astype(F32)
            own2z[...] = value
            s2z[...] = value.astype(BF16)
            for step in far_first(X):
                along_x(step).start()

    def stage3_z():
        @pl.when(is_owner)
        def _():
            value = own2z[span(x * rows_x, rows_x), :]
            for step in far_first(X):
                along_x(step).wait_recv()
                value = value + r2z[step - 1].astype(F32)
            own3z[...] = value
            s3z[...] = value.astype(BF16)
            for step in far_first(Y):
                along_y(step).start()

    def back3_z():
        @pl.when(is_owner)
        def _():
            value = own3z[span(y * small, small), :]
            for step in far_first(Y):
                along_y(step).wait_recv()
                value = value + r3z[step - 1].astype(F32)
            outb[mine_z, span(x * rows_x + y * small, small), half] = (value * inverse_root[:, :128]).astype(BF16)
            for step in far_first(Y):
                back_y(step, 0).start()

    def back2_z():
        @pl.when(is_owner)
        def _():
            for step in far_first(Y):
                back_y(step, step).wait_recv()
            for step in far_first(X):
                back_x(step, 0).start()

    def back1_z():
        @pl.when(is_owner)
        def _():
            for step in far_first(X):
                back_x(step, step).wait_recv()
            for dz in far_first(Z):
                back_z(dz).start()

    def offset_z(i, lanes, send, receive, to):
        return push((first_z + i, pl.ds(0, 256), lanes), send, receive, to)

    def back0_z():
        for i in range(count_z):
            @pl.when(z != owners[i])
            def _():
                offset_z(i, half, b1_s.at[0], b1_r.at[i], here).wait_recv()

            copy = offset_z(i, half, b0_s.at[i], b0_r.at[i], sister)
            copy.start()
            sent.append(copy)

    def finish_z():
        for i in range(count_z):
            @pl.when(z != owners[i])
            def _():
                toward(i).wait_send()

        @pl.when(is_owner)
        def _():
            for step in range(1, X):
                along_x(step).wait_send()
                back_x(step, 0).wait_send()
            for step in range(1, Y):
                along_y(step).wait_send()
                back_y(step, 0).wait_send()
            for dz in range(1, Z):
                back_z(dz).wait_send()

        for i in range(count_z):
            offset_z(i, other_half, b0_s.at[i], b0_r.at[i], here).wait_recv()

    def column_grads():
        grad_s[...] = jnp.zeros_like(grad_s)
        for k in range(27):
            a, b, shift = k // 9, k // 3 % 3, k % 3
            product = lax.dot_general(cg_s[...], weight[k], (((1,), (1,)), ((), ())), preferred_element_type=F32)
            for i in range(4):
                start = (a + i) * 96 + b * 16
                grad_s[shift, start : start + 64, :] += product[i * 64 : (i + 1) * 64, :]

    def brick_grads():
        result = None
        for shift in range(3):
            value = grad_s[shift]
            high = value.astype(BF16)
            low = (value - high.astype(F32)).astype(BF16)
            term = dot(gath_t[shift], jnp.concatenate([high, low], axis=1))
            result = term if result is None else result + term
        result = result[:, :256] + result[:, 256:]
        local_s[...] = result[:256]
        ghosts[...] = result[256:].astype(BF16).reshape(8, 64, 256)
        going["ghosts", 0] = []
        for d in range(8):
            copy = remote(ghosts.at[d], returned.at[d], gh_s.at[d], gh_r.at[d], neighbour(-ROWS[d], -COLUMNS[d]))
            copy.start()
            going["ghosts", 0].append(copy)

    def feature_grads():
        out_bricks = dot(to_bricks, out_masked.astype(BF16))
        arrive("ghosts", 0)
        for b in range(4):
            rows = slice(b * 64, (b + 1) * 64)
            extra = out_bricks[rows] + local_s[rows, :]
            for d in range(8):
                extra = extra + jnp.where(send_ref[0, d] == b, returned[d].astype(F32), 0.0)
            fgrad_ref[b] = (extra * occ_brick[rows]).astype(BF16)

    schedule = (
        (products, 0), (products, 1), (products_z,), (hear_sister,),
        (stage1, 0), (stage1, 1), (stage1_z,),
        (products, 2), (products, 3), (stage1, 2), (stage1, 3),
        (column_grads,), (settle,),
        (stage2, 0), (stage2, 1), (stage2_z,),
        (stage3,), (stage3_z,),
        (brick_grads,),
        (back3_z,), (back3,),
        (back2_z,), (back2,),
        (back1_z,), (back1, 0), (back1, 1),
        (feature_grads,), (settle,),
        (back0,), (back0_z,), (finish,), (finish_z,), (settle,),
    )
    for step, *piece in schedule:
        step(*piece)


def write_out(block, fgrad, wgrad, ggrad, bgrad, block_out, fgrad_out, wgrad_out, ggrad_out, bgrad_out, sems):
    pairs = [(block, block_out), (fgrad, fgrad_out), (ggrad, ggrad_out), (bgrad, bgrad_out)]
    pairs.append((wgrad, wgrad_out))
    copies = [pltpu.make_async_copy(source, target, sems.at[i]) for i, (source, target) in enumerate(pairs)]
    for copy in copies:
        copy.start()
    for copy in copies:
        copy.wait()


def on_device(features, occupancy, neighbours, send_list, weight, gamma, beta, out_grad):
    vmem = pl.BlockSpec(memory_space=pltpu.VMEM)
    small = 256 // (X * Y)
    near, far = max(X, Y) - 1, Z - 1
    depth = slots() // Z
    third = THIRD[1]
    pieces = len(PIECES)
    dma = pltpu.SemaphoreType.DMA
    scratch = [
        pltpu.VMEM((4, 64), I32),
        pltpu.VMEM((4, 27), I32),
        pltpu.VMEM((4, 64, 256), BF16),
        pltpu.VMEM((1, 256), F32),
        pltpu.VMEM((1, 256), F32),
        pltpu.VMEM((4, 64, 256), BF16),
        pltpu.VMEM((16, 128), F32),
        pltpu.VMEM((256, 256), F32),
        pltpu.VMEM((4, 64, 256), BF16),
        pltpu.VMEM((8, 64, 256), BF16),
        pltpu.VMEM((12, 64, 256), BF16),
        pltpu.VMEM((3, 576, 768), BF16),
        pltpu.VMEM((3, 768, 576), BF16),
        pltpu.VMEM((3, 576, 256), BF16),
        pltpu.VMEM((27, 256, 256), BF16),
        pltpu.VMEM((256, 256), F32),
        pltpu.VMEM((256, 256), F32),
        pltpu.VMEM((27, 256, 256), BF16),
        pltpu.VMEM((2 * Z, 8, 128), F32),
        pltpu.VMEM((X * Y, 8, 128), F32),
        pltpu.VMEM((2 * Z, 8, 128), F32),
        pltpu.VMEM((X * Y, 8, 128), F32),
        pltpu.VMEM((256, 256), BF16),
        pltpu.VMEM((3, 576, 256), F32),
        pltpu.VMEM((256, 256), F32),
        pltpu.VMEM((8, 64, 256), BF16),
        pltpu.VMEM((8, 64, 256), BF16),
        pltpu.VMEM((27, 256, 256), BF16),
        pltpu.VMEM((3, 256, 128), BF16),
        pltpu.VMEM((27, 256, 128), F32),
        pltpu.VMEM((27, 256, 128), BF16),
        pltpu.VMEM((near, 27, 256 // min(X, Y), 128), BF16),
        pltpu.VMEM((27, 256 // min(X, Y), 128), BF16),
        pltpu.VMEM((near, 27, small, 128), BF16),
        pltpu.VMEM((slots(), small, 128), BF16),
        pltpu.VMEM((slots(), small, 128), F32),
        pltpu.VMEM((far, depth, small, 128), BF16),
        pltpu.VMEM((slots(), small, 128), BF16),
        pltpu.VMEM((far, 256, 128), BF16),
        pltpu.VMEM((256, 128), F32),
        pltpu.VMEM((256, 128), BF16),
        pltpu.VMEM((near, 256 // X, 128), BF16),
        pltpu.VMEM((256 // X, 128), F32),
        pltpu.VMEM((256 // X, 128), BF16),
        pltpu.VMEM((near, small, 128), BF16),
        dma((7,)), dma((8,)), dma((8,)),
        dma((2 * Z - 1,)), dma((2 * Z - 1,)), dma((X * Y - 1,)), dma((X * Y - 1,)),
        dma((2 * Z - 1,)), dma((2 * Z - 1,)), dma((X * Y - 1,)), dma((X * Y - 1,)),
        dma((8,)), dma((8,)), dma((2,)), dma((2,)), dma, dma,
        dma((pieces, near)), dma((pieces, near)), dma((2, near)), dma((2, near)), dma((far,)), dma((far,)),
        dma((far,)), dma((far,)), dma((2, near)), dma((2, near)),
        dma((2, near)), dma((2, near)), dma((2, near + 1)), dma((2, near + 1)),
        dma((third,)), dma((far,)), dma((near,)), dma((near,)), dma((near,)), dma((near,)),
        dma((near,)), dma((near,)), dma((near,)), dma((near,)), dma((far,)), dma((third,)), dma((third,)), dma((third,)),
    ]
    anywhere = pl.BlockSpec(memory_space=pl.ANY)
    results = pl.pallas_call(
        kernel,
        name="brick_block",
        out_shape=(
            pltpu.VMEM((4, 64, 256), BF16),
            pltpu.VMEM((4, 64, 256), BF16),
            pltpu.VMEM((27, 256, 256), BF16),
            pltpu.VMEM((1, 256), F32),
            pltpu.VMEM((1, 256), F32),
        ),
        in_specs=[anywhere, anywhere, pl.BlockSpec(memory_space=pltpu.SMEM)] + [anywhere] * 5,
        out_specs=(vmem, vmem, vmem, vmem, vmem),
        scratch_shapes=scratch,
        compiler_params=pltpu.CompilerParams(
            collective_id=0, has_side_effects=True, vmem_limit_bytes=56 * 2**20),
    )(occupancy, neighbours, send_list.reshape(1, 8), features, gamma.reshape(1, 256), beta.reshape(1, 256), out_grad, weight)
    block, fgrad, wgrad, ggrad, bgrad = pl.pallas_call(
        write_out,
        name="write_out",
        out_shape=(
            jax.ShapeDtypeStruct((4, 64, 256), BF16),
            jax.ShapeDtypeStruct((4, 64, 256), BF16),
            jax.ShapeDtypeStruct((27, 256, 256), BF16),
            jax.ShapeDtypeStruct((1, 256), F32),
            jax.ShapeDtypeStruct((1, 256), F32),
        ),
        in_specs=[anywhere] * 5,
        out_specs=(anywhere,) * 5,
        scratch_shapes=[dma((5,))],
        compiler_params=pltpu.CompilerParams(vmem_limit_bytes=8 * 2**20),
    )(*results)
    return block, fgrad, wgrad, ggrad.reshape(256), bgrad.reshape(256)


def solution(mesh):
    placed = (
        P(("gx", "gy"), None, None),
        P(("gx", "gy"), None),
        P(("gx", "gy"), None),
        P(("gx", "gy"), None, None),
        P(),
        P(),
        P(),
        P(("gx", "gy"), None, None),
    )
    return jax.shard_map(
        on_device,
        mesh=mesh,
        in_specs=placed,
        out_specs=(P(("gx", "gy"), None, None), P(("gx", "gy"), None, None), P(), P(), P()),
        check_vma=False,
    )
```

```python
import functools

import jax
import jax.numpy as jnp
from jax import lax
from jax.experimental import pallas as pl
from jax.experimental.pallas import tpu as pltpu
from jax.sharding import PartitionSpec as P

Z, X, YH, YL = 8, 4, 2, 2
Y = YH * YL

ROWS = (-1, -1, -1, 0, 0, 1, 1, 1)
COLUMNS = (-1, 0, 1, -1, 1, -1, 0, 1)
EPSILON = 1e-05
MESH = pl.DeviceIdType.MESH
F32, BF16, I32 = jnp.float32, jnp.bfloat16, jnp.int32

PARTS = ((0, 11), (11, 11))
PIECES = ((0, 3, 0), (11, 3, 1), (3, 8, 0), (14, 8, 1))
THIRD = (22, 5)


def slots():
    return -(-THIRD[0] // Z) * Z


def far_first(count):
    return sorted(range(1, count), key=lambda step: -min(step, count - step))


def coordinates():
    gx, gy = lax.axis_index("gx"), lax.axis_index("gy")
    z = lax.div(gx, X * YH)
    x = lax.rem(lax.div(gx, YH), X)
    y = lax.rem(gx, YH) * YL + lax.div(gy, 2)
    return z, x, y, lax.rem(gy, 2)


def device(z, x, y, c):
    return (z * (X * YH) + x * YH + lax.div(y, YL), lax.rem(y, YL) * 2 + c)


def ahead(value, steps, count):
    return lax.rem(value + (steps + count) % count, count)


def dot(a, b):
    return jnp.dot(a, b, preferred_element_type=F32)


def place_row(p):
    return (p >= 1).astype(I32) + (p >= 5).astype(I32)


def kernel(
    occ_hbm, nb_hbm, send_ref, feat_hbm, gamma_hbm, beta_hbm, og_hbm, w_hbm,
    block_ref, fgrad_ref, outb, ggrad_ref, bgrad_ref,
    occ_ref, nb_ref, feat_ref, gamma_ref, beta_ref, og_ref, tab, occn, masked, packets, ext, gath, gath_t, slabs, weight, conv_s, norm_s, cols_t,
    deep1, wide1, deep2, wide2,
    cg_s, grad_s, local_s, ghosts, returned,
    cols_sister, half_grads, own, s1, r1, s2, r2, s3, t3, r3, gathered, rz, own2z, s2z, r2z, own3z, s3z, r3z,
    in_sem, halo_s, halo_r, d1_s, d1_r, w1_s, w1_r, d2_s, d2_r, w2_s, w2_r,
    gh_s, gh_r, cols_s, cols_r, c_s, c_r, q1_s, q1_r, q2_s, q2_r, q3_s, q3_r, a3_s, a3_r, a2_s, a2_r, a1_s, a1_r, a0_s, a0_r,
    z1_s, z1_r, z2_s, z2_r, z3_s, z3_r, b3_s, b3_r, b2_s, b2_r, b1_s, b1_r, b0_s, b0_r,
):
    z, x, y, c = coordinates()
    gx, gy = lax.axis_index("gx"), lax.axis_index("gy")
    ngx, ngy = Z * X * YH, YL * 2

    def neighbour(u, v):
        return (ahead(gx, u, ngx), ahead(gy, v, ngy))

    deep_group = [
        (device(ahead(z, dz, Z), x, y, ahead(c, dc, 2)), ahead(z, -dz, Z) * 2 + ahead(c, dc, 2))
        for dz in far_first(Z) + [0] for dc in (1, 0) if dz + dc > 0]
    wide_group = [
        (device(z, ahead(x, dx, X), ahead(y, dy, Y), c), ahead(x, -dx, X) * Y + ahead(y, -dy, Y))
        for dx, dy in sorted(
            ((dx, dy) for dx in range(X) for dy in range(Y) if dx + dy > 0),
            key=lambda step: -min(step[0], X - step[0]) - min(step[1], Y - step[1]))]

    inputs = [
        pltpu.make_async_copy(source, target, in_sem.at[i])
        for i, (source, target) in enumerate((
            (occ_hbm, occ_ref), (feat_hbm, feat_ref), (nb_hbm, nb_ref), (og_hbm, og_ref),
            (gamma_hbm, gamma_ref), (beta_hbm, beta_ref), (w_hbm, weight)))]
    inputs[0].start()
    inputs[1].start()

    barrier = pltpu.get_barrier_semaphore()
    friends = [neighbour(ROWS[d], COLUMNS[d]) for d in range(8)]
    friends += [friend for friend, _ in deep_group + wide_group]
    for friend in friends:
        pl.semaphore_signal(barrier, inc=1, device_id=friend, device_id_type=MESH)
    for copy in inputs[2:]:
        copy.start()

    sent = []

    def settle():
        for copy in sent:
            copy.wait_send()
        sent.clear()

    tab[...] = jnp.zeros_like(tab)
    inputs[0].wait()
    inputs[1].wait()
    tab[0:4, 0:64] = occ_ref[...].astype(F32)

    def pick(first, index):
        rows = [tab[first + n : first + n + 1, :] for n in range(4)]
        return jnp.where(index == 0, rows[0], jnp.where(index == 1, rows[1], jnp.where(index == 2, rows[2], rows[3])))

    def iotas(rows, lanes):
        shape = (rows, lanes)
        return lax.broadcasted_iota(I32, shape, 0), lax.broadcasted_iota(I32, shape, 1)

    ones = jnp.ones((128, 256), BF16)
    row, lane = iotas(256, 128)
    by_brick = jnp.where(lane == jnp.bitwise_and(row, 63), pick(0, jnp.right_shift(row, 6)), 0.0)
    occ_brick = dot(by_brick.astype(BF16), ones)
    feat = feat_ref[...].reshape(256, 256)
    masked_value = (feat.astype(F32) * occ_brick).astype(BF16)
    masked[...] = masked_value.reshape(4, 64, 256)
    ext[0:4] = masked_value.reshape(4, 64, 256)
    for d in range(8):
        packets[d] = masked[send_ref[0, d]]

    pl.semaphore_wait(barrier, len(friends))
    halo = []
    for d in range(8):
        copy = pltpu.make_async_remote_copy(
            src_ref=packets.at[d], dst_ref=ext.at[4 + d], send_sem=halo_s.at[d], recv_sem=halo_r.at[d],
            device_id=neighbour(ROWS[d], COLUMNS[d]), device_id_type=MESH)
        copy.start()
        halo.append(copy)

    for copy in inputs[2:6]:
        copy.wait()
    by_voxel = jnp.where(
        lane == jnp.right_shift(row, 4) * 4 + jnp.bitwise_and(row, 3),
        pick(0, jnp.bitwise_and(jnp.right_shift(row, 2), 3)), 0.0)
    occ = dot(by_voxel.astype(BF16), ones)
    occn[...] = occ
    row, lane = iotas(256, 256)
    order = jnp.bitwise_and(jnp.right_shift(row, 2), 3) * 64 + jnp.right_shift(row, 4) * 4 + jnp.bitwise_and(row, 3)
    to_rows = jnp.where(lane == order, occ, 0.0).astype(BF16)
    order = jnp.bitwise_and(jnp.right_shift(lane, 2), 3) * 64 + jnp.right_shift(lane, 4) * 4 + jnp.bitwise_and(lane, 3)
    to_bricks = jnp.where(row == order, 1.0, 0.0).astype(BF16)
    out_masked = dot(to_rows, og_ref[...].reshape(256, 256))

    tab[8:12, 0:27] = nb_ref[...].astype(F32)
    table = tab[8:16, :]
    for d in range(8):
        u, v = ROWS[d], COLUMNS[d]
        missing = jnp.int32(0)
        if u != 0:
            missing = missing + (gx == (0 if u > 0 else ngx - 1)).astype(I32)
        if v != 0:
            missing = missing + (gy == (0 if v > 0 else ngy - 1)).astype(I32)
        table = jnp.where((table == 4.0 + d) & (missing > 0), 12.0, table)
    tab[8:16, :] = table
    row, lane = iotas(576, 128)
    pq = jnp.right_shift(row, 4)
    p = jnp.right_shift(pq * 43, 8)
    q = pq - 6 * p
    brick, w = jnp.bitwise_and(jnp.right_shift(row, 2), 3), jnp.bitwise_and(row, 3)
    places = 9 * place_row(p) + 3 * place_row(q)
    voxels = 16 * jnp.bitwise_and(p + 3, 3) + 4 * jnp.bitwise_and(q + 3, 3)
    near = pick(8, brick)
    lane_f = lane.astype(F32)
    for shift in range(3):
        cell = w + shift
        found = dot(jnp.where(lane == places + place_row(cell), near, 0.0).astype(BF16), jnp.ones((128, 128), BF16))
        source = found * 64.0 + (voxels + jnp.bitwise_and(cell + 3, 3)).astype(F32)
        for j in range(6):
            gath[shift, :, j * 128 : (j + 1) * 128] = jnp.where(source == lane_f + 128.0 * j, 1.0, 0.0).astype(BF16)

    for copy in halo:
        copy.wait_recv()
    sent.extend(halo)
    extended = ext[...].reshape(768, 256)
    for shift in range(3):
        slabs[shift] = dot(gath[shift], extended).astype(BF16)

    def columns(k):
        a, b, shift = k // 9, k // 3 % 3, k % 3
        return jnp.concatenate(
            [slabs[shift, (a + i) * 96 + b * 16 : (a + i) * 96 + b * 16 + 64, :] for i in range(4)], axis=0)

    inputs[6].wait()
    conv = dot(columns(0), weight[0])
    for k in range(1, 27):
        conv = conv + dot(columns(k), weight[k])
    conv = conv * occ

    def two(value):
        return jnp.concatenate([value[:, :128], value[:, 128:]], axis=0)

    def one(tile):
        return jnp.concatenate([tile[0:1, :], tile[1:2, :]], axis=1)

    def spread(buffer, place, group, send, receive):
        copies = []
        for i, (friend, _) in enumerate(group):
            copy = pltpu.make_async_remote_copy(
                src_ref=buffer.at[place], dst_ref=buffer.at[place], send_sem=send.at[i], recv_sem=receive.at[i],
                device_id=friend, device_id_type=MESH)
            copy.start()
            copies.append(copy)
        return copies

    def meet(copies, buffer, group, send, receive):
        for i, (friend, behind) in enumerate(group):
            pltpu.make_async_remote_copy(
                src_ref=buffer.at[behind], dst_ref=buffer.at[behind], send_sem=send.at[i], recv_sem=receive.at[i],
                device_id=friend, device_id_type=MESH).wait_recv()
        sent.extend(copies)

    deep, wide = z * 2 + c, x * Y + y

    def sum_of(buffer, count):
        total = buffer[0]
        for i in range(1, count):
            total = total + buffer[i]
        return total

    def merge(buffer, count):
        tiles = [buffer[i] for i in range(count)]
        total = sum(tiles[1:], tiles[0])
        mean = total[0:2, :] / jnp.maximum(total[4:5, :], 1.0)
        square = total[2:4, :]
        for tile in tiles:
            gap = tile[0:2, :] / jnp.maximum(tile[4:5, :], 1.0) - mean
            square = square + tile[4:5, :] * gap * gap
        return total[0:2, :], square, total[4:5, :]

    def write(buffer, place, sums, squares, number):
        buffer[place] = jnp.concatenate([sums, squares, number, jnp.zeros((3, 128), F32)], axis=0)

    number = jnp.sum(occ, axis=0, keepdims=True)
    sums = jnp.sum(conv, axis=0, keepdims=True)
    centred = (conv - sums / jnp.maximum(number, 1.0)) * occ
    squares = jnp.sum(centred * centred, axis=0, keepdims=True)
    write(deep1, deep, two(sums), two(squares), number[:, :128])
    copies = spread(deep1, deep, deep_group, d1_s, d1_r)
    conv_s[...] = conv
    sister, here = device(z, x, y, 1 - c), device(z, x, y, c)

    def share_columns(first, count, i):
        for k in range(first, first + count):
            cols_t[k] = columns(k).T
        copy = pltpu.make_async_remote_copy(
            src_ref=cols_t.at[pl.ds(first, count)], dst_ref=cols_sister.at[pl.ds(first, count)],
            send_sem=cols_s.at[i], recv_sem=cols_r.at[i], device_id=sister, device_id_type=MESH)
        copy.start()
        return copy

    shared = [share_columns(0, 14, 0)]
    meet(copies, deep1, deep_group, d1_s, d1_r)
    write(wide1, wide, *merge(deep1, 2 * Z))
    copies = spread(wide1, wide, wide_group, w1_s, w1_r)
    for shift in range(2):
        gath_t[shift] = gath[shift].T
    meet(copies, wide1, wide_group, w1_s, w1_r)
    sums, squares, number = merge(wide1, X * Y)
    voxel_count = jnp.concatenate([number, number], axis=1)
    average = one(sums) / voxel_count
    inverse_std = lax.rsqrt(one(squares) / voxel_count + EPSILON)
    gamma, beta = gamma_ref[...], beta_ref[...]
    occ = occn[...]
    normalized = (conv_s[...] - average) * inverse_std
    normed = gamma * normalized + beta
    sigmoid = 1.0 / (1.0 + jnp.exp(-normed))
    act_grad = out_masked * sigmoid * (1.0 + normed * (1.0 - sigmoid))
    total = jnp.sum(act_grad, axis=0, keepdims=True)
    cross = jnp.sum(act_grad * normalized, axis=0, keepdims=True)
    write(deep2, deep, two(total), two(cross), jnp.zeros((1, 128), F32))
    copies = spread(deep2, deep, deep_group, d2_s, d2_r)
    centre = columns(13).astype(F32)
    block = (occ * (centre + normed * sigmoid)).astype(BF16)
    block_ref[...] = dot(to_bricks, block).astype(BF16).reshape(4, 64, 256)
    norm_s[...] = normalized
    shared.append(share_columns(14, 13, 1))
    meet(copies, deep2, deep_group, d2_s, d2_r)
    wide2[wide] = sum_of(deep2, 2 * Z)
    copies = spread(wide2, wide, wide_group, w2_s, w2_r)
    gath_t[2] = gath[2].T
    meet(copies, wide2, wide_group, w2_s, w2_r)
    tiles = sum_of(wide2, X * Y)
    total, cross = one(tiles[0:2]), one(tiles[2:4])
    inverse_root = lax.rsqrt(voxel_count)
    ggrad_ref[...] = cross * inverse_root
    bgrad_ref[...] = total * inverse_root
    conv_grad = (gamma * inverse_std * (act_grad - total / voxel_count - norm_s[...] * cross / voxel_count) * occ).astype(BF16)
    cg_s[...] = conv_grad

    half_grads[0] = jnp.where(c == 0, conv_grad[:, :128].astype(F32), conv_grad[:, 128:].astype(F32)).astype(BF16)
    half_grads[1] = jnp.where(c == 0, conv_grad[:, 128:].astype(F32), conv_grad[:, :128].astype(F32)).astype(BF16)
    shared.append(pltpu.make_async_remote_copy(
        src_ref=half_grads.at[1], dst_ref=half_grads.at[2], send_sem=c_s, recv_sem=c_r,
        device_id=sister, device_id_type=MESH))
    shared[2].start()
    small = 256 // (X * Y)
    half = pl.ds(pl.multiple_of(c * 128, 128), 128)
    other_half = pl.ds(pl.multiple_of((1 - c) * 128, 128), 128)
    depth = slots() // Z
    first_z, count_z = THIRD
    owners = [i * Z // count_z for i in range(count_z)]
    slot = sum(i * (z == owner).astype(I32) for i, owner in enumerate(owners))
    is_owner = sum((z == owner).astype(I32) for owner in owners) > 0

    def axes(part):
        return ((y, Y), (x, X)) if part else ((x, X), (y, Y))

    def mate(part, stage, step):
        if part == stage - 1:
            return device(z, ahead(x, step, X), y, c)
        return device(z, x, ahead(y, step, Y), c)

    def span(start, size):
        return pl.ds(pl.multiple_of(start, 16), size)

    def remote(source, target, send, receive, to):
        return pltpu.make_async_remote_copy(
            src_ref=source, dst_ref=target, send_sem=send, recv_sem=receive, device_id=to, device_id_type=MESH)

    going = {}

    def arrive(stage, piece):
        for copy in going.pop((stage, piece)):
            copy.wait_recv()
            sent.append(copy)

    def heard(stage, piece):
        for copy in going.pop((stage, piece)):
            copy.wait_recv()

    def products(piece):
        first, count, _ = PIECES[piece]
        for k in range(first, first + count):
            own[k] = dot(cols_t[k], half_grads[0])

    def hear_sister():
        for copy in shared:
            copy.wait_recv()
            sent.append(copy)

    def stage1(piece):
        first, count, part = PIECES[piece]
        (place, length), _ = axes(part)
        rows = 256 // length
        for k in range(first, first + count):
            value = own[k] + dot(cols_sister[k], half_grads[2])
            own[k] = value
            s1[k] = value.astype(BF16)
        for step in far_first(length):
            copy = remote(
                s1.at[pl.ds(first, count), span(ahead(place, step, length) * rows, rows)],
                r1.at[step - 1, pl.ds(first, count)],
                q1_s.at[piece, step - 1], q1_r.at[piece, step - 1], mate(part, 1, step))
            copy.start()
            going.setdefault(("one", part), []).append(copy)

    def stage2(part):
        first, count = PARTS[part]
        (place, length), (place2, length2) = axes(part)
        rows = 256 // length
        arrive("one", part)
        for k in range(first, first + count):
            value = own[k, span(place * rows, rows), :]
            for step in range(1, length):
                value = value + r1[step - 1, k].astype(F32)
            own[k, 0:rows, :] = value
            s2[k] = value.astype(BF16)
        going["two", part] = []
        for step in far_first(length2):
            copy = remote(
                s2.at[pl.ds(first, count), span(ahead(place2, step, length2) * small, small)],
                r2.at[step - 1, pl.ds(first, count)],
                q2_s.at[part, step - 1], q2_r.at[part, step - 1], mate(part, 2, step))
            copy.start()
            going["two", part].append(copy)

    def stage3():
        for part, (first, count) in enumerate(PARTS):
            _, (place2, length2) = axes(part)
            arrive("two", part)
            for k in range(first, first + count):
                value = own[k, span(place2 * small, small), :]
                for step in range(1, length2):
                    value = value + r2[step - 1, k].astype(F32)
                t3[k] = value
                s3[k] = value.astype(BF16)
        for k in range(first_z, slots()):
            t3[k] = jnp.zeros((small, 128), F32)
            s3[k] = jnp.zeros((small, 128), BF16)
        going["three", 0] = []
        for dz in far_first(Z):
            copy = remote(
                s3.at[pl.ds(ahead(z, dz, Z) * depth, depth)], r3.at[dz - 1],
                q3_s.at[dz - 1], q3_r.at[dz - 1], device(ahead(z, dz, Z), x, y, c))
            copy.start()
            going["three", 0].append(copy)

    def fine(part):
        (place, length), (place2, _) = axes(part)
        return span(place * (256 // length) + place2 * small, small)

    def push(where, send, receive, to):
        return remote(outb.at[where], outb.at[where], send, receive, to)

    def back3():
        arrive("three", 0)
        mine = pl.ds(z * depth, depth)
        value = t3[mine]
        for dz in range(1, Z):
            value = value + r3[dz - 1].astype(F32)
        gathered[mine] = (value * inverse_root[:, :128].reshape(1, 1, 128)).astype(BF16)
        going["back3", 0] = []
        for dz in far_first(Z):
            copy = remote(gathered.at[mine], gathered.at[mine], a3_s.at[dz - 1], a3_r.at[dz - 1],
                          device(ahead(z, dz, Z), x, y, c))
            copy.start()
            sent.append(copy)
            behind = gathered.at[pl.ds(ahead(z, -dz, Z) * depth, depth)]
            going["back3", 0].append(remote(behind, behind, a3_s.at[dz - 1], a3_r.at[dz - 1], here))

    def back2():
        heard("back3", 0)
        for part, (first, count) in enumerate(PARTS):
            (place, length), (place2, length2) = axes(part)
            going["back2", part] = []
            for step in far_first(length2):
                copy = remote(gathered.at[pl.ds(first, count)], outb.at[pl.ds(first, count), fine(part), half],
                              a2_s.at[part, step - 1], a2_r.at[part, step - 1], mate(part, 2, step))
                copy.start()
                sent.append(copy)
                start = place * (256 // length) + ahead(place2, -step, length2) * small
                going["back2", part].append(push(
                    (pl.ds(first, count), span(start, small), half), a2_s.at[part, step - 1],
                    a2_r.at[part, step - 1], here))
        for part, (first, count) in enumerate(PARTS):
            outb[pl.ds(first, count), fine(part), half] = gathered[first : first + count]

    def strip(part, step, lanes):
        (place, length), _ = axes(part)
        rows = 256 // length
        return pl.ds(*PARTS[part]), span(ahead(place, -step, length) * rows, rows), lanes

    def hand_over(part, step):
        copy = push(strip(part, step, half), a0_s.at[part, step], a0_r.at[part, step], sister)
        copy.start()
        sent.append(copy)

    def back1(part):
        _, length = axes(part)[0]
        heard("back2", part)
        for step in far_first(length):
            copy = push(strip(part, 0, half), a1_s.at[part, step - 1], a1_r.at[part, step - 1], mate(part, 1, step))
            copy.start()
            sent.append(copy)
        hand_over(part, 0)

    def back0():
        for step in (1, 3, 2):
            for part in range(2):
                if step < axes(part)[0][1]:
                    push(strip(part, step, half), a1_s.at[part, step - 1], a1_r.at[part, step - 1], here).wait_recv()
                    hand_over(part, step)

    def finish():
        for step in (0, 1, 3, 2):
            for part in range(2):
                if step < axes(part)[0][1]:
                    push(strip(part, step, other_half), a0_s.at[part, step], a0_r.at[part, step], here).wait_recv()

    rows_x, mine_z = 256 // X, first_z + slot

    def toward(i):
        steps = lax.rem(owners[i] + Z - z, Z)
        place = jnp.maximum(steps - 1, 0)
        return remote(s1.at[first_z + i], rz.at[place], z1_s.at[i], z1_r.at[place], device(jnp.int32(owners[i]), x, y, c))

    def along_x(step):
        return remote(s2z.at[span(ahead(x, step, X) * rows_x, rows_x)], r2z.at[step - 1], z2_s.at[step - 1],
                      z2_r.at[step - 1], device(z, ahead(x, step, X), y, c))

    def along_y(step):
        return remote(s3z.at[span(ahead(y, step, Y) * small, small)], r3z.at[step - 1], z3_s.at[step - 1],
                      z3_r.at[step - 1], device(z, x, ahead(y, step, Y), c))

    def back_y(step, behind):
        rows = span(x * rows_x + ahead(y, -behind, Y) * small, small)
        return push((mine_z, rows, half), b3_s.at[step - 1], b3_r.at[step - 1], device(z, x, ahead(y, step, Y), c))

    def back_x(step, behind):
        rows = span(ahead(x, -behind, X) * rows_x, rows_x)
        return push((mine_z, rows, half), b2_s.at[step - 1], b2_r.at[step - 1], device(z, ahead(x, step, X), y, c))

    def back_z(dz):
        return push((mine_z, pl.ds(0, 256), half), b1_s.at[dz - 1], b1_r.at[slot], device(ahead(z, dz, Z), x, y, c))

    def products_z():
        for k in range(first_z, first_z + count_z):
            own[k] = dot(cols_t[k], half_grads[0])

    def stage1_z():
        for i in range(count_z):
            k = first_z + i
            value = own[k] + dot(cols_sister[k], half_grads[2])
            own[k] = value
            s1[k] = value.astype(BF16)

            @pl.when(z != owners[i])
            def _():
                toward(i).start()

    def stage2_z():
        @pl.when(is_owner)
        def _():
            value = own[mine_z]
            for place in range(Z - 1):
                remote(s1.at[first_z], rz.at[place], z1_s.at[0], z1_r.at[place], here).wait_recv()
                value = value + rz[place].astype(F32)
            own2z[...] = value
            s2z[...] = value.astype(BF16)
            for step in far_first(X):
                along_x(step).start()

    def stage3_z():
        @pl.when(is_owner)
        def _():
            value = own2z[span(x * rows_x, rows_x), :]
            for step in far_first(X):
                along_x(step).wait_recv()
                value = value + r2z[step - 1].astype(F32)
            own3z[...] = value
            s3z[...] = value.astype(BF16)
            for step in far_first(Y):
                along_y(step).start()

    def back3_z():
        @pl.when(is_owner)
        def _():
            value = own3z[span(y * small, small), :]
            for step in far_first(Y):
                along_y(step).wait_recv()
                value = value + r3z[step - 1].astype(F32)
            outb[mine_z, span(x * rows_x + y * small, small), half] = (value * inverse_root[:, :128]).astype(BF16)
            for step in far_first(Y):
                back_y(step, 0).start()

    def back2_z():
        @pl.when(is_owner)
        def _():
            for step in far_first(Y):
                back_y(step, step).wait_recv()
            for step in far_first(X):
                back_x(step, 0).start()

    def back1_z():
        @pl.when(is_owner)
        def _():
            for step in far_first(X):
                back_x(step, step).wait_recv()
            for dz in far_first(Z):
                back_z(dz).start()

    def offset_z(i, lanes, send, receive, to):
        return push((first_z + i, pl.ds(0, 256), lanes), send, receive, to)

    def back0_z():
        for i in range(count_z):
            @pl.when(z != owners[i])
            def _():
                offset_z(i, half, b1_s.at[0], b1_r.at[i], here).wait_recv()

            copy = offset_z(i, half, b0_s.at[i], b0_r.at[i], sister)
            copy.start()
            sent.append(copy)

    def finish_z():
        for i in range(count_z):
            @pl.when(z != owners[i])
            def _():
                toward(i).wait_send()

        @pl.when(is_owner)
        def _():
            for step in range(1, X):
                along_x(step).wait_send()
                back_x(step, 0).wait_send()
            for step in range(1, Y):
                along_y(step).wait_send()
                back_y(step, 0).wait_send()
            for dz in range(1, Z):
                back_z(dz).wait_send()

        for i in range(count_z):
            offset_z(i, other_half, b0_s.at[i], b0_r.at[i], here).wait_recv()

    def column_grads():
        grad_s[...] = jnp.zeros_like(grad_s)
        for k in range(27):
            a, b, shift = k // 9, k // 3 % 3, k % 3
            product = lax.dot_general(cg_s[...], weight[k], (((1,), (1,)), ((), ())), preferred_element_type=F32)
            for i in range(4):
                start = (a + i) * 96 + b * 16
                grad_s[shift, start : start + 64, :] += product[i * 64 : (i + 1) * 64, :]

    def brick_grads():
        result = None
        for shift in range(3):
            value = grad_s[shift]
            high = value.astype(BF16)
            low = (value - high.astype(F32)).astype(BF16)
            term = dot(gath_t[shift], jnp.concatenate([high, low], axis=1))
            result = term if result is None else result + term
        result = result[:, :256] + result[:, 256:]
        local_s[...] = result[:256]
        ghosts[...] = result[256:].astype(BF16).reshape(8, 64, 256)
        going["ghosts", 0] = []
        for d in range(8):
            copy = remote(ghosts.at[d], returned.at[d], gh_s.at[d], gh_r.at[d], neighbour(-ROWS[d], -COLUMNS[d]))
            copy.start()
            going["ghosts", 0].append(copy)

    def feature_grads():
        out_bricks = dot(to_bricks, out_masked.astype(BF16))
        arrive("ghosts", 0)
        for b in range(4):
            rows = slice(b * 64, (b + 1) * 64)
            extra = out_bricks[rows] + local_s[rows, :]
            for d in range(8):
                extra = extra + jnp.where(send_ref[0, d] == b, returned[d].astype(F32), 0.0)
            fgrad_ref[b] = (extra * occ_brick[rows]).astype(BF16)

    schedule = (
        (products, 0), (products, 1), (products_z,), (hear_sister,),
        (stage1, 0), (stage1, 1), (stage1_z,),
        (products, 2), (products, 3), (stage1, 2), (stage1, 3),
        (column_grads,), (settle,),
        (stage2, 0), (stage2, 1), (stage2_z,),
        (stage3,), (stage3_z,),
        (brick_grads,),
        (back3_z,), (back3,),
        (back2_z,), (back2,),
        (back1_z,), (back1, 0), (back1, 1),
        (feature_grads,), (settle,),
        (back0,), (back0_z,), (finish,), (finish_z,), (settle,),
    )
    for step, *piece in schedule:
        step(*piece)


def write_out(block, fgrad, wgrad, ggrad, bgrad, block_out, fgrad_out, wgrad_out, ggrad_out, bgrad_out, sems):
    pairs = [(block, block_out), (fgrad, fgrad_out), (ggrad, ggrad_out), (bgrad, bgrad_out)]
    pairs.append((wgrad, wgrad_out))
    copies = [pltpu.make_async_copy(source, target, sems.at[i]) for i, (source, target) in enumerate(pairs)]
    for copy in copies:
        copy.start()
    for copy in copies:
        copy.wait()


def on_device(features, occupancy, neighbours, send_list, weight, gamma, beta, out_grad):
    vmem = pl.BlockSpec(memory_space=pltpu.VMEM)
    small = 256 // (X * Y)
    near, far = max(X, Y) - 1, Z - 1
    depth = slots() // Z
    third = THIRD[1]
    pieces = len(PIECES)
    dma = pltpu.SemaphoreType.DMA
    scratch = [
        pltpu.VMEM((4, 64), I32),
        pltpu.VMEM((4, 27), I32),
        pltpu.VMEM((4, 64, 256), BF16),
        pltpu.VMEM((1, 256), F32),
        pltpu.VMEM((1, 256), F32),
        pltpu.VMEM((4, 64, 256), BF16),
        pltpu.VMEM((16, 128), F32),
        pltpu.VMEM((256, 256), F32),
        pltpu.VMEM((4, 64, 256), BF16),
        pltpu.VMEM((8, 64, 256), BF16),
        pltpu.VMEM((12, 64, 256), BF16),
        pltpu.VMEM((3, 576, 768), BF16),
        pltpu.VMEM((3, 768, 576), BF16),
        pltpu.VMEM((3, 576, 256), BF16),
        pltpu.VMEM((27, 256, 256), BF16),
        pltpu.VMEM((256, 256), F32),
        pltpu.VMEM((256, 256), F32),
        pltpu.VMEM((27, 256, 256), BF16),
        pltpu.VMEM((2 * Z, 8, 128), F32),
        pltpu.VMEM((X * Y, 8, 128), F32),
        pltpu.VMEM((2 * Z, 8, 128), F32),
        pltpu.VMEM((X * Y, 8, 128), F32),
        pltpu.VMEM((256, 256), BF16),
        pltpu.VMEM((3, 576, 256), F32),
        pltpu.VMEM((256, 256), F32),
        pltpu.VMEM((8, 64, 256), BF16),
        pltpu.VMEM((8, 64, 256), BF16),
        pltpu.VMEM((27, 256, 256), BF16),
        pltpu.VMEM((3, 256, 128), BF16),
        pltpu.VMEM((27, 256, 128), F32),
        pltpu.VMEM((27, 256, 128), BF16),
        pltpu.VMEM((near, 27, 256 // min(X, Y), 128), BF16),
        pltpu.VMEM((27, 256 // min(X, Y), 128), BF16),
        pltpu.VMEM((near, 27, small, 128), BF16),
        pltpu.VMEM((slots(), small, 128), BF16),
        pltpu.VMEM((slots(), small, 128), F32),
        pltpu.VMEM((far, depth, small, 128), BF16),
        pltpu.VMEM((slots(), small, 128), BF16),
        pltpu.VMEM((far, 256, 128), BF16),
        pltpu.VMEM((256, 128), F32),
        pltpu.VMEM((256, 128), BF16),
        pltpu.VMEM((near, 256 // X, 128), BF16),
        pltpu.VMEM((256 // X, 128), F32),
        pltpu.VMEM((256 // X, 128), BF16),
        pltpu.VMEM((near, small, 128), BF16),
        dma((7,)), dma((8,)), dma((8,)),
        dma((2 * Z - 1,)), dma((2 * Z - 1,)), dma((X * Y - 1,)), dma((X * Y - 1,)),
        dma((2 * Z - 1,)), dma((2 * Z - 1,)), dma((X * Y - 1,)), dma((X * Y - 1,)),
        dma((8,)), dma((8,)), dma((2,)), dma((2,)), dma, dma,
        dma((pieces, near)), dma((pieces, near)), dma((2, near)), dma((2, near)), dma((far,)), dma((far,)),
        dma((far,)), dma((far,)), dma((2, near)), dma((2, near)),
        dma((2, near)), dma((2, near)), dma((2, near + 1)), dma((2, near + 1)),
        dma((third,)), dma((far,)), dma((near,)), dma((near,)), dma((near,)), dma((near,)),
        dma((near,)), dma((near,)), dma((near,)), dma((near,)), dma((far,)), dma((third,)), dma((third,)), dma((third,)),
    ]
    anywhere = pl.BlockSpec(memory_space=pl.ANY)
    results = pl.pallas_call(
        kernel,
        name="brick_block",
        out_shape=(
            pltpu.VMEM((4, 64, 256), BF16),
            pltpu.VMEM((4, 64, 256), BF16),
            pltpu.VMEM((27, 256, 256), BF16),
            pltpu.VMEM((1, 256), F32),
            pltpu.VMEM((1, 256), F32),
        ),
        in_specs=[anywhere, anywhere, pl.BlockSpec(memory_space=pltpu.SMEM)] + [anywhere] * 5,
        out_specs=(vmem, vmem, vmem, vmem, vmem),
        scratch_shapes=scratch,
        compiler_params=pltpu.CompilerParams(
            collective_id=0, has_side_effects=True, vmem_limit_bytes=56 * 2**20),
    )(occupancy, neighbours, send_list.reshape(1, 8), features, gamma.reshape(1, 256), beta.reshape(1, 256), out_grad, weight)
    block, fgrad, wgrad, ggrad, bgrad = pl.pallas_call(
        write_out,
        name="write_out",
        out_shape=(
            jax.ShapeDtypeStruct((4, 64, 256), BF16),
            jax.ShapeDtypeStruct((4, 64, 256), BF16),
            jax.ShapeDtypeStruct((27, 256, 256), BF16),
            jax.ShapeDtypeStruct((1, 256), F32),
            jax.ShapeDtypeStruct((1, 256), F32),
        ),
        in_specs=[anywhere] * 5,
        out_specs=(anywhere,) * 5,
        scratch_shapes=[dma((5,))],
        compiler_params=pltpu.CompilerParams(vmem_limit_bytes=8 * 2**20),
    )(*results)
    return block, fgrad, wgrad, ggrad.reshape(256), bgrad.reshape(256)


def solution(mesh):
    placed = (
        P(("gx", "gy"), None, None),
        P(("gx", "gy"), None),
        P(("gx", "gy"), None),
        P(("gx", "gy"), None, None),
        P(),
        P(),
        P(),
        P(("gx", "gy"), None, None),
    )
    return jax.shard_map(
        on_device,
        mesh=mesh,
        in_specs=placed,
        out_specs=(P(("gx", "gy"), None, None), P(("gx", "gy"), None, None), P(), P(), P()),
        check_vma=False,
    )
```
